32 devices in a mesh: doc: 16 (over z, x, core), half: 2 (over y).
Axes of the slice: x: 2, y: 2, z: 4, core: 2. Of those that a mesh axis runs over, the one named last changes fastest.
Arguments:
- hidden_in: bfloat16 [64, 512, 768], P('doc', 'half'), may hold values from -6 to 6
- boxes: int32 [4, 64, 512], P(None, 'doc', 'half'), may hold values from 0 to 1000, as said below
- lengths: int32 [64], P('doc'), may hold values from 128 to 512, as said below
- box_weight: bfloat16 [128, 768], replicated, may hold values from -0.5 to 0.5
- qkv_weight: bfloat16 [768, 2304], replicated, may hold values from -0.21875 to 0.21875
- qv_bias: float32 [2, 768], replicated, may hold values from -3 to 3
- out_weight: bfloat16 [768, 768], replicated, may hold values from -0.875 to 0.875
- out_bias: float32 [768], replicated, may hold values from -3 to 3
- rel_tables: float32 [32, 36], replicated, may hold values from -4 to 4
- norm_one: float32 [2, 768], replicated, may hold values from -0.5 to 1.4, as said below
- ffn_in_weight: bfloat16 [768, 3072], replicated, may hold values from -0.21875 to 0.21875
- ffn_in_bias: float32 [3072], replicated, may hold values from -3 to 3
- ffn_out_weight: bfloat16 [3072, 768], replicated, may hold values from -0.15625 to 0.15625
- ffn_out_bias: float32 [768], replicated, may hold values from -3 to 3
- norm_two: float32 [2, 768], replicated, may hold values from -0.5 to 1.4, as said below
- cotangent: bfloat16 [64, 512, 768], P('doc', 'half'), may hold values from -6 to 6
Outputs:
- layer_out: bfloat16 [64, 512, 768], P('doc', 'half')
- hidden_grad: bfloat16 [64, 512, 768], P('doc', 'half')
- box_weight_grad: float32 [128, 768], P('half')
- qkv_weight_grad: float32 [768, 2304], P('half')
- qv_bias_grad: float32 [2, 768], P('half')
- out_weight_grad: float32 [768, 768], P('half')
- out_bias_grad: float32 [768], P('half')
- rel_tables_grad: float32 [32, 36], P('half')
- norm_one_grad: float32 [2, 768], P('half')
- ffn_in_weight_grad: float32 [768, 3072], P('half')
- ffn_in_bias_grad: float32 [3072], P('half')
- ffn_out_weight_grad: float32 [3072, 768], P('half')
- ffn_out_bias_grad: float32 [768], P('half')
- norm_two_grad: float32 [2, 768], P('half')
The draws below stay inside these ranges and needn't reach their ends.
Inputs may be any that keep to these rules, and one draw needn't show every extreme that they name: `boxes`: rows hold x0, y0, x1, y1 with x1 > x0 and y1 > y0. `lengths`: tokens at positions at or past a window's length are padding. In every aligned run of 4 windows one window has length 512. `norm_one`: row 0 is a gain, row 1 a shift. `norm_two`: row 0 is a gain, row 1 a shift.
All inputs are finite; a program needn't handle non-finite values.
Results may differ from the reference program's by a relative error of at most 0.019.
Values may be sent and summed in bfloat16 or wider, within the bound.
No kernel may reach another device: no remote copies, remote signals or barrier semaphores. Data moves between devices by JAX's collectives and lax.ppermute only.
A program may use at most 256 MiB of HBM per device.

```python
from functools import partial
import jax
import jax.numpy as jnp
from jax import lax

D = 768
H = 12
DH = 64
FF = 3072
BOXF = 128
NB = 32
SEQ = 512
WIN_PAIR = 4
WINDOWS = 64


def draw_boxes(key, part):
    key = jax.random.fold_in(key, 11)
    keys_four = jax.random.split(key, 4)
    left_edge = jax.random.randint(keys_four[0], (WINDOWS, SEQ), 0, 800)
    top_edge = jax.random.randint(keys_four[1], (WINDOWS, SEQ), 0, 961)
    right_edge = left_edge + jax.random.randint(keys_four[2], (WINDOWS, SEQ), 8, 201)
    bottom_edge = top_edge + jax.random.randint(keys_four[3], (WINDOWS, SEQ), 8, 41)
    left_edge = left_edge.at[0, 0].set(0)
    bottom_edge = bottom_edge.at[0, 0].set(1000)
    return jnp.stack([left_edge, top_edge, right_edge, bottom_edge]).astype(jnp.int32)


def draw_lengths(key, part):
    key = jax.random.fold_in(key, 23)
    first_key, second_key = jax.random.split(key)
    drawn = jax.random.randint(first_key, (WINDOWS,), SEQ // 4, SEQ + 1)
    chosen = jax.random.randint(second_key, (WINDOWS // WIN_PAIR, 1), 0, WIN_PAIR)
    slots = jnp.arange(WIN_PAIR)[None, :]
    full_window = (slots == chosen).reshape(WINDOWS)
    return jnp.where(full_window, SEQ, drawn).astype(jnp.int32)


def norm_pair(key, spread):
    gain_key, shift_key = jax.random.split(key)
    gain_row = jax.random.uniform(gain_key, (D,), jnp.float32, 1.0 - spread, 1.0 + spread)
    shift_row = jax.random.uniform(shift_key, (D,), jnp.float32, -0.5, 0.5)
    return jnp.stack([gain_row, shift_row]).astype(jnp.float32)


def draw_norm_one(key, part):
    key = jax.random.fold_in(key, 31)
    return norm_pair(key, 0.4)


def draw_norm_two(key, part):
    key = jax.random.fold_in(key, 47)
    return norm_pair(key, 0.4)


def block_scale(rng, shape, cuts, low, high):
    gain, own = 1.0, jax.random.fold_in(rng, 6)
    for dim, blocks in cuts:
        draws = jnp.exp(jax.random.uniform(jax.random.fold_in(own, dim), (blocks,), jnp.float32, low / len(cuts), high / len(cuts)))
        gain = gain * jnp.repeat(draws, shape[dim] // blocks).reshape([-1 if axis == dim else 1 for axis in range(len(shape))])
    return gain


def noise(key, shape, scale, limit, pieces=(), kind=jnp.bfloat16):
    factor_of = block_scale(key, shape, pieces, -0.22, 0.18) if pieces else 1.0
    values = jax.random.normal(key, shape, jnp.float32) * scale * factor_of
    return jnp.minimum(jnp.maximum(values, -limit), limit).astype(kind)


def setup_inputs(seed: int = 0) -> dict:
    arg_keys = jax.random.split(jax.random.key(seed), 17)
    hidden_in = noise(arg_keys[0], (WINDOWS, SEQ, D), 1.0, 6.0, ((0, 16), (1, 2)))
    boxes = draw_boxes(jax.random.fold_in(arg_keys[16], 71), 0)
    lengths = draw_lengths(jax.random.fold_in(arg_keys[16], 71), 0)
    box_weight = noise(arg_keys[3], (BOXF, D), BOXF ** -0.5, 0.5)
    qkv_weight = noise(arg_keys[4], (D, 3 * D), D ** -0.5, 0.21875)
    qv_bias = noise(arg_keys[5], (2, D), 0.5, 3.0, (), jnp.float32)
    out_weight = noise(arg_keys[6], (D, D), (D // 16) ** -0.5, 0.875)
    out_bias = noise(arg_keys[7], (D,), 0.5, 3.0, (), jnp.float32)
    rel_tables = noise(arg_keys[8], (NB, 3 * H), 1.0, 4.0, (), jnp.float32)
    norm_one = draw_norm_one(jax.random.fold_in(arg_keys[16], 71), 0)
    ffn_in_weight = noise(arg_keys[10], (D, FF), D ** -0.5, 0.21875)
    ffn_in_bias = noise(arg_keys[11], (FF,), 0.5, 3.0, (), jnp.float32)
    ffn_out_weight = noise(arg_keys[12], (FF, D), (FF // 2) ** -0.5, 0.15625)
    ffn_out_bias = noise(arg_keys[13], (D,), 0.5, 3.0, (), jnp.float32)
    norm_two = draw_norm_two(jax.random.fold_in(arg_keys[16], 71), 0)
    cotangent = noise(arg_keys[15], (WINDOWS, SEQ, D), 1.0, 6.0, ((0, 16), (1, 2)))
    return {"hidden_in": hidden_in, "boxes": boxes, "lengths": lengths, "box_weight": box_weight, "qkv_weight": qkv_weight, "qv_bias": qv_bias, "out_weight": out_weight, "out_bias": out_bias, "rel_tables": rel_tables, "norm_one": norm_one, "ffn_in_weight": ffn_in_weight, "ffn_in_bias": ffn_in_bias, "ffn_out_weight": ffn_out_weight, "ffn_out_bias": ffn_out_bias, "norm_two": norm_two, "cotangent": cotangent}


@jax.custom_vjp
def low(v):
    return lax.optimization_barrier(v.astype(jnp.bfloat16)).astype(jnp.float32)

@jax.custom_vjp
def low_back(v):
    return v

def low_keep(v):
    return (low(v), None)

def low_pass(kept, grad):
    return (grad,)

def back_keep(v):
    return (v, None)

def back_low(kept, grad):
    return (low(grad),)
low.defvjp(low_keep, low_pass)
low_back.defvjp(back_keep, back_low)
highest = lax.Precision.HIGHEST
epsilon = 1e-05
thresholds = (1, 2, 3, 4, 5, 6, 7, 8, 12, 16, 24, 32, 48, 64, 96)

def bucket_of(offset, step_size):
    magnitude = jnp.abs(offset) // step_size
    counter = jnp.zeros(offset.shape, jnp.int32)
    for bound_value in thresholds:
        counter = counter + (magnitude >= bound_value).astype(jnp.int32)
    return counter + 16 * (offset > 0).astype(jnp.int32)

def box_features(boxes):
    coords = jnp.moveaxis(boxes, 0, -1).astype(jnp.float32)
    freq_count = BOXF // 8
    frequencies = 1000.0 ** (-jnp.arange(freq_count, dtype=jnp.float32) / freq_count)
    angles = coords[..., None] * frequencies
    sin_cos = jnp.stack([jnp.sin(angles), jnp.cos(angles)], axis=-2)
    return sin_cos.reshape(coords.shape[:-1] + (BOXF,))

def layer_norm(summed, params):
    centered = summed - lax.optimization_barrier(jnp.mean(summed, -1, keepdims=True))
    variance = lax.optimization_barrier(jnp.mean(centered * centered, -1, keepdims=True))
    return centered * lax.rsqrt(variance + epsilon) * params[0] + params[1]

def window_attention(rel_tables, packed):
    queries, key_rows, values, window_boxes, length = packed
    positions = jnp.arange(SEQ, dtype=jnp.int32)
    line_bucket = bucket_of(positions[None, :] - positions[:, None], 1)
    across_bucket = bucket_of(window_boxes[0][None, :] - window_boxes[0][:, None], 4)
    down_bucket = bucket_of(window_boxes[1][None, :] - window_boxes[1][:, None], 4)
    bias_map = rel_tables[line_bucket, :H] + rel_tables[across_bucket, H:2 * H] + rel_tables[down_bucket, 2 * H:]
    raw_scores = jnp.einsum('ihd,jhd->hij', queries, key_rows, precision=highest) * DH ** (-0.5)
    raw_scores = raw_scores + jnp.moveaxis(bias_map, 2, 0)
    key_valid = positions < length
    masked = low_back(jnp.where(key_valid[None, None, :], raw_scores, -1000000000.0))
    row_max = lax.optimization_barrier(jnp.max(masked, -1, keepdims=True))
    exps = jnp.exp(masked - row_max)
    probabilities = low(exps / lax.optimization_barrier(jnp.sum(exps, -1, keepdims=True)))
    return jnp.einsum('hij,jhd->ihd', probabilities, values, precision=highest)

def forward(hidden, box_weight, qkv_weight, qv_bias, out_weight, out_bias, rel_tables, norm_one, ffn_in_weight, ffn_in_bias, ffn_out_weight, ffn_out_bias, norm_two, features=None, window_boxes=None, lengths=None):
    token_rows = hidden.reshape(-1, D)
    entry_sum = token_rows + low_back(jnp.dot(features, box_weight, precision=highest))
    entry_low = low(entry_sum)
    projected = jnp.dot(entry_low, qkv_weight, precision=highest)
    queries = low(low_back(projected[:, :D] + qv_bias[0]))
    key_rows = low(low_back(projected[:, D:2 * D]))
    values = low(low_back(projected[:, 2 * D:] + qv_bias[1]))
    head_shape = (WINDOWS, SEQ, H, DH)
    attended = lax.map(jax.checkpoint(partial(window_attention, rel_tables)), (queries.reshape(head_shape), key_rows.reshape(head_shape), values.reshape(head_shape), window_boxes, lengths))
    heads_low = low(low_back(attended.reshape(-1, D)))
    branch = low_back(jnp.dot(heads_low, out_weight, precision=highest) + out_bias)
    second = layer_norm(entry_sum + branch, norm_one)
    second_low = low(second)
    inner_pre = low_back(jnp.dot(second_low, ffn_in_weight, precision=highest) + ffn_in_bias)
    active = low(jax.nn.gelu(inner_pre, approximate=False))
    outer_pre = low_back(jnp.dot(active, ffn_out_weight, precision=highest) + ffn_out_bias)
    result = layer_norm(second + outer_pre, norm_two)
    return result.reshape(WINDOWS, SEQ, D)

def reference(hidden_in, boxes, lengths, box_weight, qkv_weight, qv_bias, out_weight, out_bias, rel_tables, norm_one, ffn_in_weight, ffn_in_bias, ffn_out_weight, ffn_out_bias, norm_two, cotangent):
    features = low(box_features(boxes).reshape(-1, BOXF))
    window_boxes = jnp.moveaxis(boxes, 0, 1)
    primals = (hidden_in.astype(jnp.float32), box_weight.astype(jnp.float32), qkv_weight.astype(jnp.float32), qv_bias.astype(jnp.float32), out_weight.astype(jnp.float32), out_bias.astype(jnp.float32), rel_tables.astype(jnp.float32), norm_one.astype(jnp.float32), ffn_in_weight.astype(jnp.float32), ffn_in_bias.astype(jnp.float32), ffn_out_weight.astype(jnp.float32), ffn_out_bias.astype(jnp.float32), norm_two.astype(jnp.float32))
    applied = partial(forward, features=features, window_boxes=window_boxes, lengths=lengths)
    result, pullback = jax.vjp(applied, *primals)
    gradients = pullback(cotangent.astype(jnp.float32))
    return (result.astype(jnp.bfloat16), gradients[0].astype(jnp.bfloat16), gradients[1], gradients[2], gradients[3], gradients[4], gradients[5], gradients[6], gradients[7], gradients[8], gradients[9], gradients[10], gradients[11], gradients[12])
```

```python
from functools import partial

import jax
import jax.numpy as jnp
import numpy as np
from jax import lax
from jax.experimental import pallas as pl
from jax.experimental.pallas import tpu as pltpu
from jax.sharding import PartitionSpec as P

H = 12
DH = 64
BOXF = 128
NB = 32
EPS = 1e-05
LOG2E = 1.4426950408889634
BF = jnp.bfloat16
F32 = jnp.float32
VMEM = 56 << 20
SHORT = pl.CostEstimate(flops=1, bytes_accessed=1, transcendentals=0)


def dot(a, b, ca=1, cb=0):
    return lax.dot_general(a, b, (((ca,), (cb,)), ((), ())), preferred_element_type=F32)


ROUND = 1.5 * 2.0**23 * 2.0**-8
SMALL = 1.6e-4


def unpack(both):
    first = (both + ROUND) - ROUND
    return first, (both - first) * (1.0 / SMALL)


def bucket_of(offset, shift):
    magnitude = jnp.abs(offset)
    if shift:
        magnitude = magnitude >> shift
    count = jnp.minimum(magnitude, 8)
    for n, bound in enumerate((12, 16, 24, 32, 48, 64, 96)):
        count = jnp.where(magnitude >= bound, 9 + n, count)
    return jnp.where(offset > 0, count + 16, count)


def look_up(table, index):
    return jnp.take_along_axis(table, index, axis=1, mode="promise_in_bounds")


def sine(angle, quarter):
    n = jnp.round(angle * 0.6366197723675814)
    x = ((angle - n * 1.5703125) - n * 4.837512969970703125e-4) - n * 7.549789954891882e-8
    turn = n.astype(jnp.int32) + quarter
    y = x * x
    odd = x + x * y * (-1.6666654611e-1 + y * (8.3321608736e-3 + y * -1.9515295891e-4))
    even = 1.0 - 0.5 * y + y * y * (4.166664568298827e-2 + y * (-1.388731625493765e-3 + y * 2.443315711809948e-5))
    value = jnp.where((turn & 1) == 0, odd, even)
    return jnp.where((turn & 2) == 0, value, -value)


def bias_kernel(len_ref, box_ref, rel_ref, freq_ref, out_ref, map_ref, feat_ref, line, maps, tabs, cols, *, tile, rows):
    length = out_ref.shape[3]
    blocks = length // 128
    span = (2 * blocks - 1) * 128
    w = pl.program_id(0)
    it = pl.program_id(1)

    @pl.when((w == 0) & (it == 0))
    def _():
        cols[...] = jnp.zeros_like(cols)
        cols[0:NB, 0 : 3 * H] = rel_ref[...] * LOG2E
        t = cols[0:128, :].T
        for kind in range(3):
            for hp in range(H // 2):
                n = kind * H + 2 * hp
                first = (t[n : n + 1, :] + ROUND) - ROUND
                tabs[3 * hp + kind : 3 * hp + kind + 1, :] = first + t[n + 1 : n + 2, :] * SMALL

        mpos = lax.broadcasted_iota(jnp.int32, (8, span), 1) - (length - 128)
        ipos = lax.broadcasted_iota(jnp.int32, (8, span), 0)

        def body(g, carry):
            sl = pl.ds(pl.multiple_of(g * 8, 8), 8)
            index = bucket_of(mpos - (ipos + g * 8), 0)
            for hp in range(H // 2):
                table = jnp.broadcast_to(tabs[3 * hp : 3 * hp + 1, :], (8, 128))
                for c in range(0, span, 128):
                    a, b = unpack(look_up(table, index[:, c : c + 128]))
                    line[2 * hp, sl, c : c + 128] = a
                    line[2 * hp + 1, sl, c : c + 128] = b
            return carry

        lax.fori_loop(0, 16, body, 0)

    @pl.when(it == 0)
    def _():
        coords = jnp.concatenate([box_ref[m, pl.ds(w, 1), :] for m in range(4)] * 2, 0).astype(F32)
        by_token = coords.T
        cols[:, 0:8] = by_token
        lane = lax.broadcasted_iota(jnp.int32, (1, BOXF), 1)
        which = lane >> 5
        coord = jnp.where(
            which < 2,
            jnp.where(which == 0, by_token[:, 0:1], by_token[:, 1:2]),
            jnp.where(which == 2, by_token[:, 2:3], by_token[:, 3:4]),
        )
        feat_ref[...] = sine(coord * freq_ref[0:1, :], (lane >> 4) & 1).astype(BF)

    dead = lax.broadcasted_iota(jnp.int32, (1, length), 1) >= len_ref[w]
    first = it * tile
    line_lane = (length - 128) - (first // 128) * 128
    line_row = first % 128
    here = cols[pl.ds(pl.multiple_of(first, tile), tile), 0:8].astype(jnp.int32)
    for t in range(2):
        index = bucket_of(box_ref[t, pl.ds(w, 1), :] - here[:, t : t + 1], 2)
        map_ref[0, t] = index.astype(BF)
        maps[t] = index

    def body(g, carry):
        sl = pl.ds(pl.multiple_of(g * rows, rows), rows)
        ls = pl.ds(pl.multiple_of(line_row + g * rows, rows), rows)
        for hp in range(H // 2):
            ta = jnp.broadcast_to(tabs[3 * hp + 1 : 3 * hp + 2, :], (rows, 128))
            td = jnp.broadcast_to(tabs[3 * hp + 2 : 3 * hp + 3, :], (rows, 128))
            for c in range(0, length, 128):
                cs = slice(c, c + 128)
                lc = pl.ds(pl.multiple_of(line_lane + c, 128), 128)
                a, b = unpack(look_up(ta, maps[0, sl, cs]) + look_up(td, maps[1, sl, cs]))
                a = jnp.where(dead[:, cs], -1e9 * LOG2E, a + line[2 * hp, ls, lc])
                b = jnp.where(dead[:, cs], -1e9 * LOG2E, b + line[2 * hp + 1, ls, lc])
                out_ref[0, 2 * hp, sl, cs] = a.astype(BF)
                out_ref[0, 2 * hp + 1, sl, cs] = b.astype(BF)
        return carry

    lax.fori_loop(0, tile // rows, body, 0)


def score_bias(lengths, boxes, rel_tables):
    _, windows, length = boxes.shape
    tile, rows = 64, 32
    span = (2 * (length // 128) - 1) * 128
    freq_count = BOXF // 8
    freqs = np.float32(1000.0) ** (-np.arange(freq_count, dtype=np.float32) / np.float32(freq_count))
    freqs = jnp.asarray(np.tile(freqs.astype(np.float32), (8, 8)))
    return pl.pallas_call(
        partial(bias_kernel, tile=tile, rows=rows),
        grid=(windows, length // tile),
        in_specs=[
            pl.BlockSpec(memory_space=pltpu.SMEM),
            pl.BlockSpec((4, windows, length), lambda w, i: (0, 0, 0)),
            pl.BlockSpec((NB, 3 * H), lambda w, i: (0, 0)),
            pl.BlockSpec((8, BOXF), lambda w, i: (0, 0)),
        ],
        out_specs=[
            pl.BlockSpec((1, H, tile, length), lambda w, i: (w, 0, i, 0)),
            pl.BlockSpec((1, 2, tile, length), lambda w, i: (w, 0, i, 0)),
            pl.BlockSpec((length, BOXF), lambda w, i: (w, 0)),
        ],
        out_shape=[
            jax.ShapeDtypeStruct((windows, H, length, length), BF),
            jax.ShapeDtypeStruct((windows, 2, length, length), BF),
            jax.ShapeDtypeStruct((windows * length, BOXF), BF),
        ],
        scratch_shapes=[
            pltpu.VMEM((H, 128, span), F32),
            pltpu.VMEM((2, tile, length), jnp.int32),
            pltpu.VMEM((3 * H // 2 + 6, 128), F32),
            pltpu.VMEM((length, 128), F32),
        ],
        compiler_params=pltpu.CompilerParams(vmem_limit_bytes=VMEM),
        cost_estimate=SHORT,
        name="score_bias",
    )(lengths, boxes, rel_tables, freqs)


def attend_kernel(len_ref, q_ref, k_ref, v_ref, b_ref, o_ref, e_ref, r_ref, *, chunk):
    length = q_ref.shape[0]
    lane = lax.broadcasted_iota(jnp.int32, (length, 128), 1)
    live = lax.broadcasted_iota(jnp.int32, (length, 128), 0) < len_ref[pl.program_id(0)]
    zero, one = jnp.zeros((), BF), jnp.ones((), BF)
    q, k, v = q_ref[...], k_ref[...], v_ref[...]
    outs = []
    for h in range(2):
        mine = (lane < DH) if h == 0 else (lane >= DH)
        keys = jnp.where(mine & live, k, zero)
        values = jnp.where(mine, v, jnp.where(lane == (DH if h == 0 else 0), one, zero))
        scores = dot(q, keys, 1, 1)
        for c in range(0, length, chunk):
            t = scores[c : c + chunk] * (LOG2E * DH**-0.5) + b_ref[0, h, c : c + chunk, :].astype(F32)
            e_ref[0, h, c : c + chunk, :] = jnp.exp2(t - jnp.max(t, 1, keepdims=True)).astype(BF)
        outs.append(dot(e_ref[0, h], values))
    r = jnp.where(lane < DH, 1.0 / outs[0][:, DH : DH + 1], 1.0 / outs[1][:, 0:1])
    r_ref[...] = r
    o_ref[...] = (jnp.where(lane < DH, outs[0], outs[1]) * r).astype(BF)


def attend(lengths, qkv, bias):
    windows, _, length, _ = bias.shape
    pairs = H // 2
    col = lambda off: pl.BlockSpec((length, 128), lambda w, h: (w, off + h))
    sq = pl.BlockSpec((1, 2, length, length), lambda w, h: (w, h, 0, 0))
    width = H * DH
    return pl.pallas_call(
        partial(attend_kernel, chunk=64),
        grid=(windows, pairs),
        in_specs=[pl.BlockSpec(memory_space=pltpu.SMEM), col(0), col(pairs), col(2 * pairs), sq],
        out_specs=[col(0), sq, col(0)],
        out_shape=[
            jax.ShapeDtypeStruct((windows * length, width), BF),
            jax.ShapeDtypeStruct((windows, H, length, length), BF),
            jax.ShapeDtypeStruct((windows * length, width), F32),
        ],
        compiler_params=pltpu.CompilerParams(vmem_limit_bytes=VMEM),
        cost_estimate=SHORT,
        name="attend",
    )(lengths, qkv, qkv, qkv, bias)


def attend_back_kernel(q_ref, k_ref, v_ref, e_ref, r_ref, o_ref, do_ref, *refs, chunk):
    d_ref, ds_ref, line_ref, sum_ref = refs[-4:]
    length = q_ref.shape[0]
    blocks = length // 128
    w = pl.program_id(1)
    lane = lax.broadcasted_iota(jnp.int32, (length, 128), 1)
    zero = jnp.zeros((), BF)
    q, k, v = q_ref[...], k_ref[...], v_ref[...]
    up = do_ref[...].astype(F32) * r_ref[...]
    both = up * o_ref[...].astype(F32)
    up = up.astype(BF)
    up_t, q_t = up.T, q.T
    dq, dv_t, dk_t = None, [], []
    for h in range(2):
        mine = (lane < DH) if h == 0 else (lane >= DH)
        center = jnp.sum(jnp.where(mine, both, 0.0), 1, keepdims=True)
        dp = dot(up, jnp.where(mine, v, zero), 1, 1)
        for c in range(0, length, chunk):
            e = e_ref[0, h, c : c + chunk, :].astype(F32)
            ds_ref[0, h, c : c + chunk, :] = (e * (dp[c : c + chunk] - center[c : c + chunk])).astype(BF)
        for d in range(2 * blocks - 1):
            total = None
            for ib in range(blocks):
                jb = d - (blocks - 1) + ib
                if 0 <= jb < blocks:
                    part = ds_ref[0, h, ib * 128 : (ib + 1) * 128, jb * 128 : (jb + 1) * 128].astype(F32)
                    total = part if total is None else total + part

            @pl.when(w == 0)
            def _():
                line_ref[h, :, d * 128 : (d + 1) * 128] = total

            @pl.when(w != 0)
            def _():
                line_ref[h, :, d * 128 : (d + 1) * 128] += total

        ds = ds_ref[0, h]
        part = dot(ds, jnp.where(mine, k, zero))
        dq = part if dq is None else dq + part
        dv_t.append(dot(up_t[h * DH : (h + 1) * DH], e_ref[0, h]))
        dk_t.append(dot(q_t[h * DH : (h + 1) * DH], ds))
    parts = (dq * DH**-0.5, jnp.concatenate(dk_t, 0).T * DH**-0.5, jnp.concatenate(dv_t, 0).T)
    for n, x in enumerate(parts):
        cols = slice(n * 128, (n + 1) * 128)
        x = x.astype(BF)
        d_ref[:, cols] = x
        sums = jnp.broadcast_to(column_sums(x.astype(F32)), (8, 128))
        sum_ref[:, cols] = jnp.where(w == 0, sums, sum_ref[:, cols] + sums)


def attend_back(qkv, e, r, o, do, first, count, total, at, before=None):
    windows, _, length, _ = e.shape
    pairs = H // 2
    col = lambda off: pl.BlockSpec((length, 128), lambda h, w: (w, off + h))
    sq = pl.BlockSpec((1, 2, length, length), lambda h, w: (w, first + h, 0, 0))
    span = (2 * (length // 128) - 1) * 128
    more = [] if before is None else [before]
    return pl.pallas_call(
        partial(attend_back_kernel, chunk=64),
        grid=(count, windows),
        in_specs=[col(first), col(pairs + first), col(2 * pairs + first), sq, col(first), col(first), col(first)]
        + [pl.BlockSpec(memory_space=pl.ANY)] * len(more),
        out_specs=[
            pl.BlockSpec((length, 384), lambda h, w: (w, at + h)),
            pl.BlockSpec((1, 2, length, length), lambda h, w: (w, h, 0, 0)),
            pl.BlockSpec((2, 128, span), lambda h, w: (h, 0, 0)),
            pl.BlockSpec((8, 384), lambda h, w: (0, h)),
        ],
        out_shape=[
            jax.ShapeDtypeStruct((windows * length, total * 384), BF),
            jax.ShapeDtypeStruct((windows, 2 * count, length, length), BF),
            jax.ShapeDtypeStruct((2 * count, 128, span), F32),
            jax.ShapeDtypeStruct((8, count * 384), F32),
        ],
        input_output_aliases={7: 0} if more else {},
        compiler_params=pltpu.CompilerParams(vmem_limit_bytes=VMEM),
        cost_estimate=SHORT,
        name="attend_back",
    )(qkv, qkv, qkv, e, r, o, do, *more)


def spread(refs, rows, stride):
    h = 0
    for ref in refs:
        for n in range(ref.shape[-3]):
            x = (ref[0, n] if len(ref.shape) == 4 else ref[n]).astype(F32)
            for c in range(x.shape[1] // 128):
                rows[c, h * stride : h * stride + x.shape[0], :] = x[:, c * 128 : (c + 1) * 128]
            h += 1


def heads_of(rows, i, stride):
    return [rows[c, pl.ds(i, 16, stride=stride), :].astype(BF) for c in range(rows.shape[0])]


def one_hot(index):
    width = index.shape[1]
    ids = lax.broadcasted_iota(jnp.int32, (NB, width), 0).astype(BF)
    hit = jnp.broadcast_to(index, (NB, width)).astype(BF) == ids
    return jnp.where(hit, jnp.ones((), BF), jnp.zeros((), BF))


def table_kernel(*refs, parts, with_line):
    ds_refs, refs = refs[:parts], refs[parts:]
    line_refs, refs = refs[: parts * with_line], refs[parts * with_line :]
    map_ref, out_ref, rows, maps = refs[0], refs[1], refs[-2], refs[-1]
    tile = map_ref.shape[2]
    step = pl.program_id(0)

    @pl.when(step == 0)
    def _():
        out_ref[...] = jnp.zeros_like(out_ref)
        rows[...] = jnp.zeros_like(rows)

    if with_line:
        line_out, line_rows = refs[2], refs[3]
        share = line_refs[0].shape[1]
        span = line_refs[0].shape[2]

        @pl.when(step == 0)
        def _():
            line_out[...] = jnp.zeros_like(line_out)
            line_rows[...] = jnp.zeros_like(line_rows)

        spread(line_refs, line_rows, share + 8)
        offset = lax.broadcasted_iota(jnp.int32, (8, span), 1) - (span - 128) // 2
        down = lax.broadcasted_iota(jnp.int32, (8, span), 0) + step * share
        lhs, rhs = [], []
        for i in range(share):
            if i % 8 == 0:
                index = bucket_of(offset - (down + i), 0).astype(F32)
            lhs += heads_of(line_rows, i, share + 8)
            rhs.append(one_hot(index[i % 8 : i % 8 + 1, :]))
        line_out[...] += dot(jnp.concatenate(lhs, 1), jnp.concatenate(rhs, 1), 1, 1)

    spread(ds_refs, rows, tile + 8)
    maps[...] = map_ref[0].astype(F32)
    lhs, rhs = [], []
    for i in range(tile):
        lhs += heads_of(rows, i, tile + 8)
        rhs.append(jnp.concatenate([one_hot(maps[t, i : i + 1, :]) for t in range(2)], 0))
    out_ref[...] += dot(jnp.concatenate(lhs, 1), jnp.concatenate(rhs, 1), 1, 1)


def table_grads(ds_parts, lines, maps, w):
    _, _, length, _ = maps.shape
    tile = 64
    parts = len(ds_parts)
    steps = length // tile
    outs, out_shapes = [pl.BlockSpec((16, 2 * NB), lambda i: (0, 0))], [jax.ShapeDtypeStruct((16, 2 * NB), F32)]
    line_specs, line_rows = [], []
    if lines:
        share, span = 128 // steps, lines[0].shape[2]
        line_specs = [pl.BlockSpec((x.shape[0], share, span), lambda i: (0, i, 0)) for x in lines]
        line_rows = [pltpu.VMEM((span // 128, 16 * (share + 8), 128), F32)]
        outs.append(pl.BlockSpec((16, NB), lambda i: (0, 0)))
        out_shapes.append(jax.ShapeDtypeStruct((16, NB), F32))
    return pl.pallas_call(
        partial(table_kernel, parts=parts, with_line=bool(lines)),
        grid=(steps,),
        in_specs=[pl.BlockSpec((1, x.shape[1], tile, length), lambda i: (w, 0, i, 0)) for x in ds_parts]
        + line_specs
        + [pl.BlockSpec((1, 2, tile, length), lambda i: (w, 0, i, 0))],
        out_specs=outs,
        out_shape=out_shapes,
        scratch_shapes=line_rows
        + [pltpu.VMEM((length // 128, 16 * (tile + 8), 128), F32), pltpu.VMEM((2, tile, length), F32)],
        compiler_params=pltpu.CompilerParams(vmem_limit_bytes=VMEM),
        cost_estimate=SHORT,
        name="table_grads",
    )(*ds_parts, *lines, maps)


def gelu_both(x):
    t = 1.0 / (1.0 + (0.3275911 * 0.7071067811865476) * jnp.abs(x))
    e = jnp.exp2((-0.5 * LOG2E) * (x * x))
    poly = t * (
        0.5 * 0.254829592
        + t * (0.5 * -0.284496736 + t * (0.5 * 1.421413741 + t * (0.5 * -1.453152027 + t * (0.5 * 1.061405429))))
    )
    tail = poly * e
    cdf = jnp.where(x >= 0, 1.0 - tail, tail)
    return x * cdf, cdf + x * (e * 0.3989422804014327)


def norm_forward(summed, params):
    centered = summed - jnp.mean(summed, -1, keepdims=True)
    inverse = lax.rsqrt(jnp.mean(centered * centered, -1, keepdims=True) + EPS)
    normed = centered * inverse
    return normed * params[0:1] + params[1:2], normed, inverse


def norm_backward(upstream, normed, inverse, params):
    scaled = upstream * params[0:1]
    return inverse * (
        scaled - jnp.mean(scaled, -1, keepdims=True) - normed * jnp.mean(scaled * normed, -1, keepdims=True)
    )


def column_sums(x):
    return jnp.sum(x, 0, keepdims=True)


def feed_kernel(sec_ref, low_ref, w1_ref, b1_ref, w2_ref, b2_ref, n2_ref, cot_ref, act_ref, slope_ref, out_ref, dsum_ref, dlow_ref, sum_ref, acc, *, chunk):
    step = pl.program_id(0)
    tokens = low_ref.shape[0]

    @pl.when(step == 0)
    def _():
        acc[...] = jnp.zeros_like(acc)

    for c in range(0, tokens, chunk):
        cs = slice(c, c + chunk)
        active, slope = gelu_both(dot(low_ref[cs, :], w1_ref[...]) + b1_ref[...])
        active = active.astype(BF)
        act_ref[cs, :] = active
        slope_ref[cs, :] = slope.astype(BF)
        acc[cs, :] += dot(active, w2_ref[...])

    @pl.when(step == pl.num_programs(0) - 1)
    def _():
        sums = [0.0, 0.0, 0.0]
        for c in range(0, tokens, 128):
            cs = slice(c, c + 128)
            result, normed, inverse = norm_forward(sec_ref[cs, :] + (acc[cs, :] + b2_ref[...]), n2_ref[...])
            out_ref[cs, :] = result.astype(BF)
            up = cot_ref[cs, :].astype(F32)
            grad = norm_backward(up, normed, inverse, n2_ref[...])
            low = grad.astype(BF)
            dsum_ref[cs, :] = grad
            dlow_ref[cs, :] = low
            sums = [sums[0] + column_sums(up * normed), sums[1] + column_sums(up), sums[2] + column_sums(low.astype(F32))]
        sum_ref[...] = jnp.concatenate(sums + [jnp.zeros((5, sums[0].shape[1]), F32)], 0)


def feed(second, second_low, w1, b1, w2, b2, norm_two, cotangent):
    tokens, width = second.shape
    hidden = w1.shape[1]
    tile = 512
    whole = lambda shape: pl.BlockSpec(shape, lambda n: (0, 0))
    return pl.pallas_call(
        partial(feed_kernel, chunk=256),
        grid=(hidden // tile,),
        in_specs=[
            whole((tokens, width)),
            whole((tokens, width)),
            pl.BlockSpec((width, tile), lambda n: (0, n)),
            pl.BlockSpec((1, tile), lambda n: (0, n)),
            pl.BlockSpec((tile, width), lambda n: (n, 0)),
            whole((1, width)),
            whole((2, width)),
            whole((tokens, width)),
        ],
        out_specs=[
            pl.BlockSpec((tokens, tile), lambda n: (0, n)),
            pl.BlockSpec((tokens, tile), lambda n: (0, n)),
            whole((tokens, width)),
            whole((tokens, width)),
            whole((tokens, width)),
            whole((8, width)),
        ],
        out_shape=[
            jax.ShapeDtypeStruct((tokens, hidden), BF),
            jax.ShapeDtypeStruct((tokens, hidden), BF),
            jax.ShapeDtypeStruct((tokens, width), BF),
            jax.ShapeDtypeStruct((tokens, width), F32),
            jax.ShapeDtypeStruct((tokens, width), BF),
            jax.ShapeDtypeStruct((8, width), F32),
        ],
        scratch_shapes=[pltpu.VMEM((tokens, width), F32)],
        compiler_params=pltpu.CompilerParams(vmem_limit_bytes=VMEM),
        cost_estimate=SHORT,
        name="feed",
    )(second, second_low, w1, b1.reshape(1, -1), w2, b2.reshape(1, -1), norm_two, cotangent)


def feed_back_kernel(dlow_ref, dsum_ref, w1_ref, w2_ref, slope_ref, z_ref, n1_ref, din_ref, bias_ref, done_ref, dbr_ref, sum_ref, acc, *, chunk):
    step = pl.program_id(0)
    tokens = dlow_ref.shape[0]

    @pl.when(step == 0)
    def _():
        acc[...] = dsum_ref[...]

    sums = 0.0
    for c in range(0, tokens, chunk):
        cs = slice(c, c + chunk)
        d_inner = (dot(dlow_ref[cs, :], w2_ref[...], 1, 1) * slope_ref[cs, :].astype(F32)).astype(BF)
        din_ref[cs, :] = d_inner
        sums = sums + column_sums(d_inner.astype(F32))
        acc[cs, :] += dot(d_inner, w1_ref[...], 1, 1)
    bias_ref[...] = jnp.concatenate([sums, jnp.zeros((7, sums.shape[1]), F32)], 0)

    @pl.when(step == pl.num_programs(0) - 1)
    def _():
        totals = [0.0, 0.0, 0.0]
        for c in range(0, tokens, 128):
            cs = slice(c, c + 128)
            _, normed, inverse = norm_forward(z_ref[cs, :], n1_ref[...])
            up = acc[cs, :]
            grad = norm_backward(up, normed, inverse, n1_ref[...])
            low = grad.astype(BF)
            done_ref[cs, :] = grad
            dbr_ref[cs, :] = low
            totals = [
                totals[0] + column_sums(up * normed),
                totals[1] + column_sums(up),
                totals[2] + column_sums(low.astype(F32)),
            ]
        sum_ref[...] = jnp.concatenate(totals + [jnp.zeros((5, totals[0].shape[1]), F32)], 0)


def feed_back(d_outer, d_sum_two, w1, w2, slope, z_one, norm_one):
    tokens, width = z_one.shape
    hidden = w1.shape[1]
    tile = 512
    whole = lambda shape: pl.BlockSpec(shape, lambda n: (0, 0))
    return pl.pallas_call(
        partial(feed_back_kernel, chunk=256),
        grid=(hidden // tile,),
        in_specs=[
            whole((tokens, width)),
            whole((tokens, width)),
            pl.BlockSpec((width, tile), lambda n: (0, n)),
            pl.BlockSpec((tile, width), lambda n: (n, 0)),
            pl.BlockSpec((tokens, tile), lambda n: (0, n)),
            whole((tokens, width)),
            whole((2, width)),
        ],
        out_specs=[
            pl.BlockSpec((tokens, tile), lambda n: (0, n)),
            pl.BlockSpec((8, tile), lambda n: (0, n)),
            whole((tokens, width)),
            whole((tokens, width)),
            whole((8, width)),
        ],
        out_shape=[
            jax.ShapeDtypeStruct((tokens, hidden), BF),
            jax.ShapeDtypeStruct((8, hidden), F32),
            jax.ShapeDtypeStruct((tokens, width), F32),
            jax.ShapeDtypeStruct((tokens, width), BF),
            jax.ShapeDtypeStruct((8, width), F32),
        ],
        scratch_shapes=[pltpu.VMEM((tokens, width), F32)],
        compiler_params=pltpu.CompilerParams(vmem_limit_bytes=VMEM),
        cost_estimate=SHORT,
        name="feed_back",
    )(d_outer, d_sum_two, w1, w2, slope, z_one, norm_one)


UNIT = 384
PIECES = 2


def halves(full, place_ref):
    rows = full.shape[0] // 2
    upper = place_ref[1] == 0
    low, high = full[:rows], full[rows:]
    return jnp.where(upper, high, low).astype(BF), jnp.where(upper, low, high).astype(BF)


def wide_grads_kernel(place_ref, *refs, counts):
    step = pl.program_id(0)
    pairs = len(counts)
    outs, turned = refs[3 * pairs : -1], refs[-1]
    at = 0
    for n, count in enumerate(counts):

        @pl.when(step == at)
        def _():
            turned[...] = refs[3 * n][...].T

        @pl.when((step >= at) & (step < at + count))
        def _():
            full = dot(turned[...], jnp.concatenate([refs[3 * n + 1][...], refs[3 * n + 2][...]], 1))
            both = halves(full, place_ref)
            for m, x in enumerate(both):
                side = x.shape[0] // 2
                for k in range(2):
                    outs[2 * m + k][...] = x[k * side : (k + 1) * side, :UNIT].reshape(outs[2 * m + k].shape)
                outs[4 + m][...] = x[:, UNIT:].reshape(outs[4 + m].shape)

        at += count


def wide_grads(place, pairs):
    tokens, rows = pairs[0][0].shape
    counts = [right.shape[1] // (2 * UNIT) for _, right in pairs]
    specs, at = [], 0
    for (left, right), count in zip(pairs, counts):

        def block(i, p, send, at=at, count=count):
            owner = 1 - p[0] if send else p[0]
            return (0, owner * count + jnp.clip(i - at, 0, count - 1))

        specs += [
            pl.BlockSpec(left.shape, lambda i, p: (0, 0)),
            pl.BlockSpec((tokens, UNIT), partial(block, send=True)),
            pl.BlockSpec((tokens, UNIT), partial(block, send=False)),
        ]
        at += count
    piece = pl.BlockSpec((1, 1, rows // 4, UNIT), lambda i, p: (0, i, 0, 0))
    out = pl.BlockSpec((2, 1, rows // 4, UNIT), lambda i, p: (0, i, 0, 0))
    outs = pl.pallas_call(
        partial(wide_grads_kernel, counts=counts),
        grid_spec=pltpu.PrefetchScalarGridSpec(
            num_scalar_prefetch=1,
            grid=(at,),
            in_specs=specs,
            out_specs=[piece] * 4 + [out] * 2,
            scratch_shapes=[pltpu.VMEM((rows, tokens), BF)],
        ),
        out_shape=[jax.ShapeDtypeStruct((n, at, rows // 4, UNIT), BF) for n in (1, 1, 1, 1, 2, 2)],
        compiler_params=pltpu.CompilerParams(vmem_limit_bytes=VMEM),
        cost_estimate=SHORT,
        name="wide_grads",
    )(place, *[x for left, right in pairs for x in (left, right, right)])
    return [x.reshape(-1, UNIT) for x in outs]


def long_grads_kernel(place_ref, left_ref, send_ref, keep_ref, *outs):
    full = dot(left_ref[...], jnp.concatenate([send_ref[...], keep_ref[...]], 1), 0, 0).astype(BF)
    for n in range(4):

        @pl.when(pl.program_id(0) == n)
        def _():
            outs[n][...] = full[:, :UNIT]
            outs[4 + n // 2][...] = full[:, UNIT:]


def long_grads(place, left, right):
    tokens, rows = left.shape
    tile = rows // 4

    def quarter(i, p):
        owner = jnp.where(i < 2, 1 - p[1], p[1])
        return (0, owner * 2 + lax.rem(i, 2))

    piece = pl.BlockSpec((tile, UNIT), lambda i, p: (0, 0))
    other = pl.BlockSpec((tile, UNIT), lambda i, p: (jnp.minimum(i, 1), 0))
    own = pl.BlockSpec((tile, UNIT), lambda i, p: (jnp.maximum(i - 2, 0), 0))
    return pl.pallas_call(
        long_grads_kernel,
        grid_spec=pltpu.PrefetchScalarGridSpec(
            num_scalar_prefetch=1,
            grid=(4,),
            in_specs=[
                pl.BlockSpec((tokens, tile), quarter),
                pl.BlockSpec((tokens, UNIT), lambda i, p: (0, 1 - p[0])),
                pl.BlockSpec((tokens, UNIT), lambda i, p: (0, p[0])),
            ],
            out_specs=[piece] * 4 + [other, own],
        ),
        out_shape=[jax.ShapeDtypeStruct((n * tile, UNIT), BF) for n in (1, 1, 1, 1, 2, 2)],
        compiler_params=pltpu.CompilerParams(vmem_limit_bytes=VMEM),
        cost_estimate=SHORT,
        name="long_grads",
    )(place, left, right, right)


E_ROWS = 16


def last_kernel(place_ref, x_ref, dx_ref, f_ref, df_ref, two_ref, one_ref, in_ref, *refs):
    qv_refs, (line_ref, small0_ref, small1_ref), outs = refs[:3], refs[3:6], refs[6:]
    mine = place_ref[0] == 0
    upper = place_ref[1] == 0
    width = x_ref.shape[1]
    middle = width // 2
    x = dot(x_ref[...], dx_ref[...], 0, 0).astype(BF)
    box = dot(f_ref[...], df_ref[...], 0, 0).astype(BF)
    tables = jnp.concatenate([line_ref[...], small0_ref[...] + small1_ref[...], jnp.zeros((16, NB), F32)], 1).T
    blocks = [ref[0:1, p : p + UNIT] for ref in qv_refs for p in range(0, ref.shape[1], UNIT)]
    qv = [jnp.concatenate([y[:, at : at + 128] for y in blocks], 1) for at in (0, 256)]
    halves_of = []
    for n in range(2):
        cols = slice(n * middle, (n + 1) * middle)
        inner = in_ref[0:1, n * 2 * width : (n + 1) * 2 * width]
        sums = [
            two_ref[n : n + 1, :],
            one_ref[n : n + 1, :],
            qv[n],
            jnp.concatenate([one_ref[2:3, cols], two_ref[2:3, cols]], 1),
            inner[:, :width],
            inner[:, width:],
            jnp.zeros((E_ROWS - 6, width), F32),
        ]
        share = [tables[m * NB + n * NB // 2 : m * NB + (n + 1) * NB // 2, :] for m in range(3)]
        share = [jnp.pad(t, ((0, 0), (0, 128 - t.shape[1]))) for t in share]
        sides = [jnp.concatenate(sums, 0), jnp.concatenate(share + [jnp.zeros((E_ROWS, width - 3 * 128), F32)], 1)]
        q, h = x.shape[0] // 4, box.shape[0] // 4
        halves_of.append(
            jnp.concatenate(
                [
                    y
                    for m in range(2)
                    for y in (
                        x[(2 * n + m) * q : (2 * n + m + 1) * q],
                        box[(2 * n + m) * h : (2 * n + m + 1) * h],
                        sides[m].astype(BF),
                    )
                ],
                0,
            )
        )
    for m in range(2):
        rows = jnp.where(upper, halves_of[1 - m], halves_of[m])
        send = jnp.where(mine, rows[:, middle:], rows[:, :middle])
        side = send.shape[0] // 2
        outs[2 * m][...] = send[:side]
        outs[2 * m + 1][...] = send[side:]
        outs[4 + m][...] = jnp.where(mine, rows[:, :middle], rows[:, middle:])


def last_grads(place, x, dx, f, df, *sums):
    rows = (x.shape[1] + f.shape[1]) // 4 + E_ROWS
    vmem = pl.BlockSpec(memory_space=pltpu.VMEM)
    return pl.pallas_call(
        last_kernel,
        in_specs=[pl.BlockSpec(memory_space=pltpu.SMEM)] + [vmem] * (4 + len(sums)),
        out_specs=[vmem] * 6,
        out_shape=[jax.ShapeDtypeStruct((n * rows, UNIT), BF) for n in (1, 1, 1, 1, 2, 2)],
        compiler_params=pltpu.CompilerParams(vmem_limit_bytes=VMEM),
        cost_estimate=SHORT,
        name="last_grads",
    )(place, x, dx, f, df, *sums)


def lay_kernel(place_ref, *refs, kind, rows):
    pieces, outs = refs[:4], refs[4:]
    core, side = place_ref[0], place_ref[2]
    step = pl.program_id(0)

    def lay_piece(ref, owner):
        blocks = ref.shape[0] // rows
        for n in range(ref.shape[0] // rows if kind != "heads" else 3):
            x = ref[n * rows : (n + 1) * rows, :].astype(F32)
            if kind == "long":
                outs[0][n * rows : (n + 1) * rows, owner * UNIT : (owner + 1) * UNIT] = x
            elif kind == "wide":
                at = (owner * blocks + n) * UNIT
                outs[0][:, at : at + UNIT] = x
            elif n == 0:
                outs[0][:, owner * UNIT : (owner + 1) * UNIT] = x
            else:
                lay_pair(x, owner * 2 + n - 1)
        if kind == "heads":
            lay_pair(ref[3 * rows : 4 * rows, :].astype(F32), 4 + owner)
            at = 4 * rows
            box = BOXF // 4
            cols = slice(owner * UNIT, (owner + 1) * UNIT)
            outs[2][:, cols] = ref[at : at + box, :].astype(F32)
            small = ref[at + box : at + box + E_ROWS, :].astype(F32)

            @pl.when(step == 0)
            def _():
                for n in range(3):
                    outs[3 + n][:, cols] = small[n : n + 1]
                outs[6 + owner][...] = small[3:4]
                for n in range(2):
                    at = n * 2 * UNIT + owner * UNIT
                    outs[8][:, at : at + UNIT] = small[4 + n : 5 + n]

            if owner == 0:

                @pl.when(step == 1)
                def _():
                    outs[9][...] = jnp.concatenate([small[:, n * 128 : n * 128 + H] for n in range(3)], 1)

    def lay_pair(x, pair):
        for m in range(3):
            at = (m * (H // 2) + pair) * 128
            outs[1][:, at : at + 128] = x[:, m * 128 : (m + 1) * 128]

    for other_side in range(2):
        for owner in range(2):
            for other_core in range(2):

                @pl.when(((step == side) == (other_side == 0)) & (core == (owner ^ other_core)))
                def _():
                    lay_piece(pieces[2 * other_side + other_core], owner)


def lay(place, pieces, kind, rows):
    blocks = pieces[0].shape[0] // rows
    whole = None
    if kind == "long":
        shapes = [(2 * blocks * rows, 2 * UNIT)]
    elif kind == "wide":
        shapes = [(2 * rows, 2 * blocks * UNIT)]
    else:
        width = 2 * UNIT
        shapes = [(2 * rows, width), (2 * rows, 3 * width), (BOXF // 2, width)]
        whole = [(1, width)] * 3 + [(1, UNIT)] * 2 + [(1, 2 * width), (NB // 2, 3 * H)]
    return pl.pallas_call(
        partial(lay_kernel, kind=kind, rows=rows),
        grid=(2,),
        in_specs=[pl.BlockSpec(memory_space=pltpu.SMEM)] + [pl.BlockSpec(x.shape, lambda i: (0, 0)) for x in pieces],
        out_specs=[pl.BlockSpec((m // 2, n), lambda i: (i, 0)) for m, n in shapes]
        + [pl.BlockSpec(shape, lambda i: (0, 0)) for shape in whole or []],
        out_shape=[jax.ShapeDtypeStruct(shape, F32) for shape in shapes + (whole or [])],
        compiler_params=pltpu.CompilerParams(vmem_limit_bytes=VMEM),
        cost_estimate=SHORT,
        name="lay",
    )(place, *pieces)


def entry_kernel(a_ref, b_ref, w_ref, sum_ref, out_ref):
    pairs = H // 2
    weight = jnp.concatenate([w_ref[:, (m * pairs + n) * 128 : (m * pairs + n + 1) * 128] for n in range(pairs) for m in range(3)], 1)
    both = jnp.concatenate([a_ref[...], b_ref[...]], 1)
    out_ref[...] = (sum_ref[...] + dot(both, weight, 1, 1)).astype(BF)


def entry_grad(first, last, weight, base):
    tokens, width = base.shape
    tile = tokens // 2
    row = lambda x: pl.BlockSpec((tile, x.shape[1]), lambda i: (i, 0))
    return pl.pallas_call(
        entry_kernel,
        grid=(tokens // tile,),
        in_specs=[row(first), row(last), pl.BlockSpec(weight.shape, lambda i: (0, 0)), row(base)],
        out_specs=row(base),
        out_shape=jax.ShapeDtypeStruct((tokens, width), BF),
        compiler_params=pltpu.CompilerParams(vmem_limit_bytes=VMEM),
        cost_estimate=SHORT,
        name="entry_grad",
    )(first, last, weight, base)


def shards(
    docs,
    hidden_in,
    boxes,
    lengths,
    box_weight,
    qkv_weight,
    qv_bias,
    out_weight,
    out_bias,
    rel_tables,
    norm_one,
    ffn_in_weight,
    ffn_in_bias,
    ffn_out_weight,
    ffn_out_bias,
    norm_two,
    cotangent,
):
    half = lax.axis_index("half")
    doc = lax.axis_index("doc")
    core, side = doc & 1, (doc >> 1) & 1
    own, local_len, width = hidden_in.shape
    windows = own // 2
    length = 2 * local_len
    tokens = windows * length

    def swap_half(x):
        return lax.ppermute(x, "half", [(0, 1), (1, 0)])

    def swap_doc(x, bit):
        return lax.ppermute(x, "doc", [(i, i ^ (1 << bit)) for i in range(docs)])

    def part(x, index, axis):
        if isinstance(x, tuple):
            return jnp.where(index == 0, *x)
        size = x.shape[axis] // 2
        return lax.dynamic_slice_in_dim(x, index * size, size, axis)

    def ordered(index, mine, other, axis):
        return jnp.where(index == 0, jnp.concatenate([mine, other], axis), jnp.concatenate([other, mine], axis))

    def whole_windows(x, axis):
        return ordered(half, part(x, half, axis), swap_half(part(x, 1 - half, axis)), axis + 1)

    def half_positions(x):
        return ordered(half, part(x, half, 1), swap_half(part(x, 1 - half, 1)), 0)

    def add(x, y):
        return (x.astype(F32) + y.astype(F32)).astype(BF)

    def tie(x, *others):
        return lax.optimization_barrier((x,) + others)[0]

    box_part = swap_half(part(boxes, 1 - half, 1))
    my_boxes = ordered(half, part(boxes, half, 1), box_part, 2)
    my_lengths = part(lengths, half, 0)
    hidden_send = part(tie(hidden_in, box_part), 1 - half, 0)
    hidden = ordered(half, part(hidden_in, half, 0), swap_half(hidden_send), 1).reshape(tokens, width)
    upstream = whole_windows(tie(cotangent, hidden_send), 0).reshape(tokens, width)

    bias, maps, features = score_bias(my_lengths, my_boxes, rel_tables)
    entry = hidden.astype(F32) + dot(features, box_weight)
    entry_low = entry.astype(BF)
    qkv_shift = jnp.concatenate([qv_bias[0], jnp.zeros_like(qv_bias[0]), qv_bias[1]])
    qkv = (dot(entry_low, qkv_weight) + qkv_shift).astype(BF)

    attended, e, r = attend(my_lengths, qkv, bias)
    z_one = entry + (dot(attended, out_weight) + out_bias)
    second = norm_forward(z_one, norm_one)[0]
    second_low = second.astype(BF)
    active, slope, result, d_sum_two, d_outer, sums_two = feed(
        second, second_low, ffn_in_weight, ffn_in_bias, ffn_out_weight, ffn_out_bias, norm_two, upstream
    )
    pairs, early = H // 2, H // 3
    late_pairs = pairs - early
    step = early // 2
    more = list(range(2, docs.bit_length() - 1))
    place = jnp.stack([core, half, side]).astype(jnp.int32)
    last = [None]

    def now(x):
        return x if last[0] is None else tie(x, last[0])

    def then(x):
        last[0] = x
        return x

    def total(*xs):
        out = xs[0].astype(F32)
        for x in xs[1:]:
            out = out + x.astype(F32)
        return out.astype(BF)

    class Chain:
        def core(self, *parts):
            send, send_own, keep, keep_own = parts[:PIECES], parts[PIECES:-2], parts[-2], parts[-1]
            then(keep_own)
            self.keep, self.come = keep, jnp.concatenate([swap_doc(x, 0) for x in send], 0)
            self.own = [keep_own, tuple(swap_doc(x, 0) for x in send_own)]

        def half(self):
            send = then(total(now(self.keep), self.come))
            self.own.append(swap_half(send))

        def split(self, bit):
            b = (doc >> bit) & 1
            own = [now(self.own[0])] + self.own[1:]
            send = then(total(*[part(x, 1 - b, 0) for x in own]))
            keep = total(*[part(x, b, 0) for x in own])
            self.own = [keep, swap_doc(send, bit)]

        def double(self, bits):
            x = then(total(now(self.own[0]), *self.own[1:]))
            for bit in bits[:-1]:
                x = total(x, swap_doc(x, bit))
            self.own = [x, swap_doc(x, bits[-1])]

        def gather(self):
            x = then(total(now(self.own[0]), *self.own[1:]))
            self.mine, self.across = x, swap_doc(x, 1)
            self.beside = swap_doc(x, 0)

        def pieces(self):
            return [now(self.mine), self.beside, self.across, swap_doc(self.across, 0)]

    def back(first, count, total_pairs, at, before):
        out = attend_back(qkv, e, r, attended, now(d_attended), first, count, total_pairs, at, before)
        then(out[0])
        return out

    a, b, c, d = Chain(), Chain(), Chain(), Chain()
    block_rows = width // 4
    then(d_outer)
    a.core(*long_grads(place, active, now(d_outer)))
    a.half()
    d_inner, sums_in, d_sum_one, d_branch, sums_one = feed_back(
        now(d_outer), d_sum_two, ffn_in_weight, ffn_out_weight, slope, z_one, norm_one
    )
    then(d_branch)
    a.split(1)
    b.core(*wide_grads(place, [(second_low, now(d_inner))]))
    d_attended = then(dot(now(d_branch), out_weight, 1, 1).astype(BF))
    a.double(more[:1])
    b.half()
    first_right, ds_0, line_0, qv_0 = back(0, step, early, 0, None)
    a.double(more[1:])
    first_right, ds_1, line_1, qv_1 = back(step, early - step, early, step, first_right)
    c.core(*wide_grads(place, [(attended, d_branch), (entry_low, now(first_right))]))
    b.split(1)
    c.half()
    result = result.reshape(windows, length, width)
    out_send = then(part(now(result), 1 - half, 1))
    out_mine, out_other = part(result, half, 1), swap_half(out_send)
    last_right, ds_2, line_2, qv_2 = back(early, late_pairs, late_pairs, 0, None)
    b.double(more[:1])
    small_0, line_grad = table_grads([ds_0, ds_1, now(ds_2)], [line_0, line_1, line_2], maps, 0)
    then(small_0)
    a.gather()
    c.split(1)
    b.double(more[1:])
    layer_out = then(ordered(half, now(out_mine), out_other, 0))
    small_1 = table_grads([ds_0, ds_1, now(ds_2)], [], maps, 1)[0]
    for w in range(2, windows):
        small_1 = small_1 + table_grads([ds_0, ds_1, ds_2], [], maps, w)[0]
    then(small_1)
    c.double(more[:1])
    d_entry_low = then(entry_grad(first_right, now(last_right), qkv_weight, d_sum_one))
    d.core(
        *last_grads(
            place, entry_low, last_right, features, now(d_entry_low), sums_two, sums_one, sums_in, qv_0, qv_1, qv_2, line_grad, small_0, small_1
        )
    )
    b.gather()
    c.double(more[1:])
    d.half()
    d_entry = d_entry_low.reshape(windows, length, width)
    grad_send = then(part(now(d_entry), 1 - half, 1))
    grad_mine, grad_other = part(d_entry, half, 1), swap_half(grad_send)
    (ffn_out_grad,) = lay(place, a.pieces(), "long", block_rows)
    then(ffn_out_grad)
    d.split(1)
    (ffn_in_grad,) = lay(place, b.pieces(), "wide", block_rows)
    then(ffn_in_grad)
    d.double(more[:1])
    hidden_grad = then(ordered(half, now(grad_mine), grad_other, 0))
    d.double(more[1:])
    parts = [total(now(c.own[0]), c.own[1]), total(d.own[0], d.own[1])]
    c.own = [then(jnp.concatenate(parts, 0))]
    c.gather()
    out_grad, qkv_grad, box, two, one, qv, out_sum, ffn_out_sum, ffn_in_sum, table = lay(
        place, c.pieces(), "heads", block_rows
    )
    return (
        layer_out,
        hidden_grad,
        box,
        qkv_grad,
        qv,
        out_grad,
        out_sum.reshape(-1),
        table,
        one,
        ffn_in_grad,
        ffn_in_sum.reshape(-1),
        ffn_out_grad,
        ffn_out_sum.reshape(-1),
        two,
    )


def solution(mesh):
    rep = P()
    rows = P("half", None)
    return jax.shard_map(
        partial(shards, mesh.shape["doc"]),
        mesh=mesh,
        in_specs=(P("doc", "half", None), P(None, "doc", "half"), P("doc")) + (rep,) * 12 + (P("doc", "half", None),),
        out_specs=(
            P("doc", "half", None),
            P("doc", "half", None),
            rows,
            rows,
            rows,
            rows,
            P("half"),
            rows,
            rows,
            rows,
            P("half"),
            rows,
            P("half"),
            rows,
        ),
        check_vma=False,
    )
```

```python
from functools import partial

import jax
import jax.numpy as jnp
import numpy as np
from jax import lax
from jax.experimental import pallas as pl
from jax.experimental.pallas import tpu as pltpu
from jax.sharding import PartitionSpec as P

H = 12
DH = 64
BOXF = 128
NB = 32
EPS = 1e-05
LOG2E = 1.4426950408889634
BF = jnp.bfloat16
F32 = jnp.float32
VMEM = 56 << 20
SHORT = pl.CostEstimate(flops=1, bytes_accessed=1, transcendentals=0)


def dot(a, b, ca=1, cb=0):
    return lax.dot_general(a, b, (((ca,), (cb,)), ((), ())), preferred_element_type=F32)


ROUND = 1.5 * 2.0**23 * 2.0**-8
SMALL = 1.6e-4


def unpack(both):
    first = (both + ROUND) - ROUND
    return first, (both - first) * (1.0 / SMALL)


def bucket_of(offset, shift):
    magnitude = jnp.abs(offset)
    if shift:
        magnitude = magnitude >> shift
    count = jnp.minimum(magnitude, 8)
    for n, bound in enumerate((12, 16, 24, 32, 48, 64, 96)):
        count = jnp.where(magnitude >= bound, 9 + n, count)
    return jnp.where(offset > 0, count + 16, count)


def look_up(table, index):
    dims = lax.GatherDimensionNumbers(
        offset_dims=(),
        collapsed_slice_dims=(1,),
        start_index_map=(1,),
        operand_batching_dims=(0,),
        start_indices_batching_dims=(0,),
    )
    return lax.gather(
        table, index[..., None], dims, slice_sizes=(1, 1), mode=lax.GatherScatterMode.PROMISE_IN_BOUNDS
    )


def sine(angle, quarter):
    n = jnp.round(angle * 0.6366197723675814)
    x = ((angle - n * 1.5703125) - n * 4.837512969970703125e-4) - n * 7.549789954891882e-8
    turn = n.astype(jnp.int32) + quarter
    y = x * x
    odd = x + x * y * (-1.6666654611e-1 + y * (8.3321608736e-3 + y * -1.9515295891e-4))
    even = 1.0 - 0.5 * y + y * y * (4.166664568298827e-2 + y * (-1.388731625493765e-3 + y * 2.443315711809948e-5))
    value = jnp.where((turn & 1) == 0, odd, even)
    return jnp.where((turn & 2) == 0, value, -value)


def bias_kernel(len_ref, box_ref, rel_ref, freq_ref, out_ref, map_ref, feat_ref, line, maps, tabs, cols, *, tile, rows):
    length = out_ref.shape[3]
    blocks = length // 128
    span = (2 * blocks - 1) * 128
    w = pl.program_id(0)
    it = pl.program_id(1)

    @pl.when((w == 0) & (it == 0))
    def _():
        cols[...] = jnp.zeros_like(cols)
        cols[0:NB, 0 : 3 * H] = rel_ref[...] * LOG2E
        t = cols[0:128, :].T
        for kind in range(3):
            for hp in range(H // 2):
                n = kind * H + 2 * hp
                first = (t[n : n + 1, :] + ROUND) - ROUND
                tabs[3 * hp + kind : 3 * hp + kind + 1, :] = first + t[n + 1 : n + 2, :] * SMALL

        mpos = lax.broadcasted_iota(jnp.int32, (8, span), 1) - (length - 128)
        ipos = lax.broadcasted_iota(jnp.int32, (8, span), 0)

        def body(g, carry):
            sl = pl.ds(pl.multiple_of(g * 8, 8), 8)
            index = bucket_of(mpos - (ipos + g * 8), 0)
            for hp in range(H // 2):
                table = jnp.broadcast_to(tabs[3 * hp : 3 * hp + 1, :], (8, 128))
                for c in range(0, span, 128):
                    a, b = unpack(look_up(table, index[:, c : c + 128]))
                    line[2 * hp, sl, c : c + 128] = a
                    line[2 * hp + 1, sl, c : c + 128] = b
            return carry

        lax.fori_loop(0, 16, body, 0)

    @pl.when(it == 0)
    def _():
        coords = jnp.concatenate([box_ref[m, pl.ds(w, 1), :] for m in range(4)] * 2, 0).astype(F32)
        by_token = coords.T
        cols[:, 0:8] = by_token
        lane = lax.broadcasted_iota(jnp.int32, (1, BOXF), 1)
        which = lane >> 5
        coord = jnp.where(
            which < 2,
            jnp.where(which == 0, by_token[:, 0:1], by_token[:, 1:2]),
            jnp.where(which == 2, by_token[:, 2:3], by_token[:, 3:4]),
        )
        feat_ref[...] = sine(coord * freq_ref[0:1, :], (lane >> 4) & 1).astype(BF)

    dead = lax.broadcasted_iota(jnp.int32, (1, length), 1) >= len_ref[w]
    first = it * tile
    line_lane = (length - 128) - (first // 128) * 128
    line_row = first % 128
    here = cols[pl.ds(pl.multiple_of(first, tile), tile), 0:8].astype(jnp.int32)
    for t in range(2):
        index = bucket_of(box_ref[t, pl.ds(w, 1), :] - here[:, t : t + 1], 2)
        map_ref[0, t] = index.astype(BF)
        maps[t] = index

    def body(g, carry):
        sl = pl.ds(pl.multiple_of(g * rows, rows), rows)
        ls = pl.ds(pl.multiple_of(line_row + g * rows, rows), rows)
        for hp in range(H // 2):
            ta = jnp.broadcast_to(tabs[3 * hp + 1 : 3 * hp + 2, :], (rows, 128))
            td = jnp.broadcast_to(tabs[3 * hp + 2 : 3 * hp + 3, :], (rows, 128))
            for c in range(0, length, 128):
                cs = slice(c, c + 128)
                lc = pl.ds(pl.multiple_of(line_lane + c, 128), 128)
                a, b = unpack(look_up(ta, maps[0, sl, cs]) + look_up(td, maps[1, sl, cs]))
                a = jnp.where(dead[:, cs], -1e9 * LOG2E, a + line[2 * hp, ls, lc])
                b = jnp.where(dead[:, cs], -1e9 * LOG2E, b + line[2 * hp + 1, ls, lc])
                out_ref[0, 2 * hp, sl, cs] = a.astype(BF)
                out_ref[0, 2 * hp + 1, sl, cs] = b.astype(BF)
        return carry

    lax.fori_loop(0, tile // rows, body, 0)


def score_bias(lengths, boxes, rel_tables):
    _, windows, length = boxes.shape
    tile, rows = 64, 32
    span = (2 * (length // 128) - 1) * 128
    freq_count = BOXF // 8
    freqs = np.float32(1000.0) ** (-np.arange(freq_count, dtype=np.float32) / np.float32(freq_count))
    freqs = jnp.asarray(np.tile(freqs.astype(np.float32), (8, 8)))
    return pl.pallas_call(
        partial(bias_kernel, tile=tile, rows=rows),
        grid=(windows, length // tile),
        in_specs=[
            pl.BlockSpec(memory_space=pltpu.SMEM),
            pl.BlockSpec((4, windows, length), lambda w, i: (0, 0, 0)),
            pl.BlockSpec((NB, 3 * H), lambda w, i: (0, 0)),
            pl.BlockSpec((8, BOXF), lambda w, i: (0, 0)),
        ],
        out_specs=[
            pl.BlockSpec((1, H, tile, length), lambda w, i: (w, 0, i, 0)),
            pl.BlockSpec((1, 2, tile, length), lambda w, i: (w, 0, i, 0)),
            pl.BlockSpec((length, BOXF), lambda w, i: (w, 0)),
        ],
        out_shape=[
            jax.ShapeDtypeStruct((windows, H, length, length), BF),
            jax.ShapeDtypeStruct((windows, 2, length, length), BF),
            jax.ShapeDtypeStruct((windows * length, BOXF), BF),
        ],
        scratch_shapes=[
            pltpu.VMEM((H, 128, span), F32),
            pltpu.VMEM((2, tile, length), jnp.int32),
            pltpu.VMEM((3 * H // 2 + 6, 128), F32),
            pltpu.VMEM((length, 128), F32),
        ],
        compiler_params=pltpu.CompilerParams(vmem_limit_bytes=VMEM),
        cost_estimate=SHORT,
        name="score_bias",
    )(lengths, boxes, rel_tables, freqs)


def attend_kernel(len_ref, q_ref, k_ref, v_ref, b_ref, o_ref, e_ref, r_ref, *, chunk):
    length = q_ref.shape[0]
    lane = lax.broadcasted_iota(jnp.int32, (length, 128), 1)
    live = lax.broadcasted_iota(jnp.int32, (length, 128), 0) < len_ref[pl.program_id(0)]
    zero, one = jnp.zeros((), BF), jnp.ones((), BF)
    q, k, v = q_ref[...], k_ref[...], v_ref[...]
    outs = []
    for h in range(2):
        mine = (lane < DH) if h == 0 else (lane >= DH)
        keys = jnp.where(mine & live, k, zero)
        values = jnp.where(mine, v, jnp.where(lane == (DH if h == 0 else 0), one, zero))
        scores = dot(q, keys, 1, 1)
        for c in range(0, length, chunk):
            t = scores[c : c + chunk] * (LOG2E * DH**-0.5) + b_ref[0, h, c : c + chunk, :].astype(F32)
            e_ref[0, h, c : c + chunk, :] = jnp.exp2(t - jnp.max(t, 1, keepdims=True)).astype(BF)
        outs.append(dot(e_ref[0, h], values))
    r = jnp.where(lane < DH, 1.0 / outs[0][:, DH : DH + 1], 1.0 / outs[1][:, 0:1])
    r_ref[...] = r
    o_ref[...] = (jnp.where(lane < DH, outs[0], outs[1]) * r).astype(BF)


def attend(lengths, qkv, bias):
    windows, _, length, _ = bias.shape
    pairs = H // 2
    col = lambda off: pl.BlockSpec((length, 128), lambda w, h: (w, off + h))
    sq = pl.BlockSpec((1, 2, length, length), lambda w, h: (w, h, 0, 0))
    width = H * DH
    return pl.pallas_call(
        partial(attend_kernel, chunk=64),
        grid=(windows, pairs),
        in_specs=[pl.BlockSpec(memory_space=pltpu.SMEM), col(0), col(pairs), col(2 * pairs), sq],
        out_specs=[col(0), sq, col(0)],
        out_shape=[
            jax.ShapeDtypeStruct((windows * length, width), BF),
            jax.ShapeDtypeStruct((windows, H, length, length), BF),
            jax.ShapeDtypeStruct((windows * length, width), F32),
        ],
        compiler_params=pltpu.CompilerParams(vmem_limit_bytes=VMEM),
        cost_estimate=SHORT,
        name="attend",
    )(lengths, qkv, qkv, qkv, bias)


def attend_back_kernel(q_ref, k_ref, v_ref, e_ref, r_ref, o_ref, do_ref, *refs, chunk):
    d_ref, ds_ref, line_ref, sum_ref = refs[-4:]
    length = q_ref.shape[0]
    blocks = length // 128
    w = pl.program_id(1)
    lane = lax.broadcasted_iota(jnp.int32, (length, 128), 1)
    zero = jnp.zeros((), BF)
    q, k, v = q_ref[...], k_ref[...], v_ref[...]
    up = do_ref[...].astype(F32) * r_ref[...]
    both = up * o_ref[...].astype(F32)
    up = up.astype(BF)
    up_t, q_t = up.T, q.T
    dq, dv_t, dk_t = None, [], []
    for h in range(2):
        mine = (lane < DH) if h == 0 else (lane >= DH)
        center = jnp.sum(jnp.where(mine, both, 0.0), 1, keepdims=True)
        dp = dot(up, jnp.where(mine, v, zero), 1, 1)
        for c in range(0, length, chunk):
            e = e_ref[0, h, c : c + chunk, :].astype(F32)
            ds_ref[0, h, c : c + chunk, :] = (e * (dp[c : c + chunk] - center[c : c + chunk])).astype(BF)
        for d in range(2 * blocks - 1):
            total = None
            for ib in range(blocks):
                jb = d - (blocks - 1) + ib
                if 0 <= jb < blocks:
                    part = ds_ref[0, h, ib * 128 : (ib + 1) * 128, jb * 128 : (jb + 1) * 128].astype(F32)
                    total = part if total is None else total + part

            @pl.when(w == 0)
            def _():
                line_ref[h, :, d * 128 : (d + 1) * 128] = total

            @pl.when(w != 0)
            def _():
                line_ref[h, :, d * 128 : (d + 1) * 128] += total

        ds = ds_ref[0, h]
        part = dot(ds, jnp.where(mine, k, zero))
        dq = part if dq is None else dq + part
        dv_t.append(dot(up_t[h * DH : (h + 1) * DH], e_ref[0, h]))
        dk_t.append(dot(q_t[h * DH : (h + 1) * DH], ds))
    parts = (dq * DH**-0.5, jnp.concatenate(dk_t, 0).T * DH**-0.5, jnp.concatenate(dv_t, 0).T)
    for n, x in enumerate(parts):
        cols = slice(n * 128, (n + 1) * 128)
        x = x.astype(BF)
        d_ref[:, cols] = x
        sums = jnp.broadcast_to(column_sums(x.astype(F32)), (8, 128))
        sum_ref[:, cols] = jnp.where(w == 0, sums, sum_ref[:, cols] + sums)


def attend_back(qkv, e, r, o, do, first, count, total, at, before=None):
    windows, _, length, _ = e.shape
    pairs = H // 2
    col = lambda off: pl.BlockSpec((length, 128), lambda h, w: (w, off + h))
    sq = pl.BlockSpec((1, 2, length, length), lambda h, w: (w, first + h, 0, 0))
    span = (2 * (length // 128) - 1) * 128
    more = [] if before is None else [before]
    return pl.pallas_call(
        partial(attend_back_kernel, chunk=64),
        grid=(count, windows),
        in_specs=[col(first), col(pairs + first), col(2 * pairs + first), sq, col(first), col(first), col(first)]
        + [pl.BlockSpec(memory_space=pl.ANY)] * len(more),
        out_specs=[
            pl.BlockSpec((length, 384), lambda h, w: (w, at + h)),
            pl.BlockSpec((1, 2, length, length), lambda h, w: (w, h, 0, 0)),
            pl.BlockSpec((2, 128, span), lambda h, w: (h, 0, 0)),
            pl.BlockSpec((8, 384), lambda h, w: (0, h)),
        ],
        out_shape=[
            jax.ShapeDtypeStruct((windows * length, total * 384), BF),
            jax.ShapeDtypeStruct((windows, 2 * count, length, length), BF),
            jax.ShapeDtypeStruct((2 * count, 128, span), F32),
            jax.ShapeDtypeStruct((8, count * 384), F32),
        ],
        input_output_aliases={7: 0} if more else {},
        compiler_params=pltpu.CompilerParams(vmem_limit_bytes=VMEM),
        cost_estimate=SHORT,
        name="attend_back",
    )(qkv, qkv, qkv, e, r, o, do, *more)


def spread(refs, rows, stride):
    h = 0
    for ref in refs:
        for n in range(ref.shape[-3]):
            x = (ref[0, n] if len(ref.shape) == 4 else ref[n]).astype(F32)
            for c in range(x.shape[1] // 128):
                rows[c, h * stride : h * stride + x.shape[0], :] = x[:, c * 128 : (c + 1) * 128]
            h += 1


def heads_of(rows, i, stride):
    return [rows[c, pl.ds(i, 16, stride=stride), :].astype(BF) for c in range(rows.shape[0])]


def one_hot(index):
    width = index.shape[1]
    ids = lax.broadcasted_iota(jnp.int32, (NB, width), 0).astype(BF)
    hit = jnp.broadcast_to(index, (NB, width)).astype(BF) == ids
    return jnp.where(hit, jnp.ones((), BF), jnp.zeros((), BF))


def table_kernel(*refs, parts, with_line):
    ds_refs, refs = refs[:parts], refs[parts:]
    line_refs, refs = refs[: parts * with_line], refs[parts * with_line :]
    map_ref, out_ref, rows, maps = refs[0], refs[1], refs[-2], refs[-1]
    tile = map_ref.shape[2]
    step = pl.program_id(0)

    @pl.when(step == 0)
    def _():
        out_ref[...] = jnp.zeros_like(out_ref)
        rows[...] = jnp.zeros_like(rows)

    if with_line:
        line_out, line_rows = refs[2], refs[3]
        share = line_refs[0].shape[1]
        span = line_refs[0].shape[2]

        @pl.when(step == 0)
        def _():
            line_out[...] = jnp.zeros_like(line_out)
            line_rows[...] = jnp.zeros_like(line_rows)

        spread(line_refs, line_rows, share + 8)
        offset = lax.broadcasted_iota(jnp.int32, (8, span), 1) - (span - 128) // 2
        down = lax.broadcasted_iota(jnp.int32, (8, span), 0) + step * share
        lhs, rhs = [], []
        for i in range(share):
            if i % 8 == 0:
                index = bucket_of(offset - (down + i), 0).astype(F32)
            lhs += heads_of(line_rows, i, share + 8)
            rhs.append(one_hot(index[i % 8 : i % 8 + 1, :]))
        line_out[...] += dot(jnp.concatenate(lhs, 1), jnp.concatenate(rhs, 1), 1, 1)

    spread(ds_refs, rows, tile + 8)
    maps[...] = map_ref[0].astype(F32)
    lhs, rhs = [], []
    for i in range(tile):
        lhs += heads_of(rows, i, tile + 8)
        rhs.append(jnp.concatenate([one_hot(maps[t, i : i + 1, :]) for t in range(2)], 0))
    out_ref[...] += dot(jnp.concatenate(lhs, 1), jnp.concatenate(rhs, 1), 1, 1)


def table_grads(ds_parts, lines, maps, w):
    _, _, length, _ = maps.shape
    tile = 64
    parts = len(ds_parts)
    steps = length // tile
    outs, out_shapes = [pl.BlockSpec((16, 2 * NB), lambda i: (0, 0))], [jax.ShapeDtypeStruct((16, 2 * NB), F32)]
    line_specs, line_rows = [], []
    if lines:
        share, span = 128 // steps, lines[0].shape[2]
        line_specs = [pl.BlockSpec((x.shape[0], share, span), lambda i: (0, i, 0)) for x in lines]
        line_rows = [pltpu.VMEM((span // 128, 16 * (share + 8), 128), F32)]
        outs.append(pl.BlockSpec((16, NB), lambda i: (0, 0)))
        out_shapes.append(jax.ShapeDtypeStruct((16, NB), F32))
    return pl.pallas_call(
        partial(table_kernel, parts=parts, with_line=bool(lines)),
        grid=(steps,),
        in_specs=[pl.BlockSpec((1, x.shape[1], tile, length), lambda i: (w, 0, i, 0)) for x in ds_parts]
        + line_specs
        + [pl.BlockSpec((1, 2, tile, length), lambda i: (w, 0, i, 0))],
        out_specs=outs,
        out_shape=out_shapes,
        scratch_shapes=line_rows
        + [pltpu.VMEM((length // 128, 16 * (tile + 8), 128), F32), pltpu.VMEM((2, tile, length), F32)],
        compiler_params=pltpu.CompilerParams(vmem_limit_bytes=VMEM),
        cost_estimate=SHORT,
        name="table_grads",
    )(*ds_parts, *lines, maps)


def gelu_both(x):
    t = 1.0 / (1.0 + (0.3275911 * 0.7071067811865476) * jnp.abs(x))
    e = jnp.exp2((-0.5 * LOG2E) * (x * x))
    poly = t * (
        0.5 * 0.254829592
        + t * (0.5 * -0.284496736 + t * (0.5 * 1.421413741 + t * (0.5 * -1.453152027 + t * (0.5 * 1.061405429))))
    )
    tail = poly * e
    cdf = jnp.where(x >= 0, 1.0 - tail, tail)
    return x * cdf, cdf + x * (e * 0.3989422804014327)


def norm_forward(summed, params):
    centered = summed - jnp.mean(summed, -1, keepdims=True)
    inverse = lax.rsqrt(jnp.mean(centered * centered, -1, keepdims=True) + EPS)
    normed = centered * inverse
    return normed * params[0:1] + params[1:2], normed, inverse


def norm_backward(upstream, normed, inverse, params):
    scaled = upstream * params[0:1]
    return inverse * (
        scaled - jnp.mean(scaled, -1, keepdims=True) - normed * jnp.mean(scaled * normed, -1, keepdims=True)
    )


def column_sums(x):
    return jnp.sum(x, 0, keepdims=True)


def front_kernel(hid_ref, f_ref, box_ref, w_ref, qv_ref, low_ref, out_ref):
    step = pl.program_id(0)
    third = pl.num_programs(0) // 3

    @pl.when(step == 0)
    def _():
        low_ref[...] = (hid_ref[...].astype(F32) + dot(f_ref[...], box_ref[...])).astype(BF)

    wide = out_ref.shape[1]
    cols = pl.ds(pl.multiple_of(lax.rem(step, third) * wide, wide), wide)
    shift = jnp.where(step < third, qv_ref[0:1, cols], jnp.where(step < 2 * third, 0.0, qv_ref[1:2, cols]))
    out_ref[...] = (dot(low_ref[...], w_ref[...]) + shift).astype(BF)


def front(hidden, features, box_weight, qkv_weight, qv_bias):
    tokens, width = hidden.shape
    cols = qkv_weight.shape[1]
    whole = lambda x: pl.BlockSpec(x.shape, lambda n: (0, 0))
    return pl.pallas_call(
        front_kernel,
        grid=(cols // width,),
        in_specs=[
            whole(hidden),
            whole(features),
            whole(box_weight),
            pl.BlockSpec((width, width), lambda n: (0, n)),
            whole(qv_bias),
        ],
        out_specs=[whole(hidden), pl.BlockSpec((tokens, width), lambda n: (0, n))],
        out_shape=[jax.ShapeDtypeStruct((tokens, width), BF), jax.ShapeDtypeStruct((tokens, cols), BF)],
        compiler_params=pltpu.CompilerParams(vmem_limit_bytes=VMEM),
        cost_estimate=SHORT,
        name="front",
    )(hidden, features, box_weight, qkv_weight, qv_bias)


def feed_kernel(hid_ref, f_ref, box_ref, att_ref, wo_ref, bo_ref, n1_ref, w1_ref, b1_ref, w2_ref, b2_ref, n2_ref, cot_ref, z_ref, low_ref, act_ref, slope_ref, out_ref, dlow_ref, sum_ref, acc, *, chunk):
    step = pl.program_id(0)
    tokens = low_ref.shape[0]

    @pl.when(step == 0)
    def _():
        for c in range(0, tokens, chunk):
            cs = slice(c, c + chunk)
            entry = hid_ref[cs, :].astype(F32) + dot(f_ref[cs, :], box_ref[...])
            z = entry + (dot(att_ref[cs, :], wo_ref[...]) + bo_ref[...])
            second = norm_forward(z, n1_ref[...])[0]
            z_ref[cs, :] = z.astype(BF)
            low_ref[cs, :] = second.astype(BF)
            acc[cs, :] = second

    for c in range(0, tokens, chunk):
        cs = slice(c, c + chunk)
        active, slope = gelu_both(dot(low_ref[cs, :], w1_ref[...]) + b1_ref[...])
        active = active.astype(BF)
        act_ref[cs, :] = active
        slope_ref[cs, :] = slope.astype(BF)
        acc[cs, :] += dot(active, w2_ref[...])

    @pl.when(step == pl.num_programs(0) - 1)
    def _():
        sums = [0.0, 0.0, 0.0]
        for c in range(0, tokens, 128):
            cs = slice(c, c + 128)
            result, normed, inverse = norm_forward(acc[cs, :] + b2_ref[...], n2_ref[...])
            out_ref[cs, :] = result.astype(BF)
            up = cot_ref[cs, :].astype(F32)
            low = norm_backward(up, normed, inverse, n2_ref[...]).astype(BF)
            dlow_ref[cs, :] = low
            sums = [sums[0] + column_sums(up * normed), sums[1] + column_sums(up), sums[2] + column_sums(low.astype(F32))]
        sum_ref[...] = jnp.concatenate(sums + [jnp.zeros((5, sums[0].shape[1]), F32)], 0)


def feed(hidden, features, box_weight, attended, out_weight, out_bias, norm_one, w1, b1, w2, b2, norm_two, cotangent):
    tokens, width = hidden.shape
    inner = w1.shape[1]
    tile = 512
    whole = lambda shape: pl.BlockSpec(shape, lambda n: (0, 0))
    full = whole((tokens, width))
    part = pl.BlockSpec((tokens, tile), lambda n: (0, n))
    return pl.pallas_call(
        partial(feed_kernel, chunk=256),
        grid=(inner // tile,),
        in_specs=[
            full,
            whole(features.shape),
            whole(box_weight.shape),
            full,
            whole(out_weight.shape),
            whole((1, width)),
            whole((2, width)),
            pl.BlockSpec((width, tile), lambda n: (0, n)),
            pl.BlockSpec((1, tile), lambda n: (0, n)),
            pl.BlockSpec((tile, width), lambda n: (n, 0)),
            whole((1, width)),
            whole((2, width)),
            full,
        ],
        out_specs=[full, full, part, part, full, full, whole((8, width))],
        out_shape=[
            jax.ShapeDtypeStruct((tokens, width), BF),
            jax.ShapeDtypeStruct((tokens, width), BF),
            jax.ShapeDtypeStruct((tokens, inner), BF),
            jax.ShapeDtypeStruct((tokens, inner), BF),
            jax.ShapeDtypeStruct((tokens, width), BF),
            jax.ShapeDtypeStruct((tokens, width), BF),
            jax.ShapeDtypeStruct((8, width), F32),
        ],
        scratch_shapes=[pltpu.VMEM((tokens, width), F32)],
        compiler_params=pltpu.CompilerParams(vmem_limit_bytes=VMEM),
        cost_estimate=SHORT,
        name="feed",
    )(
        hidden, features, box_weight, attended, out_weight, out_bias.reshape(1, -1), norm_one,
        w1, b1.reshape(1, -1), w2, b2.reshape(1, -1), norm_two, cotangent,
    )


def feed_back_kernel(dlow_ref, w1_ref, w2_ref, slope_ref, z_ref, n1_ref, wo_ref, din_ref, bias_ref, dbr_ref, datt_ref, sum_ref, acc, *, chunk):
    step = pl.program_id(0)
    tokens = dlow_ref.shape[0]

    @pl.when(step == 0)
    def _():
        acc[...] = dlow_ref[...].astype(F32)

    sums = 0.0
    for c in range(0, tokens, chunk):
        cs = slice(c, c + chunk)
        d_inner = (dot(dlow_ref[cs, :], w2_ref[...], 1, 1) * slope_ref[cs, :].astype(F32)).astype(BF)
        din_ref[cs, :] = d_inner
        sums = sums + column_sums(d_inner.astype(F32))
        acc[cs, :] += dot(d_inner, w1_ref[...], 1, 1)
    bias_ref[...] = jnp.concatenate([sums, jnp.zeros((7, sums.shape[1]), F32)], 0)

    @pl.when(step == pl.num_programs(0) - 1)
    def _():
        totals = [0.0, 0.0, 0.0]
        for c in range(0, tokens, 128):
            cs = slice(c, c + 128)
            _, normed, inverse = norm_forward(z_ref[cs, :].astype(F32), n1_ref[...])
            up = acc[cs, :]
            low = norm_backward(up, normed, inverse, n1_ref[...]).astype(BF)
            dbr_ref[cs, :] = low
            totals = [
                totals[0] + column_sums(up * normed),
                totals[1] + column_sums(up),
                totals[2] + column_sums(low.astype(F32)),
            ]
        sum_ref[...] = jnp.concatenate(totals + [jnp.zeros((5, totals[0].shape[1]), F32)], 0)
        datt_ref[...] = dot(dbr_ref[...], wo_ref[...], 1, 1).astype(BF)


def feed_back(d_outer, w1, w2, slope, z_one, norm_one, out_weight):
    tokens, width = z_one.shape
    inner = w1.shape[1]
    tile = 512
    whole = lambda shape: pl.BlockSpec(shape, lambda n: (0, 0))
    full = whole((tokens, width))
    return pl.pallas_call(
        partial(feed_back_kernel, chunk=256),
        grid=(inner // tile,),
        in_specs=[
            full,
            pl.BlockSpec((width, tile), lambda n: (0, n)),
            pl.BlockSpec((tile, width), lambda n: (n, 0)),
            pl.BlockSpec((tokens, tile), lambda n: (0, n)),
            full,
            whole((2, width)),
            whole((width, width)),
        ],
        out_specs=[
            pl.BlockSpec((tokens, tile), lambda n: (0, n)),
            pl.BlockSpec((8, tile), lambda n: (0, n)),
            full,
            full,
            whole((8, width)),
        ],
        out_shape=[
            jax.ShapeDtypeStruct((tokens, inner), BF),
            jax.ShapeDtypeStruct((8, inner), F32),
            jax.ShapeDtypeStruct((tokens, width), BF),
            jax.ShapeDtypeStruct((tokens, width), BF),
            jax.ShapeDtypeStruct((8, width), F32),
        ],
        scratch_shapes=[pltpu.VMEM((tokens, width), F32)],
        compiler_params=pltpu.CompilerParams(vmem_limit_bytes=VMEM),
        cost_estimate=SHORT,
        name="feed_back",
    )(d_outer, w1, w2, slope, z_one, norm_one, out_weight)


UNIT = 384
PIECES = 2


def halves(full, place_ref):
    rows = full.shape[0] // 2
    upper = place_ref[1] == 0
    low, high = full[:rows], full[rows:]
    return jnp.where(upper, high, low).astype(BF), jnp.where(upper, low, high).astype(BF)


def wide_grads_kernel(place_ref, *refs, counts):
    step = pl.program_id(0)
    pairs = len(counts)
    outs, turned = refs[3 * pairs : -1], refs[-1]
    at = 0
    for n, count in enumerate(counts):

        @pl.when(step == at)
        def _():
            turned[...] = refs[3 * n][...].T

        @pl.when((step >= at) & (step < at + count))
        def _():
            full = dot(turned[...], jnp.concatenate([refs[3 * n + 1][...], refs[3 * n + 2][...]], 1))
            both = halves(full, place_ref)
            for m, x in enumerate(both):
                side = x.shape[0] // 2
                for k in range(2):
                    outs[2 * m + k][...] = x[k * side : (k + 1) * side, :UNIT].reshape(outs[2 * m + k].shape)
                outs[4 + m][...] = x[:, UNIT:].reshape(outs[4 + m].shape)

        at += count


def wide_grads(place, pairs):
    tokens, rows = pairs[0][0].shape
    counts = [right.shape[1] // (2 * UNIT) for _, right in pairs]
    specs, at = [], 0
    for (left, right), count in zip(pairs, counts):

        def block(i, p, send, at=at, count=count):
            owner = 1 - p[0] if send else p[0]
            return (0, owner * count + jnp.clip(i - at, 0, count - 1))

        specs += [
            pl.BlockSpec(left.shape, lambda i, p: (0, 0)),
            pl.BlockSpec((tokens, UNIT), partial(block, send=True)),
            pl.BlockSpec((tokens, UNIT), partial(block, send=False)),
        ]
        at += count
    piece = pl.BlockSpec((1, 1, rows // 4, UNIT), lambda i, p: (0, i, 0, 0))
    out = pl.BlockSpec((2, 1, rows // 4, UNIT), lambda i, p: (0, i, 0, 0))
    outs = pl.pallas_call(
        partial(wide_grads_kernel, counts=counts),
        grid_spec=pltpu.PrefetchScalarGridSpec(
            num_scalar_prefetch=1,
            grid=(at,),
            in_specs=specs,
            out_specs=[piece] * 4 + [out] * 2,
            scratch_shapes=[pltpu.VMEM((rows, tokens), BF)],
        ),
        out_shape=[jax.ShapeDtypeStruct((n, at, rows // 4, UNIT), BF) for n in (1, 1, 1, 1, 2, 2)],
        compiler_params=pltpu.CompilerParams(vmem_limit_bytes=VMEM),
        cost_estimate=SHORT,
        name="wide_grads",
    )(place, *[x for left, right in pairs for x in (left, right, right)])
    return [x.reshape(-1, UNIT) for x in outs]


def long_grads_kernel(place_ref, left_ref, send_ref, keep_ref, *outs):
    full = dot(left_ref[...], jnp.concatenate([send_ref[...], keep_ref[...]], 1), 0, 0).astype(BF)
    for n in range(4):

        @pl.when(pl.program_id(0) == n)
        def _():
            outs[n][...] = full[:, :UNIT]
            outs[4 + n // 2][...] = full[:, UNIT:]


def long_grads(place, left, right):
    tokens, rows = left.shape
    tile = rows // 4

    def quarter(i, p):
        owner = jnp.where(i < 2, 1 - p[1], p[1])
        return (0, owner * 2 + lax.rem(i, 2))

    piece = pl.BlockSpec((tile, UNIT), lambda i, p: (0, 0))
    other = pl.BlockSpec((tile, UNIT), lambda i, p: (jnp.minimum(i, 1), 0))
    own = pl.BlockSpec((tile, UNIT), lambda i, p: (jnp.maximum(i - 2, 0), 0))
    return pl.pallas_call(
        long_grads_kernel,
        grid_spec=pltpu.PrefetchScalarGridSpec(
            num_scalar_prefetch=1,
            grid=(4,),
            in_specs=[
                pl.BlockSpec((tokens, tile), quarter),
                pl.BlockSpec((tokens, UNIT), lambda i, p: (0, 1 - p[0])),
                pl.BlockSpec((tokens, UNIT), lambda i, p: (0, p[0])),
            ],
            out_specs=[piece] * 4 + [other, own],
        ),
        out_shape=[jax.ShapeDtypeStruct((n * tile, UNIT), BF) for n in (1, 1, 1, 1, 2, 2)],
        compiler_params=pltpu.CompilerParams(vmem_limit_bytes=VMEM),
        cost_estimate=SHORT,
        name="long_grads",
    )(place, left, right, right)


E_ROWS = 16


def last_kernel(place_ref, x_ref, dx_ref, f_ref, df_ref, two_ref, one_ref, in_ref, *refs):
    qv_refs, (line_ref, small0_ref, small1_ref), outs = refs[:3], refs[3:6], refs[6:]
    mine = place_ref[0] == 0
    upper = place_ref[1] == 0
    width = x_ref.shape[1]
    middle = width // 2
    x = dot(x_ref[...], dx_ref[...], 0, 0).astype(BF)
    box = dot(f_ref[...], df_ref[...], 0, 0).astype(BF)
    tables = jnp.concatenate([line_ref[...], small0_ref[...] + small1_ref[...], jnp.zeros((16, NB), F32)], 1).T
    blocks = [ref[0:1, p : p + UNIT] for ref in qv_refs for p in range(0, ref.shape[1], UNIT)]
    qv = [jnp.concatenate([y[:, at : at + 128] for y in blocks], 1) for at in (0, 256)]
    halves_of = []
    for n in range(2):
        cols = slice(n * middle, (n + 1) * middle)
        inner = in_ref[0:1, n * 2 * width : (n + 1) * 2 * width]
        sums = [
            two_ref[n : n + 1, :],
            one_ref[n : n + 1, :],
            qv[n],
            jnp.concatenate([one_ref[2:3, cols], two_ref[2:3, cols]], 1),
            inner[:, :width],
            inner[:, width:],
            jnp.zeros((E_ROWS - 6, width), F32),
        ]
        share = [tables[m * NB + n * NB // 2 : m * NB + (n + 1) * NB // 2, :] for m in range(3)]
        share = [jnp.pad(t, ((0, 0), (0, 128 - t.shape[1]))) for t in share]
        sides = [jnp.concatenate(sums, 0), jnp.concatenate(share + [jnp.zeros((E_ROWS, width - 3 * 128), F32)], 1)]
        q, h = x.shape[0] // 4, box.shape[0] // 4
        halves_of.append(
            jnp.concatenate(
                [
                    y
                    for m in range(2)
                    for y in (
                        x[(2 * n + m) * q : (2 * n + m + 1) * q],
                        box[(2 * n + m) * h : (2 * n + m + 1) * h],
                        sides[m].astype(BF),
                    )
                ],
                0,
            )
        )
    for m in range(2):
        rows = jnp.where(upper, halves_of[1 - m], halves_of[m])
        outs[m][...] = jnp.where(mine, rows[:, middle:], rows[:, :middle])
        outs[2 + m][...] = jnp.where(mine, rows[:, :middle], rows[:, middle:])


def last_grads(place, x, dx, f, df, *sums):
    rows = (x.shape[1] + f.shape[1]) // 4 + E_ROWS
    vmem = pl.BlockSpec(memory_space=pltpu.VMEM)
    return pl.pallas_call(
        last_kernel,
        in_specs=[pl.BlockSpec(memory_space=pltpu.SMEM)] + [vmem] * (4 + len(sums)),
        out_specs=[vmem] * 4,
        out_shape=[jax.ShapeDtypeStruct((2 * rows, UNIT), BF)] * 4,
        compiler_params=pltpu.CompilerParams(vmem_limit_bytes=VMEM),
        cost_estimate=SHORT,
        name="last_grads",
    )(place, x, dx, f, df, *sums)


def lay_kernel(place_ref, *refs, kind, rows):
    last = refs[4:8] if kind == "heads" else refs[:4]
    pieces, outs = refs[:4], refs[8 if kind == "heads" else 4 :]
    core, step = place_ref[0], pl.program_id(0)

    def lay_piece(ref, owner):
        blocks = ref.shape[0] // rows
        for n in range(blocks):
            x = ref[n * rows : (n + 1) * rows, :].astype(F32)
            if kind == "long":
                outs[0][n * rows : (n + 1) * rows, owner * UNIT : (owner + 1) * UNIT] = x
            elif kind == "wide":
                at = (owner * blocks + n) * UNIT
                outs[0][:, at : at + UNIT] = x
            elif n == 0:
                outs[0][:, owner * UNIT : (owner + 1) * UNIT] = x
            else:
                lay_pair(x, owner * 2 + n - 1)

    def lay_last(ref, owner):
        lay_pair(ref[:rows, :].astype(F32), 4 + owner)
        box = BOXF // 4
        cols = slice(owner * UNIT, (owner + 1) * UNIT)
        outs[2][:, cols] = ref[rows : rows + box, :].astype(F32)
        small = ref[rows + box : rows + box + E_ROWS, :].astype(F32)

        @pl.when(step == 0)
        def _():
            for n in range(3):
                outs[3 + n][:, cols] = small[n : n + 1]
            outs[6 + owner][...] = small[3]
            for n in range(2):
                at = n * 2 * UNIT + owner * UNIT
                outs[8][at : at + UNIT] = small[4 + n]

        if owner == 0:

            @pl.when(step == 1)
            def _():
                outs[9][...] = jnp.concatenate([small[:, n * 128 : n * 128 + H] for n in range(3)], 1)

    def lay_pair(x, pair):
        for m in range(3):
            at = (m * (H // 2) + pair) * 128
            outs[1][:, at : at + 128] = x[:, m * 128 : (m + 1) * 128]

    def choose(refs, side, lay_one):
        for other_side in range(2):
            for owner in range(2):
                for other_core in range(2):

                    @pl.when(((step == side) == (other_side == 0)) & (core == (owner ^ other_core)))
                    def _():
                        lay_one(refs[2 * other_side + other_core], owner)

    choose(pieces, place_ref[2], lay_piece)
    if kind == "heads":
        choose(last, place_ref[3], lay_last)


def lay(place, pieces, kind, rows):
    blocks = pieces[0].shape[0] // rows
    whole = None
    if kind == "long":
        shapes = [(2 * blocks * rows, 2 * UNIT)]
    elif kind == "wide":
        shapes = [(2 * rows, 2 * blocks * UNIT)]
    else:
        width = 2 * UNIT
        shapes = [(2 * rows, width), (2 * rows, 3 * width), (BOXF // 2, width)]
        whole = [(1, width)] * 3 + [(UNIT,)] * 2 + [(2 * width,), (NB // 2, 3 * H)]
    return pl.pallas_call(
        partial(lay_kernel, kind=kind, rows=rows),
        grid=(2,),
        in_specs=[pl.BlockSpec(memory_space=pltpu.SMEM)] + [pl.BlockSpec(x.shape, lambda i: (0, 0)) for x in pieces],
        out_specs=[pl.BlockSpec((m // 2, n), lambda i: (i, 0)) for m, n in shapes]
        + [pl.BlockSpec(shape, lambda i, n=len(shape): (0,) * n) for shape in whole or []],
        out_shape=[jax.ShapeDtypeStruct(shape, F32) for shape in shapes + (whole or [])],
        compiler_params=pltpu.CompilerParams(vmem_limit_bytes=VMEM),
        cost_estimate=SHORT,
        name="lay",
    )(place, *pieces)


def entry_kernel(a_ref, b_ref, w_ref, sum_ref, out_ref):
    pairs = H // 2
    weight = jnp.concatenate([w_ref[:, (m * pairs + n) * 128 : (m * pairs + n + 1) * 128] for n in range(pairs) for m in range(3)], 1)
    both = jnp.concatenate([a_ref[...], b_ref[...]], 1)
    out_ref[...] = (sum_ref[...].astype(F32) + dot(both, weight, 1, 1)).astype(BF)


def entry_grad(first, last, weight, base):
    tokens, width = base.shape
    tile = tokens // 2
    row = lambda x: pl.BlockSpec((tile, x.shape[1]), lambda i: (i, 0))
    return pl.pallas_call(
        entry_kernel,
        grid=(tokens // tile,),
        in_specs=[row(first), row(last), pl.BlockSpec(weight.shape, lambda i: (0, 0)), row(base)],
        out_specs=row(base),
        out_shape=jax.ShapeDtypeStruct((tokens, width), BF),
        compiler_params=pltpu.CompilerParams(vmem_limit_bytes=VMEM),
        cost_estimate=SHORT,
        name="entry_grad",
    )(first, last, weight, base)


def shards(
    docs,
    hidden_in,
    boxes,
    lengths,
    box_weight,
    qkv_weight,
    qv_bias,
    out_weight,
    out_bias,
    rel_tables,
    norm_one,
    ffn_in_weight,
    ffn_in_bias,
    ffn_out_weight,
    ffn_out_bias,
    norm_two,
    cotangent,
):
    half = lax.axis_index("half")
    doc = lax.axis_index("doc")
    core, side = doc & 1, (doc >> 1) & 1
    own, local_len, width = hidden_in.shape
    windows = own // 2
    length = 2 * local_len
    tokens = windows * length

    def swap_half(x):
        return lax.ppermute(x, "half", [(0, 1), (1, 0)])

    def swap_doc(x, bit):
        return lax.ppermute(x, "doc", [(i, i ^ (1 << bit)) for i in range(docs)])

    def part(x, index, axis):
        size = x.shape[axis] // 2
        return lax.dynamic_slice_in_dim(x, index * size, size, axis)

    def ordered(index, mine, other, axis):
        return jnp.where(index == 0, jnp.concatenate([mine, other], axis), jnp.concatenate([other, mine], axis))

    def whole_windows(x, axis):
        return ordered(half, part(x, half, axis), swap_half(part(x, 1 - half, axis)), axis + 1)

    def half_positions(x):
        return ordered(half, part(x, half, 1), swap_half(part(x, 1 - half, 1)), 0)

    def add(x, y):
        return (x.astype(F32) + y.astype(F32)).astype(BF)

    def tie(x, *others):
        return lax.optimization_barrier((x,) + others)[0]

    box_part = swap_half(part(boxes, 1 - half, 1))
    my_boxes = ordered(half, part(boxes, half, 1), box_part, 2)
    my_lengths = part(lengths, half, 0)
    hidden_send = part(tie(hidden_in, box_part), 1 - half, 0)
    hidden = ordered(half, part(hidden_in, half, 0), swap_half(hidden_send), 1).reshape(tokens, width)

    bias, maps, features = score_bias(my_lengths, my_boxes, rel_tables)
    upstream = whole_windows(tie(cotangent, maps), 0).reshape(tokens, width)
    entry_low, qkv = front(hidden, features, box_weight, qkv_weight, qv_bias)
    attended, e, r = attend(my_lengths, qkv, bias)
    z_one, second_low, active, slope, result, d_outer, sums_two = feed(
        hidden,
        features,
        box_weight,
        attended,
        out_weight,
        out_bias,
        norm_one,
        ffn_in_weight,
        ffn_in_bias,
        ffn_out_weight,
        ffn_out_bias,
        norm_two,
        upstream,
    )

    pairs, early = H // 2, H // 3
    late_pairs = pairs - early
    step = early // 2
    more = list(range(2, docs.bit_length() - 1))
    place = jnp.stack([core, half, side, (doc >> 2) & 1]).astype(jnp.int32)
    last = [None]

    def now(x):
        return x if last[0] is None else tie(x, *last[0])

    def then(x, *more):
        last[0] = (x,) + more
        return x

    def joined(pieces):
        return jnp.concatenate(pieces, 0) if len(pieces) > 1 else pieces[0]

    def total(*xs):
        out = xs[0].astype(F32)
        for x in xs[1:]:
            out = out + x.astype(F32)
        return out.astype(BF)

    class Chain:
        def core(self, *parts):
            pieces, keep, keep_own = parts[:-2], parts[-2], parts[-1]
            count = len(pieces) // 2
            then(keep_own)
            pieces = [swap_doc(x, 0) for x in pieces]
            self.own = [keep, pieces[:count], keep_own, pieces[count:]]

        def half(self):
            keep, come, keep_own, come_own = self.own
            keep, keep_own = lax.optimization_barrier((keep, keep_own) + last[0])[:2]
            send, own = total(keep, joined(come)), total(keep_own, joined(come_own))
            then(send, own)
            self.own = [own, swap_half(send)]

        def split(self, bit):
            b = (doc >> bit) & 1
            own = [now(self.own[0])] + self.own[1:]
            send = then(total(*[part(x, 1 - b, 0) for x in own]))
            keep = total(*[part(x, b, 0) for x in own])
            self.own = [keep, swap_doc(send, bit)]

        def double(self, bits):
            x = then(total(now(self.own[0]), *self.own[1:]))
            for bit in bits[:-1]:
                x = total(x, swap_doc(x, bit))
            self.own = [x, swap_doc(x, bits[-1])]

        def back(self, bit):
            x = then(total(now(self.own[0]), *self.own[1:]))
            self.parted, self.own = bit, [x, swap_doc(x, bit)]

        def gather(self, bit=1):
            if hasattr(self, "parted"):
                x = then(ordered((doc >> self.parted) & 1, now(self.own[0]), self.own[1], 0))
            else:
                x = then(total(now(self.own[0]), *self.own[1:]))
            self.mine, self.across = x, swap_doc(x, bit)
            self.beside = swap_doc(x, 0)

        def settle(self, *others):
            then(*last[0], self.beside, *others)

        def pieces(self):
            return [now(self.mine), self.beside, self.across, swap_doc(now(self.across), 0)]

    def back(first, count, total_pairs, at, before):
        out = attend_back(qkv, e, r, attended, now(d_attended), first, count, total_pairs, at, before)
        then(out[0])
        return out

    a, b, c, d = Chain(), Chain(), Chain(), Chain()
    block_rows = width // 4
    then(d_outer)
    a.core(*long_grads(place, active, now(d_outer)))
    a.half()
    d_inner, sums_in, d_branch, d_attended, sums_one = feed_back(
        now(d_outer), ffn_in_weight, ffn_out_weight, slope, z_one, norm_one, out_weight
    )
    then(d_branch)
    a.split(1)
    b.core(*wide_grads(place, [(second_low, now(d_inner))]))
    a.split(more[0])
    b.half()
    first_right, ds_0, line_0, qv_0 = back(0, step, early, 0, None)
    a.double(more[1:])
    first_right, ds_1, line_1, qv_1 = back(step, early - step, early, step, first_right)
    a.back(more[0])
    b.split(1)
    c.core(*wide_grads(place, [(attended, d_branch), (entry_low, now(first_right))]))
    c.half()
    last_right, ds_2, line_2, qv_2 = back(early, late_pairs, late_pairs, 0, None)
    a.gather()
    b.split(more[0])
    small_0, line_grad = table_grads([ds_0, ds_1, now(ds_2)], [line_0, line_1, line_2], maps, 0)
    then(small_0)
    a.settle(a.across)
    b.double(more[1:])
    c.split(1)
    d_entry_low = then(entry_grad(first_right, now(last_right), qkv_weight, d_branch))
    c.split(more[0])
    b.back(more[0])
    d_entry = d_entry_low.reshape(windows, length, width)
    grad_send = then(part(now(d_entry), 1 - half, 1))
    grad_mine, grad_other = part(d_entry, half, 1), swap_half(grad_send)
    small_1 = table_grads([ds_0, ds_1, now(ds_2)], [], maps, 1)[0]
    for w in range(2, windows):
        small_1 = small_1 + table_grads([ds_0, ds_1, ds_2], [], maps, w)[0]
    then(small_1)
    c.double(more[1:])
    b.gather()
    then(*last[0], grad_other)
    d.core(
        *last_grads(
            place, entry_low, last_right, features, now(d_entry_low), sums_two, sums_one, sums_in, qv_0, qv_1, qv_2, line_grad, small_0, small_1
        )
    )
    c.back(more[0])
    d.half()
    (ffn_out_grad,) = lay(place, a.pieces(), "long", block_rows)
    then(ffn_out_grad)
    d.split(more[0])
    result = result.reshape(windows, length, width)
    out_send = then(part(now(result), 1 - half, 1))
    out_mine, out_other = part(result, half, 1), swap_half(out_send)
    c.gather()
    b.settle()
    d.double(more[1:])
    (ffn_in_grad,) = lay(place, b.pieces(), "wide", block_rows)
    then(ffn_in_grad)
    d.double([1])
    hidden_grad = then(ordered(half, now(grad_mine), grad_other, 0))
    c.settle()
    c_pieces = c.pieces()
    d.gather(more[0])
    out_grad, qkv_grad, box, two, one, qv, out_sum, ffn_out_sum, ffn_in_sum, table = lay(
        place, c_pieces + d.pieces(), "heads", block_rows
    )
    layer_out = ordered(half, now(out_mine), out_other, 0)
    return (
        layer_out,
        hidden_grad,
        box,
        qkv_grad,
        qv,
        out_grad,
        out_sum,
        table,
        one,
        ffn_in_grad,
        ffn_in_sum,
        ffn_out_grad,
        ffn_out_sum,
        two,
    )


def solution(mesh):
    rep = P()
    rows = P("half", None)
    return jax.shard_map(
        partial(shards, mesh.shape["doc"]),
        mesh=mesh,
        in_specs=(P("doc", "half", None), P(None, "doc", "half"), P("doc")) + (rep,) * 12 + (P("doc", "half", None),),
        out_specs=(
            P("doc", "half", None),
            P("doc", "half", None),
            rows,
            rows,
            rows,
            rows,
            P("half"),
            rows,
            rows,
            rows,
            P("half"),
            rows,
            P("half"),
            rows,
        ),
        check_vma=False,
    )
```

```python
from functools import partial

import jax
import jax.numpy as jnp
import numpy as np
from jax import lax
from jax.experimental import pallas as pl
from jax.experimental.pallas import tpu as pltpu
from jax.sharding import PartitionSpec as P

H = 12
DH = 64
BOXF = 128
NB = 32
EPS = 1e-05
LOG2E = 1.4426950408889634
BF = jnp.bfloat16
F32 = jnp.float32
VMEM = 56 << 20
SHORT = pl.CostEstimate(flops=1, bytes_accessed=1, transcendentals=0)


def dot(a, b, ca=1, cb=0):
    return lax.dot_general(a, b, (((ca,), (cb,)), ((), ())), preferred_element_type=F32)


ROUND = 1.5 * 2.0**23 * 2.0**-8
SMALL = 1.6e-4


def unpack(both):
    first = (both + ROUND) - ROUND
    return first, (both - first) * (1.0 / SMALL)


def bucket_of(offset, shift):
    magnitude = jnp.abs(offset)
    if shift:
        magnitude = magnitude >> shift
    count = jnp.minimum(magnitude, 8)
    for n, bound in enumerate((12, 16, 24, 32, 48, 64, 96)):
        count = jnp.where(magnitude >= bound, 9 + n, count)
    return jnp.where(offset > 0, count + 16, count)


def look_up(table, index):
    dims = lax.GatherDimensionNumbers(
        offset_dims=(),
        collapsed_slice_dims=(1,),
        start_index_map=(1,),
        operand_batching_dims=(0,),
        start_indices_batching_dims=(0,),
    )
    return lax.gather(
        table, index[..., None], dims, slice_sizes=(1, 1), mode=lax.GatherScatterMode.PROMISE_IN_BOUNDS
    )


def sine(angle, quarter):
    n = jnp.round(angle * 0.6366197723675814)
    x = ((angle - n * 1.5703125) - n * 4.837512969970703125e-4) - n * 7.549789954891882e-8
    turn = n.astype(jnp.int32) + quarter
    y = x * x
    odd = x + x * y * (-1.6666654611e-1 + y * (8.3321608736e-3 + y * -1.9515295891e-4))
    even = 1.0 - 0.5 * y + y * y * (4.166664568298827e-2 + y * (-1.388731625493765e-3 + y * 2.443315711809948e-5))
    value = jnp.where((turn & 1) == 0, odd, even)
    return jnp.where((turn & 2) == 0, value, -value)


def window_length(meta_ref, w, windows):
    return meta_ref[4 + meta_ref[1] * windows + w]


def position(index, half, length):
    shifted = index + half * (length // 2)
    return jnp.where(shifted >= length, shifted - length, shifted)


def bias_kernel(meta_ref, own_ref, other_ref, rel_ref, freq_ref, out_ref, map_ref, feat_ref, line, maps, tabs, cols, *, rows):
    length = out_ref.shape[3]
    windows = other_ref.shape[1]
    blocks = length // 128
    span = (2 * blocks - 1) * 128
    w = pl.program_id(0)
    it = pl.program_id(1)
    half = meta_ref[1]

    def box_row(m):
        return jnp.concatenate([own_ref[m, pl.ds(half * windows + w, 1), :], other_ref[m, pl.ds(w, 1), :]], 1)

    @pl.when((w == 0) & (it == 0))
    def _():
        cols[...] = jnp.zeros_like(cols)
        cols[0:NB, 0 : 3 * H] = rel_ref[...] * LOG2E
        t = cols[0:128, :].T
        for kind in range(3):
            for hp in range(H // 2):
                n = kind * H + 2 * hp
                first = (t[n : n + 1, :] + ROUND) - ROUND
                tabs[3 * hp + kind : 3 * hp + kind + 1, :] = first + t[n + 1 : n + 2, :] * SMALL

        mpos = lax.broadcasted_iota(jnp.int32, (32, span), 1) - (length - 128)
        ipos = lax.broadcasted_iota(jnp.int32, (32, span), 0)

        def body(g, carry):
            sl = pl.ds(pl.multiple_of(g * 32, 32), 32)
            index = bucket_of(mpos - (ipos + g * 32), 0)
            for c in range(0, span, 128):
                for hp in range(H // 2):
                    table = jnp.broadcast_to(tabs[3 * hp : 3 * hp + 1, :], (32, 128))
                    a, b = unpack(look_up(table, index[:, c : c + 128]))
                    line[2 * hp, sl, c : c + 128] = a
                    line[2 * hp + 1, sl, c : c + 128] = b
            return carry

        lax.fori_loop(0, 4, body, 0)

    @pl.when(it == 0)
    def _():
        coords = jnp.concatenate([box_row(m) for m in range(4)] * 2, 0).astype(F32)
        by_token = coords.T
        cols[:, 0:8] = by_token
        lane = lax.broadcasted_iota(jnp.int32, (1, BOXF), 1)
        which = lane >> 5
        coord = jnp.where(
            which < 2,
            jnp.where(which == 0, by_token[:, 0:1], by_token[:, 1:2]),
            jnp.where(which == 2, by_token[:, 2:3], by_token[:, 3:4]),
        )
        feat_ref[...] = sine(coord * freq_ref[0:1, :], (lane >> 4) & 1).astype(BF)

    place = position(lax.broadcasted_iota(jnp.int32, (1, length), 1), half, length)
    dead = place >= window_length(meta_ref, w, windows)
    first = it * 128
    here = cols[pl.ds(pl.multiple_of(first, 128), 128), 0:8].astype(jnp.int32)
    for t in range(2):
        index = bucket_of(box_row(t) - here[:, t : t + 1], 2)
        map_ref[0, t] = index.astype(BF)
        maps[t] = index

    def block_of(n):
        return lax.rem(n + half * (blocks // 2), blocks)

    for r in range(0, 128, rows):
        rs = slice(r, r + rows)
        for n in range(blocks):
            cs = slice(n * 128, (n + 1) * 128)
            lc = pl.ds(pl.multiple_of((blocks - 1 + block_of(n) - block_of(it)) * 128, 128), 128)
            ia, idown = maps[0, rs, cs], maps[1, rs, cs]
            for hp in range(H // 2):
                ta = jnp.broadcast_to(tabs[3 * hp + 1 : 3 * hp + 2, :], (rows, 128))
                td = jnp.broadcast_to(tabs[3 * hp + 2 : 3 * hp + 3, :], (rows, 128))
                a, b = unpack(look_up(ta, ia) + look_up(td, idown))
                a = jnp.where(dead[:, cs], -1e9 * LOG2E, a + line[2 * hp, rs, lc])
                b = jnp.where(dead[:, cs], -1e9 * LOG2E, b + line[2 * hp + 1, rs, lc])
                out_ref[0, 2 * hp, rs, cs] = a.astype(BF)
                out_ref[0, 2 * hp + 1, rs, cs] = b.astype(BF)


def score_bias(meta, own, other, rel_tables):
    windows, length = other.shape[1], 2 * other.shape[2]
    span = (2 * (length // 128) - 1) * 128
    freq_count = BOXF // 8
    freqs = np.float32(1000.0) ** (-np.arange(freq_count, dtype=np.float32) / np.float32(freq_count))
    freqs = jnp.asarray(np.tile(freqs.astype(np.float32), (8, 8)))
    return pl.pallas_call(
        partial(bias_kernel, rows=128),
        grid=(windows, length // 128),
        in_specs=[
            pl.BlockSpec(memory_space=pltpu.SMEM),
            pl.BlockSpec(own.shape, lambda w, i: (0, 0, 0)),
            pl.BlockSpec(other.shape, lambda w, i: (0, 0, 0)),
            pl.BlockSpec((NB, 3 * H), lambda w, i: (0, 0)),
            pl.BlockSpec((8, BOXF), lambda w, i: (0, 0)),
        ],
        out_specs=[
            pl.BlockSpec((1, H, 128, length), lambda w, i: (w, 0, i, 0)),
            pl.BlockSpec((1, 2, 128, length), lambda w, i: (w, 0, i, 0)),
            pl.BlockSpec((length, BOXF), lambda w, i: (w, 0)),
        ],
        out_shape=[
            jax.ShapeDtypeStruct((windows, H, length, length), BF),
            jax.ShapeDtypeStruct((windows, 2, length, length), BF),
            jax.ShapeDtypeStruct((windows * length, BOXF), BF),
        ],
        scratch_shapes=[
            pltpu.VMEM((H, 128, span), F32),
            pltpu.VMEM((2, 128, length), jnp.int32),
            pltpu.VMEM((3 * H // 2 + 6, 128), F32),
            pltpu.VMEM((length, 128), F32),
        ],
        compiler_params=pltpu.CompilerParams(vmem_limit_bytes=VMEM),
        cost_estimate=SHORT,
        name="score_bias",
    )(meta, own, other, rel_tables, freqs)


def attend_kernel(meta_ref, q_ref, k_ref, v_ref, b_ref, o_ref, e_ref, r_ref, *, chunk):
    length = q_ref.shape[0]
    lane = lax.broadcasted_iota(jnp.int32, (length, 128), 1)
    place = position(lax.broadcasted_iota(jnp.int32, (length, 128), 0), meta_ref[1], length)
    live = place < window_length(meta_ref, pl.program_id(0), pl.num_programs(0))
    zero, one = jnp.zeros((), BF), jnp.ones((), BF)
    q, k, v = q_ref[...], k_ref[...], v_ref[...]
    outs = []
    for h in range(2):
        mine = (lane < DH) if h == 0 else (lane >= DH)
        keys = jnp.where(mine & live, k, zero)
        values = jnp.where(mine, v, jnp.where(lane == (DH if h == 0 else 0), one, zero))
        scores = dot(q, keys, 1, 1)
        for c in range(0, length, chunk):
            t = scores[c : c + chunk] * (LOG2E * DH**-0.5) + b_ref[0, h, c : c + chunk, :].astype(F32)
            e_ref[0, h, c : c + chunk, :] = jnp.exp2(t - jnp.max(t, 1, keepdims=True)).astype(BF)
        outs.append(dot(e_ref[0, h], values))
    r = jnp.where(lane < DH, 1.0 / outs[0][:, DH : DH + 1], 1.0 / outs[1][:, 0:1])
    r_ref[...] = r
    o_ref[...] = (jnp.where(lane < DH, outs[0], outs[1]) * r).astype(BF)


def attend(meta, qkv, bias):
    windows, _, length, _ = bias.shape
    pairs = H // 2
    col = lambda off: pl.BlockSpec((length, 128), lambda w, h: (w, off + h))
    sq = pl.BlockSpec((1, 2, length, length), lambda w, h: (w, h, 0, 0))
    width = H * DH
    return pl.pallas_call(
        partial(attend_kernel, chunk=64),
        grid=(windows, pairs),
        in_specs=[pl.BlockSpec(memory_space=pltpu.SMEM), col(0), col(pairs), col(2 * pairs), sq],
        out_specs=[col(0), sq, col(0)],
        out_shape=[
            jax.ShapeDtypeStruct((windows * length, width), BF),
            jax.ShapeDtypeStruct((windows, H, length, length), BF),
            jax.ShapeDtypeStruct((windows * length, width), F32),
        ],
        compiler_params=pltpu.CompilerParams(vmem_limit_bytes=VMEM),
        cost_estimate=SHORT,
        name="attend",
    )(meta, qkv, qkv, qkv, bias)


def attend_back_kernel(meta_ref, q_ref, k_ref, v_ref, e_ref, r_ref, o_ref, do_ref, *refs, chunk):
    d_ref, ds_ref, line_ref, sum_ref = refs[-4:]
    length = q_ref.shape[0]
    blocks = length // 128
    w = pl.program_id(1)
    lane = lax.broadcasted_iota(jnp.int32, (length, 128), 1)
    zero = jnp.zeros((), BF)
    q, k, v = q_ref[...], k_ref[...], v_ref[...]
    up = do_ref[...].astype(F32) * r_ref[...]
    both = up * o_ref[...].astype(F32)
    up = up.astype(BF)
    up_t, q_t = up.T, q.T
    dq, dv_t, dk_t = None, [], []
    for h in range(2):
        mine = (lane < DH) if h == 0 else (lane >= DH)
        center = jnp.sum(jnp.where(mine, both, 0.0), 1, keepdims=True)
        dp = dot(up, jnp.where(mine, v, zero), 1, 1)
        for c in range(0, length, chunk):
            e = e_ref[0, h, c : c + chunk, :].astype(F32)
            ds_ref[0, h, c : c + chunk, :] = (e * (dp[c : c + chunk] - center[c : c + chunk])).astype(BF)
        for half in range(2):
            at = lambda n: (n + half * blocks // 2) % blocks

            @pl.when(meta_ref[1] == half)
            def _():
                for d in range(2 * blocks - 1):
                    cols = slice(d * 128, (d + 1) * 128)
                    total = jnp.where(w == 0, 0.0, line_ref[h, :, cols])
                    for ib in range(blocks):
                        for jb in range(blocks):
                            if at(jb) - at(ib) + blocks - 1 == d:
                                rows = slice(ib * 128, (ib + 1) * 128)
                                total = total + ds_ref[0, h, rows, jb * 128 : (jb + 1) * 128].astype(F32)
                    line_ref[h, :, cols] = total

        ds = ds_ref[0, h]
        part = dot(ds, jnp.where(mine, k, zero))
        dq = part if dq is None else dq + part
        dv_t.append(dot(up_t[h * DH : (h + 1) * DH], e_ref[0, h]))
        dk_t.append(dot(q_t[h * DH : (h + 1) * DH], ds))
    parts = (dq * DH**-0.5, jnp.concatenate(dk_t, 0).T * DH**-0.5, jnp.concatenate(dv_t, 0).T)
    for n, x in enumerate(parts):
        cols = slice(n * 128, (n + 1) * 128)
        x = x.astype(BF)
        d_ref[:, cols] = x
        sums = jnp.broadcast_to(column_sums(x.astype(F32)), (8, 128))
        sum_ref[:, cols] = jnp.where(w == 0, sums, sum_ref[:, cols] + sums)


def attend_back(meta, qkv, e, r, o, do, first, count, total, at, before=None):
    windows, _, length, _ = e.shape
    pairs = H // 2
    col = lambda off: pl.BlockSpec((length, 128), lambda h, w: (w, off + h))
    sq = pl.BlockSpec((1, 2, length, length), lambda h, w: (w, first + h, 0, 0))
    span = (2 * (length // 128) - 1) * 128
    more = [] if before is None else [before]
    return pl.pallas_call(
        partial(attend_back_kernel, chunk=64),
        grid=(count, windows),
        in_specs=[pl.BlockSpec(memory_space=pltpu.SMEM)]
        + [col(first), col(pairs + first), col(2 * pairs + first), sq, col(first), col(first), col(first)]
        + [pl.BlockSpec(memory_space=pl.ANY)] * len(more),
        out_specs=[
            pl.BlockSpec((length, 384), lambda h, w: (w, at + h)),
            pl.BlockSpec((1, 2, length, length), lambda h, w: (w, h, 0, 0)),
            pl.BlockSpec((2, 128, span), lambda h, w: (h, 0, 0)),
            pl.BlockSpec((8, 384), lambda h, w: (0, h)),
        ],
        out_shape=[
            jax.ShapeDtypeStruct((windows * length, total * 384), BF),
            jax.ShapeDtypeStruct((windows, 2 * count, length, length), BF),
            jax.ShapeDtypeStruct((2 * count, 128, span), F32),
            jax.ShapeDtypeStruct((8, count * 384), F32),
        ],
        input_output_aliases={8: 0} if more else {},
        compiler_params=pltpu.CompilerParams(vmem_limit_bytes=VMEM),
        cost_estimate=SHORT,
        name="attend_back",
    )(meta, qkv, qkv, qkv, e, r, o, do, *more)


def spread(refs, rows, stride):
    h = 0
    for ref in refs:
        for n in range(ref.shape[-3]):
            x = (ref[0, n] if len(ref.shape) == 4 else ref[n]).astype(F32)
            for c in range(x.shape[1] // 128):
                rows[c, h * stride : h * stride + x.shape[0], :] = x[:, c * 128 : (c + 1) * 128]
            h += 1


def heads_of(rows, i, stride):
    return [rows[c, pl.ds(i, 16, stride=stride), :].astype(BF) for c in range(rows.shape[0])]


def one_hot(index):
    width = index.shape[1]
    ids = lax.broadcasted_iota(jnp.int32, (NB, width), 0).astype(BF)
    hit = jnp.broadcast_to(index, (NB, width)).astype(BF) == ids
    return jnp.where(hit, jnp.ones((), BF), jnp.zeros((), BF))


def table_kernel(*refs, parts, with_line):
    ds_refs, refs = refs[:parts], refs[parts:]
    line_refs, refs = refs[: parts * with_line], refs[parts * with_line :]
    map_ref, out_ref, rows, maps = refs[0], refs[1], refs[-2], refs[-1]
    tile = map_ref.shape[2]
    step = pl.program_id(0)

    @pl.when(step == 0)
    def _():
        out_ref[...] = jnp.zeros_like(out_ref)
        rows[...] = jnp.zeros_like(rows)

    if with_line:
        line_out, line_rows = refs[2], refs[3]
        share = line_refs[0].shape[1]
        span = line_refs[0].shape[2]

        @pl.when(step == 0)
        def _():
            line_out[...] = jnp.zeros_like(line_out)
            line_rows[...] = jnp.zeros_like(line_rows)

        spread(line_refs, line_rows, share + 8)
        offset = lax.broadcasted_iota(jnp.int32, (8, span), 1) - (span - 128) // 2
        down = lax.broadcasted_iota(jnp.int32, (8, span), 0) + step * share
        lhs, rhs = [], []
        for i in range(share):
            if i % 8 == 0:
                index = bucket_of(offset - (down + i), 0).astype(F32)
            lhs += heads_of(line_rows, i, share + 8)
            rhs.append(one_hot(index[i % 8 : i % 8 + 1, :]))
        line_out[...] += dot(jnp.concatenate(lhs, 1), jnp.concatenate(rhs, 1), 1, 1)

    spread(ds_refs, rows, tile + 8)
    maps[...] = map_ref[0].astype(F32)
    lhs, rhs = [], []
    for i in range(tile):
        lhs += heads_of(rows, i, tile + 8)
        rhs.append(jnp.concatenate([one_hot(maps[t, i : i + 1, :]) for t in range(2)], 0))
    out_ref[...] += dot(jnp.concatenate(lhs, 1), jnp.concatenate(rhs, 1), 1, 1)


def table_grads(ds_parts, lines, maps, w):
    _, _, length, _ = maps.shape
    tile = 64
    parts = len(ds_parts)
    steps = length // tile
    outs, out_shapes = [pl.BlockSpec((16, 2 * NB), lambda i: (0, 0))], [jax.ShapeDtypeStruct((16, 2 * NB), F32)]
    line_specs, line_rows = [], []
    if lines:
        share, span = 128 // steps, lines[0].shape[2]
        line_specs = [pl.BlockSpec((x.shape[0], share, span), lambda i: (0, i, 0)) for x in lines]
        line_rows = [pltpu.VMEM((span // 128, 16 * (share + 8), 128), F32)]
        outs.append(pl.BlockSpec((16, NB), lambda i: (0, 0)))
        out_shapes.append(jax.ShapeDtypeStruct((16, NB), F32))
    return pl.pallas_call(
        partial(table_kernel, parts=parts, with_line=bool(lines)),
        grid=(steps,),
        in_specs=[pl.BlockSpec((1, x.shape[1], tile, length), lambda i: (w, 0, i, 0)) for x in ds_parts]
        + line_specs
        + [pl.BlockSpec((1, 2, tile, length), lambda i: (w, 0, i, 0))],
        out_specs=outs,
        out_shape=out_shapes,
        scratch_shapes=line_rows
        + [pltpu.VMEM((length // 128, 16 * (tile + 8), 128), F32), pltpu.VMEM((2, tile, length), F32)],
        compiler_params=pltpu.CompilerParams(vmem_limit_bytes=VMEM),
        cost_estimate=SHORT,
        name="table_grads",
    )(*ds_parts, *lines, maps)


def gelu_both(x):
    t = 1.0 / (1.0 + (0.3275911 * 0.7071067811865476) * jnp.abs(x))
    e = jnp.exp2((-0.5 * LOG2E) * (x * x))
    poly = t * (
        0.5 * 0.254829592
        + t * (0.5 * -0.284496736 + t * (0.5 * 1.421413741 + t * (0.5 * -1.453152027 + t * (0.5 * 1.061405429))))
    )
    tail = poly * e
    cdf = jnp.where(x >= 0, 1.0 - tail, tail)
    return x * cdf, cdf + x * (e * 0.3989422804014327)


def norm_forward(summed, params):
    centered = summed - jnp.mean(summed, -1, keepdims=True)
    inverse = lax.rsqrt(jnp.mean(centered * centered, -1, keepdims=True) + EPS)
    normed = centered * inverse
    return normed * params[0:1] + params[1:2], normed, inverse


def norm_backward(upstream, normed, inverse, params):
    scaled = upstream * params[0:1]
    return inverse * (
        scaled - jnp.mean(scaled, -1, keepdims=True) - normed * jnp.mean(scaled * normed, -1, keepdims=True)
    )


def column_sums(x):
    return jnp.sum(x, 0, keepdims=True)


def tokens_of(own_ref, other_ref, chunk):
    windows, local, _ = other_ref.shape
    step = min(chunk, local)
    for w in range(windows):
        for n, ref in enumerate((own_ref, other_ref)):
            for c in range(0, local, step):
                yield slice((2 * w + n) * local + c, (2 * w + n) * local + c + step), ref[w, c : c + step, :]


def front_kernel(meta_ref, own_ref, other_ref, f_ref, box_ref, w_ref, qv_ref, low_ref, out_ref):
    step = pl.program_id(0)
    third = pl.num_programs(0) // 3

    @pl.when(step == 0)
    def _():
        for cs, x in tokens_of(own_ref, other_ref, 256):
            low_ref[cs, :] = (x.astype(F32) + dot(f_ref[cs, :], box_ref[...])).astype(BF)

    wide = out_ref.shape[1]
    cols = pl.ds(pl.multiple_of(lax.rem(step, third) * wide, wide), wide)
    shift = jnp.where(step < third, qv_ref[0:1, cols], jnp.where(step < 2 * third, 0.0, qv_ref[1:2, cols]))
    out_ref[...] = (dot(low_ref[...], w_ref[...]) + shift).astype(BF)


def front(meta, own, other, features, box_weight, qkv_weight, qv_bias):
    windows, local, width = other.shape
    tokens = 2 * windows * local
    cols = qkv_weight.shape[1]
    whole = lambda x: pl.BlockSpec(x.shape, lambda n, p: (0,) * len(x.shape))
    return pl.pallas_call(
        front_kernel,
        grid_spec=pltpu.PrefetchScalarGridSpec(
            num_scalar_prefetch=1,
            grid=(cols // width,),
            in_specs=[
                pl.BlockSpec(other.shape, lambda n, p: (p[1], 0, 0)),
                whole(other),
                whole(features),
                whole(box_weight),
                pl.BlockSpec((width, width), lambda n, p: (0, n)),
                whole(qv_bias),
            ],
            out_specs=[
                pl.BlockSpec((tokens, width), lambda n, p: (0, 0)),
                pl.BlockSpec((tokens, width), lambda n, p: (0, n)),
            ],
        ),
        out_shape=[jax.ShapeDtypeStruct((tokens, width), BF), jax.ShapeDtypeStruct((tokens, cols), BF)],
        compiler_params=pltpu.CompilerParams(vmem_limit_bytes=VMEM),
        cost_estimate=SHORT,
        name="front",
    )(meta, own, other, features, box_weight, qkv_weight, qv_bias)


def feed_kernel(meta_ref, own_ref, other_ref, f_ref, box_ref, att_ref, wo_ref, bo_ref, n1_ref, w1_ref, b1_ref, w2_ref, b2_ref, n2_ref, cot_own_ref, cot_other_ref, z_ref, low_ref, act_ref, slope_ref, out_own_ref, out_other_ref, dlow_ref, sum_ref, acc, *, chunk):
    step = pl.program_id(0)
    tokens = low_ref.shape[0]

    @pl.when(step == 0)
    def _():
        for cs, x in tokens_of(own_ref, other_ref, chunk):
            entry = x.astype(F32) + dot(f_ref[cs, :], box_ref[...])
            z = entry + (dot(att_ref[cs, :], wo_ref[...]) + bo_ref[...])
            second = norm_forward(z, n1_ref[...])[0]
            z_ref[cs, :] = z.astype(BF)
            low_ref[cs, :] = second.astype(BF)
            acc[cs, :] = second

    for c in range(0, tokens, chunk):
        cs = slice(c, c + chunk)
        active, slope = gelu_both(dot(low_ref[cs, :], w1_ref[...]) + b1_ref[...])
        active = active.astype(BF)
        act_ref[cs, :] = active
        slope_ref[cs, :] = slope.astype(BF)
        acc[cs, :] += dot(active, w2_ref[...])

    @pl.when(step == pl.num_programs(0) - 1)
    def _():
        sums = [0.0, 0.0, 0.0]
        local = cot_other_ref.shape[1]
        for cs, x in tokens_of(cot_own_ref, cot_other_ref, 128):
            result, normed, inverse = norm_forward(acc[cs, :] + b2_ref[...], n2_ref[...])
            place = cs.start % local
            out = (out_own_ref, out_other_ref)[cs.start // local % 2]
            out[cs.start // local // 2, place : place + 128, :] = result.astype(BF)
            up = x.astype(F32)
            low = norm_backward(up, normed, inverse, n2_ref[...]).astype(BF)
            dlow_ref[cs, :] = low
            sums = [sums[0] + column_sums(up * normed), sums[1] + column_sums(up), sums[2] + column_sums(low.astype(F32))]
        sum_ref[...] = jnp.concatenate(sums + [jnp.zeros((5, sums[0].shape[1]), F32)], 0)


def feed(meta, own, other, features, box_weight, attended, out_weight, out_bias, norm_one, w1, b1, w2, b2, norm_two, cot_own, cot_other):
    tokens, width = attended.shape
    inner = w1.shape[1]
    tile = 512
    whole = lambda shape: pl.BlockSpec(shape, lambda n, p: (0,) * len(shape))
    mine = pl.BlockSpec(other.shape, lambda n, p: (p[1], 0, 0))
    full = whole((tokens, width))
    part = pl.BlockSpec((tokens, tile), lambda n, p: (0, n))
    return pl.pallas_call(
        partial(feed_kernel, chunk=256),
        grid_spec=pltpu.PrefetchScalarGridSpec(
            num_scalar_prefetch=1,
            grid=(inner // tile,),
            in_specs=[
                mine,
                whole(other.shape),
                whole(features.shape),
                whole(box_weight.shape),
                full,
                whole(out_weight.shape),
                whole((1, width)),
                whole((2, width)),
                pl.BlockSpec((width, tile), lambda n, p: (0, n)),
                pl.BlockSpec((1, tile), lambda n, p: (0, n)),
                pl.BlockSpec((tile, width), lambda n, p: (n, 0)),
                whole((1, width)),
                whole((2, width)),
                mine,
                whole(other.shape),
            ],
            out_specs=[full, full, part, part, whole(other.shape), whole(other.shape), full, whole((8, width))],
            scratch_shapes=[pltpu.VMEM((tokens, width), F32)],
        ),
        out_shape=[
            jax.ShapeDtypeStruct((tokens, width), BF),
            jax.ShapeDtypeStruct((tokens, width), BF),
            jax.ShapeDtypeStruct((tokens, inner), BF),
            jax.ShapeDtypeStruct((tokens, inner), BF),
            jax.ShapeDtypeStruct(other.shape, BF),
            jax.ShapeDtypeStruct(other.shape, BF),
            jax.ShapeDtypeStruct((tokens, width), BF),
            jax.ShapeDtypeStruct((8, width), F32),
        ],
        compiler_params=pltpu.CompilerParams(vmem_limit_bytes=VMEM),
        cost_estimate=SHORT,
        name="feed",
    )(
        meta, own, other, features, box_weight, attended, out_weight, out_bias.reshape(1, -1), norm_one,
        w1, b1.reshape(1, -1), w2, b2.reshape(1, -1), norm_two, cot_own, cot_other,
    )


def feed_back_kernel(dlow_ref, w1_ref, w2_ref, slope_ref, z_ref, n1_ref, wo_ref, din_ref, bias_ref, dbr_ref, datt_ref, sum_ref, acc, *, chunk):
    step = pl.program_id(0)
    tokens = dlow_ref.shape[0]

    @pl.when(step == 0)
    def _():
        acc[...] = dlow_ref[...].astype(F32)

    sums = 0.0
    for c in range(0, tokens, chunk):
        cs = slice(c, c + chunk)
        d_inner = (dot(dlow_ref[cs, :], w2_ref[...], 1, 1) * slope_ref[cs, :].astype(F32)).astype(BF)
        din_ref[cs, :] = d_inner
        sums = sums + column_sums(d_inner.astype(F32))
        acc[cs, :] += dot(d_inner, w1_ref[...], 1, 1)
    bias_ref[...] = jnp.concatenate([sums, jnp.zeros((7, sums.shape[1]), F32)], 0)

    @pl.when(step == pl.num_programs(0) - 1)
    def _():
        totals = [0.0, 0.0, 0.0]
        for c in range(0, tokens, 128):
            cs = slice(c, c + 128)
            _, normed, inverse = norm_forward(z_ref[cs, :].astype(F32), n1_ref[...])
            up = acc[cs, :]
            low = norm_backward(up, normed, inverse, n1_ref[...]).astype(BF)
            dbr_ref[cs, :] = low
            totals = [
                totals[0] + column_sums(up * normed),
                totals[1] + column_sums(up),
                totals[2] + column_sums(low.astype(F32)),
            ]
        sum_ref[...] = jnp.concatenate(totals + [jnp.zeros((5, totals[0].shape[1]), F32)], 0)
        datt_ref[...] = dot(dbr_ref[...], wo_ref[...], 1, 1).astype(BF)


def feed_back(d_outer, w1, w2, slope, z_one, norm_one, out_weight):
    tokens, width = z_one.shape
    inner = w1.shape[1]
    tile = 512
    whole = lambda shape: pl.BlockSpec(shape, lambda n: (0, 0))
    full = whole((tokens, width))
    return pl.pallas_call(
        partial(feed_back_kernel, chunk=256),
        grid=(inner // tile,),
        in_specs=[
            full,
            pl.BlockSpec((width, tile), lambda n: (0, n)),
            pl.BlockSpec((tile, width), lambda n: (n, 0)),
            pl.BlockSpec((tokens, tile), lambda n: (0, n)),
            full,
            whole((2, width)),
            whole((width, width)),
        ],
        out_specs=[
            pl.BlockSpec((tokens, tile), lambda n: (0, n)),
            pl.BlockSpec((8, tile), lambda n: (0, n)),
            full,
            full,
            whole((8, width)),
        ],
        out_shape=[
            jax.ShapeDtypeStruct((tokens, inner), BF),
            jax.ShapeDtypeStruct((8, inner), F32),
            jax.ShapeDtypeStruct((tokens, width), BF),
            jax.ShapeDtypeStruct((tokens, width), BF),
            jax.ShapeDtypeStruct((8, width), F32),
        ],
        scratch_shapes=[pltpu.VMEM((tokens, width), F32)],
        compiler_params=pltpu.CompilerParams(vmem_limit_bytes=VMEM),
        cost_estimate=SHORT,
        name="feed_back",
    )(d_outer, w1, w2, slope, z_one, norm_one, out_weight)


UNIT = 384
PIECES = 2


def halves(full, place_ref):
    rows = full.shape[0] // 2
    upper = place_ref[1] == 0
    low, high = full[:rows], full[rows:]
    return jnp.where(upper, high, low).astype(BF), jnp.where(upper, low, high).astype(BF)


def wide_grads_kernel(place_ref, *refs, counts):
    step = pl.program_id(0)
    pairs = len(counts)
    outs, turned = refs[3 * pairs : -1], refs[-1]
    at = 0
    for n, count in enumerate(counts):

        @pl.when(step == at)
        def _():
            turned[...] = refs[3 * n][...].T

        @pl.when((step >= at) & (step < at + count))
        def _():
            full = dot(turned[...], jnp.concatenate([refs[3 * n + 1][...], refs[3 * n + 2][...]], 1))
            both = halves(full, place_ref)
            for m, x in enumerate(both):
                side = x.shape[0] // 2
                for k in range(2):
                    outs[2 * m + k][...] = x[k * side : (k + 1) * side, :UNIT].reshape(outs[2 * m + k].shape)
                outs[4 + m][...] = x[:, UNIT:].reshape(outs[4 + m].shape)

        at += count


def wide_grads(place, pairs):
    tokens, rows = pairs[0][0].shape
    counts = [right.shape[1] // (2 * UNIT) for _, right in pairs]
    specs, at = [], 0
    for (left, right), count in zip(pairs, counts):

        def block(i, p, send, at=at, count=count):
            owner = 1 - p[0] if send else p[0]
            return (0, owner * count + jnp.clip(i - at, 0, count - 1))

        specs += [
            pl.BlockSpec(left.shape, lambda i, p: (0, 0)),
            pl.BlockSpec((tokens, UNIT), partial(block, send=True)),
            pl.BlockSpec((tokens, UNIT), partial(block, send=False)),
        ]
        at += count
    piece = pl.BlockSpec((1, 1, rows // 4, UNIT), lambda i, p: (0, i, 0, 0))
    out = pl.BlockSpec((2, 1, rows // 4, UNIT), lambda i, p: (0, i, 0, 0))
    outs = pl.pallas_call(
        partial(wide_grads_kernel, counts=counts),
        grid_spec=pltpu.PrefetchScalarGridSpec(
            num_scalar_prefetch=1,
            grid=(at,),
            in_specs=specs,
            out_specs=[piece] * 4 + [out] * 2,
            scratch_shapes=[pltpu.VMEM((rows, tokens), BF)],
        ),
        out_shape=[jax.ShapeDtypeStruct((n, at, rows // 4, UNIT), BF) for n in (1, 1, 1, 1, 2, 2)],
        compiler_params=pltpu.CompilerParams(vmem_limit_bytes=VMEM),
        cost_estimate=SHORT,
        name="wide_grads",
    )(place, *[x for left, right in pairs for x in (left, right, right)])
    return [x.reshape(-1, UNIT) for x in outs]


def long_grads_kernel(place_ref, left_ref, send_ref, keep_ref, *outs):
    full = dot(left_ref[...], jnp.concatenate([send_ref[...], keep_ref[...]], 1), 0, 0).astype(BF)
    for n in range(4):

        @pl.when(pl.program_id(0) == n)
        def _():
            outs[n][...] = full[:, :UNIT]
            outs[4 + n // 2][...] = full[:, UNIT:]


def long_grads(place, left, right):
    tokens, rows = left.shape
    tile = rows // 4

    def quarter(i, p):
        owner = jnp.where(i < 2, 1 - p[1], p[1])
        return (0, owner * 2 + lax.rem(i, 2))

    piece = pl.BlockSpec((tile, UNIT), lambda i, p: (0, 0))
    other = pl.BlockSpec((tile, UNIT), lambda i, p: (jnp.minimum(i, 1), 0))
    own = pl.BlockSpec((tile, UNIT), lambda i, p: (jnp.maximum(i - 2, 0), 0))
    return pl.pallas_call(
        long_grads_kernel,
        grid_spec=pltpu.PrefetchScalarGridSpec(
            num_scalar_prefetch=1,
            grid=(4,),
            in_specs=[
                pl.BlockSpec((tokens, tile), quarter),
                pl.BlockSpec((tokens, UNIT), lambda i, p: (0, 1 - p[0])),
                pl.BlockSpec((tokens, UNIT), lambda i, p: (0, p[0])),
            ],
            out_specs=[piece] * 4 + [other, own],
        ),
        out_shape=[jax.ShapeDtypeStruct((n * tile, UNIT), BF) for n in (1, 1, 1, 1, 2, 2)],
        compiler_params=pltpu.CompilerParams(vmem_limit_bytes=VMEM),
        cost_estimate=SHORT,
        name="long_grads",
    )(place, left, right, right)


E_ROWS = 16


def last_kernel(place_ref, x_ref, dx_ref, f_ref, own_ref, other_ref, two_ref, one_ref, in_ref, *refs):
    qv_refs, (line_ref, small0_ref, small1_ref), outs = refs[:3], refs[3:6], refs[6:]
    mine = place_ref[0] == 0
    upper = place_ref[1] == 0
    width = x_ref.shape[1]
    middle = width // 2
    x = dot(x_ref[...], dx_ref[...], 0, 0).astype(BF)
    entry = jnp.concatenate([ref[w] for w in range(own_ref.shape[0]) for ref in (own_ref, other_ref)], 0)
    box = dot(f_ref[...], entry, 0, 0).astype(BF)
    tables = jnp.concatenate([line_ref[...], small0_ref[...] + small1_ref[...], jnp.zeros((16, NB), F32)], 1).T
    blocks = [ref[0:1, p : p + UNIT] for ref in qv_refs for p in range(0, ref.shape[1], UNIT)]
    qv = [jnp.concatenate([y[:, at : at + 128] for y in blocks], 1) for at in (0, 256)]
    halves_of = []
    for n in range(2):
        cols = slice(n * middle, (n + 1) * middle)
        inner = in_ref[0:1, n * 2 * width : (n + 1) * 2 * width]
        sums = [
            two_ref[n : n + 1, :],
            one_ref[n : n + 1, :],
            qv[n],
            jnp.concatenate([one_ref[2:3, cols], two_ref[2:3, cols]], 1),
            inner[:, :width],
            inner[:, width:],
            jnp.zeros((E_ROWS - 6, width), F32),
        ]
        share = [tables[m * NB + n * NB // 2 : m * NB + (n + 1) * NB // 2, :] for m in range(3)]
        share = [jnp.pad(t, ((0, 0), (0, 128 - t.shape[1]))) for t in share]
        sides = [jnp.concatenate(sums, 0), jnp.concatenate(share + [jnp.zeros((E_ROWS, width - 3 * 128), F32)], 1)]
        q, h = x.shape[0] // 4, box.shape[0] // 4
        halves_of.append(
            jnp.concatenate(
                [
                    y
                    for m in range(2)
                    for y in (
                        x[(2 * n + m) * q : (2 * n + m + 1) * q],
                        box[(2 * n + m) * h : (2 * n + m + 1) * h],
                        sides[m].astype(BF),
                    )
                ],
                0,
            )
        )
    for m in range(2):
        rows = jnp.where(upper, halves_of[1 - m], halves_of[m])
        outs[m][...] = jnp.where(mine, rows[:, middle:], rows[:, :middle])
        outs[2 + m][...] = jnp.where(mine, rows[:, :middle], rows[:, middle:])


def last_grads(place, x, dx, f, own, other, *sums):
    rows = (x.shape[1] + f.shape[1]) // 4 + E_ROWS
    vmem = pl.BlockSpec(memory_space=pltpu.VMEM)
    return pl.pallas_call(
        last_kernel,
        in_specs=[pl.BlockSpec(memory_space=pltpu.SMEM)] + [vmem] * (5 + len(sums)),
        out_specs=[vmem] * 4,
        out_shape=[jax.ShapeDtypeStruct((2 * rows, UNIT), BF)] * 4,
        compiler_params=pltpu.CompilerParams(vmem_limit_bytes=VMEM),
        cost_estimate=SHORT,
        name="last_grads",
    )(place, x, dx, f, own, other, *sums)


def lay_kernel(place_ref, *refs, kind, rows):
    last = refs[4:8] if kind == "heads" else refs[:4]
    pieces, outs = refs[:4], refs[8 if kind == "heads" else 4 :]
    core, step = place_ref[0], pl.program_id(0)

    def lay_piece(ref, owner):
        blocks = ref.shape[0] // rows
        for n in range(blocks):
            x = ref[n * rows : (n + 1) * rows, :].astype(F32)
            if kind == "long":
                outs[0][n * rows : (n + 1) * rows, owner * UNIT : (owner + 1) * UNIT] = x
            elif kind == "wide":
                at = (owner * blocks + n) * UNIT
                outs[0][:, at : at + UNIT] = x
            elif n == 0:
                outs[0][:, owner * UNIT : (owner + 1) * UNIT] = x
            else:
                lay_pair(x, owner * 2 + n - 1)

    def lay_last(ref, owner):
        lay_pair(ref[:rows, :].astype(F32), 4 + owner)
        box = BOXF // 4
        cols = slice(owner * UNIT, (owner + 1) * UNIT)
        outs[2][:, cols] = ref[rows : rows + box, :].astype(F32)
        small = ref[rows + box : rows + box + E_ROWS, :].astype(F32)

        @pl.when(step == 0)
        def _():
            for n in range(3):
                outs[3 + n][:, cols] = small[n : n + 1]
            outs[6 + owner][...] = small[3]
            for n in range(2):
                at = n * 2 * UNIT + owner * UNIT
                outs[8][at : at + UNIT] = small[4 + n]

        if owner == 0:

            @pl.when(step == 1)
            def _():
                outs[9][...] = jnp.concatenate([small[:, n * 128 : n * 128 + H] for n in range(3)], 1)

    def lay_pair(x, pair):
        for m in range(3):
            at = (m * (H // 2) + pair) * 128
            outs[1][:, at : at + 128] = x[:, m * 128 : (m + 1) * 128]

    def choose(refs, side, lay_one):
        for other_side in range(2):
            for owner in range(2):
                for other_core in range(2):

                    @pl.when(((step == side) == (other_side == 0)) & (core == (owner ^ other_core)))
                    def _():
                        lay_one(refs[2 * other_side + other_core], owner)

    choose(pieces, place_ref[2], lay_piece)
    if kind == "heads":
        choose(last, place_ref[3], lay_last)


def lay(place, pieces, kind, rows):
    blocks = pieces[0].shape[0] // rows
    whole = None
    if kind == "long":
        shapes = [(2 * blocks * rows, 2 * UNIT)]
    elif kind == "wide":
        shapes = [(2 * rows, 2 * blocks * UNIT)]
    else:
        width = 2 * UNIT
        shapes = [(2 * rows, width), (2 * rows, 3 * width), (BOXF // 2, width)]
        whole = [(1, width)] * 3 + [(UNIT,)] * 2 + [(2 * width,), (NB // 2, 3 * H)]
    return pl.pallas_call(
        partial(lay_kernel, kind=kind, rows=rows),
        grid=(2,),
        in_specs=[pl.BlockSpec(memory_space=pltpu.SMEM)] + [pl.BlockSpec(x.shape, lambda i: (0, 0)) for x in pieces],
        out_specs=[pl.BlockSpec((m // 2, n), lambda i: (i, 0)) for m, n in shapes]
        + [pl.BlockSpec(shape, lambda i, n=len(shape): (0,) * n) for shape in whole or []],
        out_shape=[jax.ShapeDtypeStruct(shape, F32) for shape in shapes + (whole or [])],
        compiler_params=pltpu.CompilerParams(vmem_limit_bytes=VMEM),
        cost_estimate=SHORT,
        name="lay",
    )(place, *pieces)


def entry_kernel(a_ref, b_ref, w_ref, sum_ref, own_ref, other_ref):
    pairs = H // 2
    weight = jnp.concatenate([w_ref[:, (m * pairs + n) * 128 : (m * pairs + n + 1) * 128] for n in range(pairs) for m in range(3)], 1)
    both = jnp.concatenate([a_ref[...], b_ref[...]], 1)
    out = (sum_ref[...].astype(F32) + dot(both, weight, 1, 1)).astype(BF)
    local = own_ref.shape[1]
    own_ref[0] = out[:local]
    other_ref[0] = out[local:]


def entry_grad(first, last, weight, base, windows):
    tokens, width = base.shape
    tile = tokens // windows
    row = lambda x: pl.BlockSpec((tile, x.shape[1]), lambda i: (i, 0))
    out = pl.BlockSpec((1, tile // 2, width), lambda i: (i, 0, 0))
    return pl.pallas_call(
        entry_kernel,
        grid=(windows,),
        in_specs=[row(first), row(last), pl.BlockSpec(weight.shape, lambda i: (0, 0)), row(base)],
        out_specs=[out, out],
        out_shape=[jax.ShapeDtypeStruct((windows, tile // 2, width), BF)] * 2,
        compiler_params=pltpu.CompilerParams(vmem_limit_bytes=VMEM),
        cost_estimate=SHORT,
        name="entry_grad",
    )(first, last, weight, base)


def shards(
    docs,
    hidden_in,
    boxes,
    lengths,
    box_weight,
    qkv_weight,
    qv_bias,
    out_weight,
    out_bias,
    rel_tables,
    norm_one,
    ffn_in_weight,
    ffn_in_bias,
    ffn_out_weight,
    ffn_out_bias,
    norm_two,
    cotangent,
):
    half = lax.axis_index("half")
    doc = lax.axis_index("doc")
    core, side = doc & 1, (doc >> 1) & 1
    own, local_len, width = hidden_in.shape
    windows = own // 2
    length = 2 * local_len
    tokens = windows * length

    def swap_half(x):
        return lax.ppermute(x, "half", [(0, 1), (1, 0)])

    def swap_doc(x, bit):
        return lax.ppermute(x, "doc", [(i, i ^ (1 << bit)) for i in range(docs)])

    def part(x, index, axis):
        if isinstance(x, list):
            return jnp.where(index == 0, *x)
        size = x.shape[axis] // 2
        return lax.dynamic_slice_in_dim(x, index * size, size, axis)

    def ordered(index, mine, other, axis):
        return jnp.where(index == 0, jnp.concatenate([mine, other], axis), jnp.concatenate([other, mine], axis))

    def tie(x, *others):
        return lax.optimization_barrier((x,) + others)[0]

    meta = jnp.concatenate([jnp.stack([core, half, side, (doc >> 2) & 1]).astype(jnp.int32), lengths])
    box_other = swap_half(part(boxes, 1 - half, 1))
    hidden_other = swap_half(part(tie(hidden_in, box_other), 1 - half, 0))
    bias, maps, features = score_bias(meta, boxes, box_other, rel_tables)
    cot_other = swap_half(part(tie(cotangent, maps), 1 - half, 0))
    entry_low, qkv = front(meta, hidden_in, hidden_other, features, box_weight, qkv_weight, qv_bias)
    attended, e, r = attend(meta, qkv, bias)
    z_one, second_low, active, slope, out_mine, out_send, d_outer, sums_two = feed(
        meta,
        hidden_in,
        hidden_other,
        features,
        box_weight,
        attended,
        out_weight,
        out_bias,
        norm_one,
        ffn_in_weight,
        ffn_in_bias,
        ffn_out_weight,
        ffn_out_bias,
        norm_two,
        cotangent,
        cot_other,
    )

    pairs, early = H // 2, H // 3
    late_pairs = pairs - early
    step = early // 2
    more = list(range(2, docs.bit_length() - 1))
    place = meta
    last = [None]

    def now(x):
        return x if last[0] is None else tie(x, *last[0])

    def then(x, *more):
        last[0] = (x,) + more
        return x

    def joined(pieces):
        return jnp.concatenate(pieces, 0) if len(pieces) > 1 else pieces[0]

    def total(*xs):
        out = xs[0].astype(F32)
        for x in xs[1:]:
            out = out + x.astype(F32)
        return out.astype(BF)

    class Chain:
        def core(self, *parts):
            pieces, keep, keep_own = parts[:-2], parts[-2], parts[-1]
            count = len(pieces) // 2
            then(keep_own)
            pieces = [swap_doc(x, 0) for x in pieces]
            self.own = [keep, pieces[:count], keep_own, pieces[count:]]

        def half_later(self):
            keep, come, keep_own, come_own = self.own
            send = then(total(now(keep), joined(come)))
            self.own = [keep_own, come_own, swap_half(send)]

        def half(self):
            keep, come, keep_own, come_own = self.own
            keep, keep_own = lax.optimization_barrier((keep, keep_own) + last[0])[:2]
            send, own = total(keep, joined(come)), total(keep_own, joined(come_own))
            then(send, own)
            self.own = [own, swap_half(send)]

        def split(self, bit):
            b = (doc >> bit) & 1
            own = [now(self.own[0])] + self.own[1:]
            send = then(total(*[part(x, 1 - b, 0) for x in own]))
            keep = total(*[part(x, b, 0) for x in own])
            self.own = [keep, swap_doc(send, bit)]

        def double(self, bits):
            x = then(total(now(self.own[0]), *self.own[1:]))
            for bit in bits[:-1]:
                x = total(x, swap_doc(x, bit))
            self.own = [x, swap_doc(x, bits[-1])]

        def back(self, bit):
            x = then(total(now(self.own[0]), *self.own[1:]))
            self.parted, self.own = bit, [x, swap_doc(x, bit)]

        def gather(self, bit=1):
            if hasattr(self, "parted"):
                x = then(ordered((doc >> self.parted) & 1, now(self.own[0]), self.own[1], 0))
            else:
                x = then(total(now(self.own[0]), *self.own[1:]))
            self.mine, self.across = x, swap_doc(x, bit)
            self.beside = swap_doc(x, 0)

        def settle(self, *others):
            then(*last[0], self.beside, *others)

        def pieces(self):
            return [now(self.mine), self.beside, self.across, swap_doc(now(self.across), 0)]

    def back(first, count, total_pairs, at, before):
        out = attend_back(meta, qkv, e, r, attended, now(d_attended), first, count, total_pairs, at, before)
        then(out[0])
        return out

    a, b, c, d = Chain(), Chain(), Chain(), Chain()
    block_rows = width // 4
    then(d_outer)
    a.core(*long_grads(place, active, now(d_outer)))
    a.half_later()
    d_inner, sums_in, d_branch, d_attended, sums_one = feed_back(
        now(d_outer), ffn_in_weight, ffn_out_weight, slope, z_one, norm_one, out_weight
    )
    then(d_branch)
    a.split(1)
    b.core(*wide_grads(place, [(second_low, now(d_inner))]))
    a.split(more[0])
    b.half()
    first_right, ds_0, line_0, qv_0 = back(0, step, early, 0, None)
    a.double(more[1:])
    first_right, ds_1, line_1, qv_1 = back(step, early - step, early, step, first_right)
    a.back(more[0])
    b.split(1)
    c.core(*wide_grads(place, [(attended, d_branch), (entry_low, now(first_right))]))
    c.half()
    last_right, ds_2, line_2, qv_2 = back(early, late_pairs, late_pairs, 0, None)
    a.gather()
    b.split(more[0])
    small_0, line_grad = table_grads([ds_0, ds_1, now(ds_2)], [line_0, line_1, line_2], maps, 0)
    then(small_0)
    a.settle(a.across)
    b.double(more[1:])
    c.split(1)
    grad_mine, grad_send = entry_grad(first_right, now(last_right), qkv_weight, d_branch, windows)
    then(grad_send)
    c.split(more[0])
    b.back(more[0])
    grad_other = swap_half(grad_send)
    small_1 = table_grads([ds_0, ds_1, now(ds_2)], [], maps, 1)[0]
    for w in range(2, windows):
        small_1 = small_1 + table_grads([ds_0, ds_1, ds_2], [], maps, w)[0]
    then(small_1)
    c.double(more[1:])
    b.gather()
    then(*last[0], grad_other)
    d.core(
        *last_grads(
            place, entry_low, last_right, features, now(grad_mine), grad_send, sums_two, sums_one, sums_in, qv_0, qv_1, qv_2, line_grad, small_0, small_1
        )
    )
    c.back(more[0])
    d.half()
    (ffn_out_grad,) = lay(place, a.pieces(), "long", block_rows)
    then(ffn_out_grad)
    d.split(more[0])
    out_other = swap_half(now(out_send))
    c.gather()
    b.settle()
    d.double(more[1:])
    (ffn_in_grad,) = lay(place, b.pieces(), "wide", block_rows)
    then(ffn_in_grad)
    d.double([1])
    hidden_grad = then(ordered(half, now(grad_mine), grad_other, 0))
    c.settle()
    c_pieces = c.pieces()
    d.gather(more[0])
    out_grad, qkv_grad, box, two, one, qv, out_sum, ffn_out_sum, ffn_in_sum, table = lay(
        place, c_pieces + d.pieces(), "heads", block_rows
    )
    layer_out = ordered(half, now(out_mine), out_other, 0)
    return (
        layer_out,
        hidden_grad,
        box,
        qkv_grad,
        qv,
        out_grad,
        out_sum,
        table,
        one,
        ffn_in_grad,
        ffn_in_sum,
        ffn_out_grad,
        ffn_out_sum,
        two,
    )


def solution(mesh):
    rep = P()
    rows = P("half", None)
    return jax.shard_map(
        partial(shards, mesh.shape["doc"]),
        mesh=mesh,
        in_specs=(P("doc", "half", None), P(None, "doc", "half"), P("doc")) + (rep,) * 12 + (P("doc", "half", None),),
        out_specs=(
            P("doc", "half", None),
            P("doc", "half", None),
            rows,
            rows,
            rows,
            rows,
            P("half"),
            rows,
            rows,
            rows,
            P("half"),
            rows,
            P("half"),
            rows,
        ),
        check_vma=False,
    )
```

```python
from functools import partial

import jax
import jax.numpy as jnp
import numpy as np
from jax import lax
from jax.experimental import pallas as pl
from jax.experimental.pallas import tpu as pltpu
from jax.sharding import PartitionSpec as P

H = 12
DH = 64
BOXF = 128
NB = 32
EPS = 1e-05
LOG2E = 1.4426950408889634
BF = jnp.bfloat16
F32 = jnp.float32
VMEM = 56 << 20
SHORT = pl.CostEstimate(flops=1, bytes_accessed=1, transcendentals=0)


def dot(a, b, ca=1, cb=0):
    return lax.dot_general(a, b, (((ca,), (cb,)), ((), ())), preferred_element_type=F32)


ROUND = 1.5 * 2.0**23 * 2.0**-8
SMALL = 1.6e-4


def unpack(both):
    first = (both + ROUND) - ROUND
    return first, (both - first) * (1.0 / SMALL)


def bucket_of(offset, shift):
    magnitude = jnp.abs(offset)
    if shift:
        magnitude = magnitude >> shift
    count = jnp.minimum(magnitude, 8)
    for n, bound in enumerate((12, 16, 24, 32, 48, 64, 96)):
        count = jnp.where(magnitude >= bound, 9 + n, count)
    return jnp.where(offset > 0, count + 16, count)


def look_up(table, index):
    dims = lax.GatherDimensionNumbers(
        offset_dims=(),
        collapsed_slice_dims=(1,),
        start_index_map=(1,),
        operand_batching_dims=(0,),
        start_indices_batching_dims=(0,),
    )
    return lax.gather(
        table, index[..., None], dims, slice_sizes=(1, 1), mode=lax.GatherScatterMode.PROMISE_IN_BOUNDS
    )


def sine(angle, quarter):
    n = jnp.round(angle * 0.6366197723675814)
    x = ((angle - n * 1.5703125) - n * 4.837512969970703125e-4) - n * 7.549789954891882e-8
    turn = n.astype(jnp.int32) + quarter
    y = x * x
    odd = x + x * y * (-1.6666654611e-1 + y * (8.3321608736e-3 + y * -1.9515295891e-4))
    even = 1.0 - 0.5 * y + y * y * (4.166664568298827e-2 + y * (-1.388731625493765e-3 + y * 2.443315711809948e-5))
    value = jnp.where((turn & 1) == 0, odd, even)
    return jnp.where((turn & 2) == 0, value, -value)


def window_length(meta_ref, w, windows):
    return meta_ref[4 + meta_ref[1] * windows + w]


def position(index, half, length):
    shifted = index + half * (length // 2)
    return jnp.where(shifted >= length, shifted - length, shifted)


def bias_kernel(meta_ref, own_ref, other_ref, rel_ref, freq_ref, out_ref, map_ref, feat_ref, line, maps, tabs, cols, *, rows):
    length = out_ref.shape[3]
    windows = other_ref.shape[1]
    blocks = length // 128
    span = (2 * blocks - 1) * 128
    w = pl.program_id(0)
    it = pl.program_id(1)
    half = meta_ref[1]

    def box_row(m):
        return jnp.concatenate([own_ref[m, pl.ds(half * windows + w, 1), :], other_ref[m, pl.ds(w, 1), :]], 1)

    @pl.when((w == 0) & (it == 0))
    def _():
        cols[...] = jnp.zeros_like(cols)
        cols[0:NB, 0 : 3 * H] = rel_ref[...] * LOG2E
        t = cols[0:128, :].T
        for kind in range(3):
            for hp in range(H // 2):
                n = kind * H + 2 * hp
                first = (t[n : n + 1, :] + ROUND) - ROUND
                tabs[3 * hp + kind : 3 * hp + kind + 1, :] = first + t[n + 1 : n + 2, :] * SMALL

        mpos = lax.broadcasted_iota(jnp.int32, (32, span), 1) - (length - 128)
        ipos = lax.broadcasted_iota(jnp.int32, (32, span), 0)

        def body(g, carry):
            sl = pl.ds(pl.multiple_of(g * 32, 32), 32)
            index = bucket_of(mpos - (ipos + g * 32), 0)
            for c in range(0, span, 128):
                for hp in range(H // 2):
                    table = jnp.broadcast_to(tabs[3 * hp : 3 * hp + 1, :], (32, 128))
                    a, b = unpack(look_up(table, index[:, c : c + 128]))
                    line[2 * hp, sl, c : c + 128] = a
                    line[2 * hp + 1, sl, c : c + 128] = b
            return carry

        lax.fori_loop(0, 4, body, 0)

    @pl.when(it == 0)
    def _():
        coords = jnp.concatenate([box_row(m) for m in range(4)] * 2, 0).astype(F32)
        by_token = coords.T
        cols[:, 0:8] = by_token
        lane = lax.broadcasted_iota(jnp.int32, (1, BOXF), 1)
        which = lane >> 5
        coord = jnp.where(
            which < 2,
            jnp.where(which == 0, by_token[:, 0:1], by_token[:, 1:2]),
            jnp.where(which == 2, by_token[:, 2:3], by_token[:, 3:4]),
        )
        feat_ref[...] = sine(coord * freq_ref[0:1, :], (lane >> 4) & 1).astype(BF)

    place = position(lax.broadcasted_iota(jnp.int32, (1, length), 1), half, length)
    dead = place >= window_length(meta_ref, w, windows)
    first = it * 128
    here = cols[pl.ds(pl.multiple_of(first, 128), 128), 0:8].astype(jnp.int32)
    for t in range(2):
        index = bucket_of(box_row(t) - here[:, t : t + 1], 2)
        map_ref[0, t] = index.astype(BF)
        maps[t] = index

    def block_of(n):
        return lax.rem(n + half * (blocks // 2), blocks)

    for r in range(0, 128, rows):
        rs = slice(r, r + rows)
        for n in range(blocks):
            cs = slice(n * 128, (n + 1) * 128)
            lc = pl.ds(pl.multiple_of((blocks - 1 + block_of(n) - block_of(it)) * 128, 128), 128)
            ia, idown = maps[0, rs, cs], maps[1, rs, cs]
            for hp in range(H // 2):
                ta = jnp.broadcast_to(tabs[3 * hp + 1 : 3 * hp + 2, :], (rows, 128))
                td = jnp.broadcast_to(tabs[3 * hp + 2 : 3 * hp + 3, :], (rows, 128))
                a, b = unpack(look_up(ta, ia) + look_up(td, idown))
                a = jnp.where(dead[:, cs], -1e9 * LOG2E, a + line[2 * hp, rs, lc])
                b = jnp.where(dead[:, cs], -1e9 * LOG2E, b + line[2 * hp + 1, rs, lc])
                out_ref[0, 2 * hp, rs, cs] = a.astype(BF)
                out_ref[0, 2 * hp + 1, rs, cs] = b.astype(BF)


def score_bias(meta, own, other, rel_tables):
    windows, length = other.shape[1], 2 * other.shape[2]
    span = (2 * (length // 128) - 1) * 128
    freq_count = BOXF // 8
    freqs = np.float32(1000.0) ** (-np.arange(freq_count, dtype=np.float32) / np.float32(freq_count))
    freqs = jnp.asarray(np.tile(freqs.astype(np.float32), (8, 8)))
    return pl.pallas_call(
        partial(bias_kernel, rows=128),
        grid=(windows, length // 128),
        in_specs=[
            pl.BlockSpec(memory_space=pltpu.SMEM),
            pl.BlockSpec(own.shape, lambda w, i: (0, 0, 0)),
            pl.BlockSpec(other.shape, lambda w, i: (0, 0, 0)),
            pl.BlockSpec((NB, 3 * H), lambda w, i: (0, 0)),
            pl.BlockSpec((8, BOXF), lambda w, i: (0, 0)),
        ],
        out_specs=[
            pl.BlockSpec((1, H, 128, length), lambda w, i: (w, 0, i, 0)),
            pl.BlockSpec((1, 2, 128, length), lambda w, i: (w, 0, i, 0)),
            pl.BlockSpec((length, BOXF), lambda w, i: (w, 0)),
        ],
        out_shape=[
            jax.ShapeDtypeStruct((windows, H, length, length), BF),
            jax.ShapeDtypeStruct((windows, 2, length, length), BF),
            jax.ShapeDtypeStruct((windows * length, BOXF), BF),
        ],
        scratch_shapes=[
            pltpu.VMEM((H, 128, span), F32),
            pltpu.VMEM((2, 128, length), jnp.int32),
            pltpu.VMEM((3 * H // 2 + 6, 128), F32),
            pltpu.VMEM((length, 128), F32),
        ],
        compiler_params=pltpu.CompilerParams(vmem_limit_bytes=VMEM),
        cost_estimate=SHORT,
        name="score_bias",
    )(meta, own, other, rel_tables, freqs)


def attend_kernel(meta_ref, q_ref, k_ref, v_ref, b_ref, o_ref, e_ref, r_ref, *, chunk):
    length = q_ref.shape[0]
    lane = lax.broadcasted_iota(jnp.int32, (length, 128), 1)
    place = position(lax.broadcasted_iota(jnp.int32, (length, 128), 0), meta_ref[1], length)
    live = place < window_length(meta_ref, pl.program_id(0), pl.num_programs(0))
    zero, one = jnp.zeros((), BF), jnp.ones((), BF)
    q, k, v = q_ref[...], k_ref[...], v_ref[...]
    outs = []
    for h in range(2):
        mine = (lane < DH) if h == 0 else (lane >= DH)
        keys = jnp.where(mine & live, k, zero)
        values = jnp.where(mine, v, jnp.where(lane == (DH if h == 0 else 0), one, zero))
        scores = dot(q, keys, 1, 1)
        for c in range(0, length, chunk):
            t = scores[c : c + chunk] * (LOG2E * DH**-0.5) + b_ref[0, h, c : c + chunk, :].astype(F32)
            e_ref[0, h, c : c + chunk, :] = jnp.exp2(t - jnp.max(t, 1, keepdims=True)).astype(BF)
        outs.append(dot(e_ref[0, h], values))
    r = jnp.where(lane < DH, 1.0 / outs[0][:, DH : DH + 1], 1.0 / outs[1][:, 0:1])
    r_ref[...] = r
    o_ref[...] = (jnp.where(lane < DH, outs[0], outs[1]) * r).astype(BF)


def attend(meta, qkv, bias):
    windows, _, length, _ = bias.shape
    pairs = H // 2
    col = lambda off: pl.BlockSpec((length, 128), lambda w, h: (w, off + h))
    sq = pl.BlockSpec((1, 2, length, length), lambda w, h: (w, h, 0, 0))
    width = H * DH
    return pl.pallas_call(
        partial(attend_kernel, chunk=64),
        grid=(windows, pairs),
        in_specs=[pl.BlockSpec(memory_space=pltpu.SMEM), col(0), col(pairs), col(2 * pairs), sq],
        out_specs=[col(0), sq, col(0)],
        out_shape=[
            jax.ShapeDtypeStruct((windows * length, width), BF),
            jax.ShapeDtypeStruct((windows, H, length, length), BF),
            jax.ShapeDtypeStruct((windows * length, width), F32),
        ],
        compiler_params=pltpu.CompilerParams(vmem_limit_bytes=VMEM),
        cost_estimate=SHORT,
        name="attend",
    )(meta, qkv, qkv, qkv, bias)


def attend_back_kernel(meta_ref, q_ref, k_ref, v_ref, e_ref, r_ref, o_ref, do_ref, *refs, chunk):
    d_ref, ds_ref, line_ref, sum_ref = refs[-4:]
    length = q_ref.shape[0]
    blocks = length // 128
    w = pl.program_id(1)
    lane = lax.broadcasted_iota(jnp.int32, (length, 128), 1)
    zero = jnp.zeros((), BF)
    q, k, v = q_ref[...], k_ref[...], v_ref[...]
    up = do_ref[...].astype(F32) * r_ref[...]
    both = up * o_ref[...].astype(F32)
    up = up.astype(BF)
    up_t, q_t = up.T, q.T
    dq, dv_t, dk_t = None, [], []

    def block_of(n):
        return lax.rem(n + meta_ref[1] * (blocks // 2), blocks)

    @pl.when(w == 0)
    def _():
        line_ref[...] = jnp.zeros_like(line_ref)

    for h in range(2):
        mine = (lane < DH) if h == 0 else (lane >= DH)
        center = jnp.sum(jnp.where(mine, both, 0.0), 1, keepdims=True)
        dp = dot(up, jnp.where(mine, v, zero), 1, 1)
        for c in range(0, length, chunk):
            e = e_ref[0, h, c : c + chunk, :].astype(F32)
            ds = e * (dp[c : c + chunk] - center[c : c + chunk])
            ds_ref[0, h, c : c + chunk, :] = ds.astype(BF)
            rows = slice(c % 128, c % 128 + chunk)
            for n in range(blocks):
                d = blocks - 1 + block_of(n) - block_of(c // 128)
                line_ref[h, rows, pl.ds(pl.multiple_of(d * 128, 128), 128)] += ds[:, n * 128 : (n + 1) * 128]
        ds = ds_ref[0, h]
        part = dot(ds, jnp.where(mine, k, zero))
        dq = part if dq is None else dq + part
        dv_t.append(dot(up_t[h * DH : (h + 1) * DH], e_ref[0, h]))
        dk_t.append(dot(q_t[h * DH : (h + 1) * DH], ds))
    parts = (dq * DH**-0.5, jnp.concatenate(dk_t, 0).T * DH**-0.5, jnp.concatenate(dv_t, 0).T)
    for n, x in enumerate(parts):
        cols = slice(n * 128, (n + 1) * 128)
        x = x.astype(BF)
        d_ref[:, cols] = x
        sums = jnp.broadcast_to(column_sums(x.astype(F32)), (8, 128))
        sum_ref[:, cols] = jnp.where(w == 0, sums, sum_ref[:, cols] + sums)


def attend_back(meta, qkv, e, r, o, do, first, count, total, at, before=None):
    windows, _, length, _ = e.shape
    pairs = H // 2
    col = lambda off: pl.BlockSpec((length, 128), lambda h, w: (w, off + h))
    sq = pl.BlockSpec((1, 2, length, length), lambda h, w: (w, first + h, 0, 0))
    span = (2 * (length // 128) - 1) * 128
    more = [] if before is None else [before]
    return pl.pallas_call(
        partial(attend_back_kernel, chunk=64),
        grid=(count, windows),
        in_specs=[pl.BlockSpec(memory_space=pltpu.SMEM)]
        + [col(first), col(pairs + first), col(2 * pairs + first), sq, col(first), col(first), col(first)]
        + [pl.BlockSpec(memory_space=pl.ANY)] * len(more),
        out_specs=[
            pl.BlockSpec((length, 384), lambda h, w: (w, at + h)),
            pl.BlockSpec((1, 2, length, length), lambda h, w: (w, h, 0, 0)),
            pl.BlockSpec((2, 128, span), lambda h, w: (h, 0, 0)),
            pl.BlockSpec((8, 384), lambda h, w: (0, h)),
        ],
        out_shape=[
            jax.ShapeDtypeStruct((windows * length, total * 384), BF),
            jax.ShapeDtypeStruct((windows, 2 * count, length, length), BF),
            jax.ShapeDtypeStruct((2 * count, 128, span), F32),
            jax.ShapeDtypeStruct((8, count * 384), F32),
        ],
        input_output_aliases={8: 0} if more else {},
        compiler_params=pltpu.CompilerParams(vmem_limit_bytes=VMEM),
        cost_estimate=SHORT,
        name="attend_back",
    )(meta, qkv, qkv, qkv, e, r, o, do, *more)


def spread(refs, rows, stride):
    h = 0
    for ref in refs:
        for n in range(ref.shape[-3]):
            x = (ref[0, n] if len(ref.shape) == 4 else ref[n]).astype(F32)
            for c in range(x.shape[1] // 128):
                rows[c, h * stride : h * stride + x.shape[0], :] = x[:, c * 128 : (c + 1) * 128]
            h += 1


def heads_of(rows, i, stride):
    return [rows[c, pl.ds(i, 16, stride=stride), :].astype(BF) for c in range(rows.shape[0])]


def one_hot(index):
    width = index.shape[1]
    ids = lax.broadcasted_iota(jnp.int32, (NB, width), 0).astype(BF)
    hit = jnp.broadcast_to(index, (NB, width)).astype(BF) == ids
    return jnp.where(hit, jnp.ones((), BF), jnp.zeros((), BF))


def table_kernel(*refs, parts, with_line):
    ds_refs, refs = refs[:parts], refs[parts:]
    line_refs, refs = refs[: parts * with_line], refs[parts * with_line :]
    map_ref, out_ref, rows, maps = refs[0], refs[1], refs[-2], refs[-1]
    tile = map_ref.shape[2]
    step = pl.program_id(0)

    @pl.when(step == 0)
    def _():
        out_ref[...] = jnp.zeros_like(out_ref)
        rows[...] = jnp.zeros_like(rows)

    if with_line:
        line_out, line_rows = refs[2], refs[3]
        share = line_refs[0].shape[1]
        span = line_refs[0].shape[2]

        @pl.when(step == 0)
        def _():
            line_out[...] = jnp.zeros_like(line_out)
            line_rows[...] = jnp.zeros_like(line_rows)

        spread(line_refs, line_rows, share + 8)
        offset = lax.broadcasted_iota(jnp.int32, (8, span), 1) - (span - 128) // 2
        down = lax.broadcasted_iota(jnp.int32, (8, span), 0) + step * share
        lhs, rhs = [], []
        for i in range(share):
            if i % 8 == 0:
                index = bucket_of(offset - (down + i), 0).astype(F32)
            lhs += heads_of(line_rows, i, share + 8)
            rhs.append(one_hot(index[i % 8 : i % 8 + 1, :]))
        line_out[...] += dot(jnp.concatenate(lhs, 1), jnp.concatenate(rhs, 1), 1, 1)

    spread(ds_refs, rows, tile + 8)
    maps[...] = map_ref[0].astype(F32)
    lhs, rhs = [], []
    for i in range(tile):
        lhs += heads_of(rows, i, tile + 8)
        rhs.append(jnp.concatenate([one_hot(maps[t, i : i + 1, :]) for t in range(2)], 0))
    out_ref[...] += dot(jnp.concatenate(lhs, 1), jnp.concatenate(rhs, 1), 1, 1)


def table_grads(ds_parts, lines, maps, w):
    _, _, length, _ = maps.shape
    tile = 64
    parts = len(ds_parts)
    steps = length // tile
    outs, out_shapes = [pl.BlockSpec((16, 2 * NB), lambda i: (0, 0))], [jax.ShapeDtypeStruct((16, 2 * NB), F32)]
    line_specs, line_rows = [], []
    if lines:
        share, span = 128 // steps, lines[0].shape[2]
        line_specs = [pl.BlockSpec((x.shape[0], share, span), lambda i: (0, i, 0)) for x in lines]
        line_rows = [pltpu.VMEM((span // 128, 16 * (share + 8), 128), F32)]
        outs.append(pl.BlockSpec((16, NB), lambda i: (0, 0)))
        out_shapes.append(jax.ShapeDtypeStruct((16, NB), F32))
    return pl.pallas_call(
        partial(table_kernel, parts=parts, with_line=bool(lines)),
        grid=(steps,),
        in_specs=[pl.BlockSpec((1, x.shape[1], tile, length), lambda i: (w, 0, i, 0)) for x in ds_parts]
        + line_specs
        + [pl.BlockSpec((1, 2, tile, length), lambda i: (w, 0, i, 0))],
        out_specs=outs,
        out_shape=out_shapes,
        scratch_shapes=line_rows
        + [pltpu.VMEM((length // 128, 16 * (tile + 8), 128), F32), pltpu.VMEM((2, tile, length), F32)],
        compiler_params=pltpu.CompilerParams(vmem_limit_bytes=VMEM),
        cost_estimate=SHORT,
        name="table_grads",
    )(*ds_parts, *lines, maps)


def gelu_both(x):
    cdf = 0.5 + 0.5 * lax.erf(x * 0.7071067811865476)
    density = jnp.exp2((-0.5 * LOG2E) * (x * x)) * 0.3989422804014327
    return x * cdf, cdf + x * density


def norm_forward(summed, params):
    centered = summed - jnp.mean(summed, -1, keepdims=True)
    inverse = lax.rsqrt(jnp.mean(centered * centered, -1, keepdims=True) + EPS)
    normed = centered * inverse
    return normed * params[0:1] + params[1:2], normed, inverse


def norm_backward(upstream, normed, inverse, params):
    scaled = upstream * params[0:1]
    return inverse * (
        scaled - jnp.mean(scaled, -1, keepdims=True) - normed * jnp.mean(scaled * normed, -1, keepdims=True)
    )


def column_sums(x):
    return jnp.sum(x, 0, keepdims=True)


def tokens_of(own_ref, other_ref, chunk):
    windows, local, _ = other_ref.shape
    step = min(chunk, local)
    for w in range(windows):
        for n, ref in enumerate((own_ref, other_ref)):
            for c in range(0, local, step):
                yield slice((2 * w + n) * local + c, (2 * w + n) * local + c + step), ref[w, c : c + step, :]


def front_kernel(meta_ref, own_ref, other_ref, f_ref, box_ref, w_ref, qv_ref, low_ref, out_ref):
    step = pl.program_id(0)
    third = pl.num_programs(0) // 3

    @pl.when(step == 0)
    def _():
        for cs, x in tokens_of(own_ref, other_ref, 256):
            low_ref[cs, :] = (x.astype(F32) + dot(f_ref[cs, :], box_ref[...])).astype(BF)

    wide = out_ref.shape[1]
    cols = pl.ds(pl.multiple_of(lax.rem(step, third) * wide, wide), wide)
    shift = jnp.where(step < third, qv_ref[0:1, cols], jnp.where(step < 2 * third, 0.0, qv_ref[1:2, cols]))
    out_ref[...] = (dot(low_ref[...], w_ref[...]) + shift).astype(BF)


def front(meta, own, other, features, box_weight, qkv_weight, qv_bias):
    windows, local, width = other.shape
    tokens = 2 * windows * local
    cols = qkv_weight.shape[1]
    whole = lambda x: pl.BlockSpec(x.shape, lambda n, p: (0,) * len(x.shape))
    return pl.pallas_call(
        front_kernel,
        grid_spec=pltpu.PrefetchScalarGridSpec(
            num_scalar_prefetch=1,
            grid=(cols // width,),
            in_specs=[
                pl.BlockSpec(other.shape, lambda n, p: (p[1], 0, 0)),
                whole(other),
                whole(features),
                whole(box_weight),
                pl.BlockSpec((width, width), lambda n, p: (0, n)),
                whole(qv_bias),
            ],
            out_specs=[
                pl.BlockSpec((tokens, width), lambda n, p: (0, 0)),
                pl.BlockSpec((tokens, width), lambda n, p: (0, n)),
            ],
        ),
        out_shape=[jax.ShapeDtypeStruct((tokens, width), BF), jax.ShapeDtypeStruct((tokens, cols), BF)],
        compiler_params=pltpu.CompilerParams(vmem_limit_bytes=VMEM),
        cost_estimate=SHORT,
        name="front",
    )(meta, own, other, features, box_weight, qkv_weight, qv_bias)


def feed_kernel(meta_ref, own_ref, other_ref, f_ref, box_ref, att_ref, wo_ref, bo_ref, n1_ref, w1_ref, b1_ref, w2_ref, b2_ref, n2_ref, cot_own_ref, cot_other_ref, z_ref, low_ref, act_ref, slope_ref, out_own_ref, out_other_ref, dlow_ref, sum_ref, acc, *, chunk):
    step = pl.program_id(0)
    tokens = low_ref.shape[0]

    @pl.when(step == 0)
    def _():
        for cs, x in tokens_of(own_ref, other_ref, chunk):
            entry = x.astype(F32) + dot(f_ref[cs, :], box_ref[...])
            z = entry + (dot(att_ref[cs, :], wo_ref[...]) + bo_ref[...])
            second = norm_forward(z, n1_ref[...])[0]
            z_ref[cs, :] = z.astype(BF)
            low_ref[cs, :] = second.astype(BF)
            acc[cs, :] = second

    for c in range(0, tokens, chunk):
        cs = slice(c, c + chunk)
        active, slope = gelu_both(dot(low_ref[cs, :], w1_ref[...]) + b1_ref[...])
        active = active.astype(BF)
        act_ref[cs, :] = active
        slope_ref[cs, :] = slope.astype(BF)
        acc[cs, :] += dot(active, w2_ref[...])

    @pl.when(step == pl.num_programs(0) - 1)
    def _():
        sums = [0.0, 0.0, 0.0]
        local = cot_other_ref.shape[1]
        for cs, x in tokens_of(cot_own_ref, cot_other_ref, 128):
            result, normed, inverse = norm_forward(acc[cs, :] + b2_ref[...], n2_ref[...])
            place = cs.start % local
            out = (out_own_ref, out_other_ref)[cs.start // local % 2]
            out[cs.start // local // 2, place : place + 128, :] = result.astype(BF)
            up = x.astype(F32)
            low = norm_backward(up, normed, inverse, n2_ref[...]).astype(BF)
            dlow_ref[cs, :] = low
            sums = [sums[0] + column_sums(up * normed), sums[1] + column_sums(up), sums[2] + column_sums(low.astype(F32))]
        sum_ref[...] = jnp.concatenate(sums + [jnp.zeros((5, sums[0].shape[1]), F32)], 0)


def feed(meta, own, other, features, box_weight, attended, out_weight, out_bias, norm_one, w1, b1, w2, b2, norm_two, cot_own, cot_other):
    tokens, width = attended.shape
    inner = w1.shape[1]
    tile = 1024
    whole = lambda shape: pl.BlockSpec(shape, lambda n, p: (0,) * len(shape))
    mine = pl.BlockSpec(other.shape, lambda n, p: (p[1], 0, 0))
    full = whole((tokens, width))
    part = pl.BlockSpec((tokens, tile), lambda n, p: (0, n))
    return pl.pallas_call(
        partial(feed_kernel, chunk=512),
        grid_spec=pltpu.PrefetchScalarGridSpec(
            num_scalar_prefetch=1,
            grid=(inner // tile,),
            in_specs=[
                mine,
                whole(other.shape),
                whole(features.shape),
                whole(box_weight.shape),
                full,
                whole(out_weight.shape),
                whole((1, width)),
                whole((2, width)),
                pl.BlockSpec((width, tile), lambda n, p: (0, n)),
                pl.BlockSpec((1, tile), lambda n, p: (0, n)),
                pl.BlockSpec((tile, width), lambda n, p: (n, 0)),
                whole((1, width)),
                whole((2, width)),
                mine,
                whole(other.shape),
            ],
            out_specs=[full, full, part, part, whole(other.shape), whole(other.shape), full, whole((8, width))],
            scratch_shapes=[pltpu.VMEM((tokens, width), F32)],
        ),
        out_shape=[
            jax.ShapeDtypeStruct((tokens, width), BF),
            jax.ShapeDtypeStruct((tokens, width), BF),
            jax.ShapeDtypeStruct((tokens, inner), BF),
            jax.ShapeDtypeStruct((tokens, inner), BF),
            jax.ShapeDtypeStruct(other.shape, BF),
            jax.ShapeDtypeStruct(other.shape, BF),
            jax.ShapeDtypeStruct((tokens, width), BF),
            jax.ShapeDtypeStruct((8, width), F32),
        ],
        compiler_params=pltpu.CompilerParams(vmem_limit_bytes=VMEM),
        cost_estimate=SHORT,
        name="feed",
    )(
        meta, own, other, features, box_weight, attended, out_weight, out_bias.reshape(1, -1), norm_one,
        w1, b1.reshape(1, -1), w2, b2.reshape(1, -1), norm_two, cot_own, cot_other,
    )


def feed_back_kernel(dlow_ref, w1_ref, w2_ref, slope_ref, z_ref, n1_ref, wo_ref, din_ref, bias_ref, dbr_ref, datt_ref, sum_ref, acc, *, chunk):
    step = pl.program_id(0)
    tokens = dlow_ref.shape[0]

    @pl.when(step == 0)
    def _():
        acc[...] = dlow_ref[...].astype(F32)

    sums = 0.0
    for c in range(0, tokens, chunk):
        cs = slice(c, c + chunk)
        d_inner = (dot(dlow_ref[cs, :], w2_ref[...], 1, 1) * slope_ref[cs, :].astype(F32)).astype(BF)
        din_ref[cs, :] = d_inner
        sums = sums + column_sums(d_inner.astype(F32))
        acc[cs, :] += dot(d_inner, w1_ref[...], 1, 1)
    bias_ref[...] = jnp.concatenate([sums, jnp.zeros((7, sums.shape[1]), F32)], 0)

    @pl.when(step == pl.num_programs(0) - 1)
    def _():
        totals = [0.0, 0.0, 0.0]
        for c in range(0, tokens, 128):
            cs = slice(c, c + 128)
            _, normed, inverse = norm_forward(z_ref[cs, :].astype(F32), n1_ref[...])
            up = acc[cs, :]
            low = norm_backward(up, normed, inverse, n1_ref[...]).astype(BF)
            dbr_ref[cs, :] = low
            totals = [
                totals[0] + column_sums(up * normed),
                totals[1] + column_sums(up),
                totals[2] + column_sums(low.astype(F32)),
            ]
        sum_ref[...] = jnp.concatenate(totals + [jnp.zeros((5, totals[0].shape[1]), F32)], 0)
        datt_ref[...] = dot(dbr_ref[...], wo_ref[...], 1, 1).astype(BF)


def feed_back(d_outer, w1, w2, slope, z_one, norm_one, out_weight):
    tokens, width = z_one.shape
    inner = w1.shape[1]
    tile = 1024
    whole = lambda shape: pl.BlockSpec(shape, lambda n: (0, 0))
    full = whole((tokens, width))
    return pl.pallas_call(
        partial(feed_back_kernel, chunk=512),
        grid=(inner // tile,),
        in_specs=[
            full,
            pl.BlockSpec((width, tile), lambda n: (0, n)),
            pl.BlockSpec((tile, width), lambda n: (n, 0)),
            pl.BlockSpec((tokens, tile), lambda n: (0, n)),
            full,
            whole((2, width)),
            whole((width, width)),
        ],
        out_specs=[
            pl.BlockSpec((tokens, tile), lambda n: (0, n)),
            pl.BlockSpec((8, tile), lambda n: (0, n)),
            full,
            full,
            whole((8, width)),
        ],
        out_shape=[
            jax.ShapeDtypeStruct((tokens, inner), BF),
            jax.ShapeDtypeStruct((8, inner), F32),
            jax.ShapeDtypeStruct((tokens, width), BF),
            jax.ShapeDtypeStruct((tokens, width), BF),
            jax.ShapeDtypeStruct((8, width), F32),
        ],
        scratch_shapes=[pltpu.VMEM((tokens, width), F32)],
        compiler_params=pltpu.CompilerParams(vmem_limit_bytes=VMEM),
        cost_estimate=SHORT,
        name="feed_back",
    )(d_outer, w1, w2, slope, z_one, norm_one, out_weight)


UNIT = 384
PIECES = 2


def halves(full, place_ref):
    rows = full.shape[0] // 2
    upper = place_ref[1] == 0
    low, high = full[:rows], full[rows:]
    return jnp.where(upper, high, low).astype(BF), jnp.where(upper, low, high).astype(BF)


def wide_grads_kernel(place_ref, *refs, counts):
    step = pl.program_id(0)
    pairs = len(counts)
    outs = refs[3 * pairs :]
    at = 0
    for n, count in enumerate(counts):

        @pl.when((step >= at) & (step < at + count))
        def _():
            full = dot(refs[3 * n][...], jnp.concatenate([refs[3 * n + 1][...], refs[3 * n + 2][...]], 1), 0, 0)
            both = halves(full, place_ref)
            for m, x in enumerate(both):
                side = x.shape[0] // 2
                for k in range(2):
                    outs[2 * m + k][...] = x[k * side : (k + 1) * side, :UNIT].reshape(outs[2 * m + k].shape)
                outs[4 + m][...] = x[:, UNIT:].reshape(outs[4 + m].shape)

        at += count


def wide_grads(place, pairs):
    tokens, rows = pairs[0][0].shape
    counts = [right.shape[1] // (2 * UNIT) for _, right in pairs]
    specs, at = [], 0
    for (left, right), count in zip(pairs, counts):

        def block(i, p, send, at=at, count=count):
            owner = 1 - p[0] if send else p[0]
            return (0, owner * count + jnp.clip(i - at, 0, count - 1))

        specs += [
            pl.BlockSpec(left.shape, lambda i, p: (0, 0)),
            pl.BlockSpec((tokens, UNIT), partial(block, send=True)),
            pl.BlockSpec((tokens, UNIT), partial(block, send=False)),
        ]
        at += count
    piece = pl.BlockSpec((1, 1, rows // 4, UNIT), lambda i, p: (0, i, 0, 0))
    out = pl.BlockSpec((2, 1, rows // 4, UNIT), lambda i, p: (0, i, 0, 0))
    outs = pl.pallas_call(
        partial(wide_grads_kernel, counts=counts),
        grid_spec=pltpu.PrefetchScalarGridSpec(
            num_scalar_prefetch=1,
            grid=(at,),
            in_specs=specs,
            out_specs=[piece] * 4 + [out] * 2,
        ),
        out_shape=[jax.ShapeDtypeStruct((n, at, rows // 4, UNIT), BF) for n in (1, 1, 1, 1, 2, 2)],
        compiler_params=pltpu.CompilerParams(vmem_limit_bytes=VMEM),
        cost_estimate=SHORT,
        name="wide_grads",
    )(place, *[x for left, right in pairs for x in (left, right, right)])
    return [x.reshape(-1, UNIT) for x in outs]


def long_grads_kernel(place_ref, left_ref, send_ref, keep_ref, *outs):
    full = dot(left_ref[...], jnp.concatenate([send_ref[...], keep_ref[...]], 1), 0, 0).astype(BF)
    for n in range(4):

        @pl.when(pl.program_id(0) == n)
        def _():
            outs[n][...] = full[:, :UNIT]
            outs[4 + n // 2][...] = full[:, UNIT:]


def long_grads(place, left, right):
    tokens, rows = left.shape
    tile = rows // 4

    def quarter(i, p):
        owner = jnp.where(i < 2, 1 - p[1], p[1])
        return (0, owner * 2 + lax.rem(i, 2))

    piece = pl.BlockSpec((tile, UNIT), lambda i, p: (0, 0))
    other = pl.BlockSpec((tile, UNIT), lambda i, p: (jnp.minimum(i, 1), 0))
    own = pl.BlockSpec((tile, UNIT), lambda i, p: (jnp.maximum(i - 2, 0), 0))
    return pl.pallas_call(
        long_grads_kernel,
        grid_spec=pltpu.PrefetchScalarGridSpec(
            num_scalar_prefetch=1,
            grid=(4,),
            in_specs=[
                pl.BlockSpec((tokens, tile), quarter),
                pl.BlockSpec((tokens, UNIT), lambda i, p: (0, 1 - p[0])),
                pl.BlockSpec((tokens, UNIT), lambda i, p: (0, p[0])),
            ],
            out_specs=[piece] * 4 + [other, own],
        ),
        out_shape=[jax.ShapeDtypeStruct((n * tile, UNIT), BF) for n in (1, 1, 1, 1, 2, 2)],
        compiler_params=pltpu.CompilerParams(vmem_limit_bytes=VMEM),
        cost_estimate=SHORT,
        name="long_grads",
    )(place, left, right, right)


E_ROWS = 16


def last_kernel(place_ref, x_ref, dx_ref, f_ref, own_ref, other_ref, two_ref, one_ref, in_ref, *refs):
    qv_refs, (line_ref, small0_ref, small1_ref), outs = refs[:3], refs[3:6], refs[6:]
    mine = place_ref[0] == 0
    upper = place_ref[1] == 0
    width = x_ref.shape[1]
    middle = width // 2
    x = dot(x_ref[...], dx_ref[...], 0, 0).astype(BF)
    entry = jnp.concatenate([ref[w] for w in range(own_ref.shape[0]) for ref in (own_ref, other_ref)], 0)
    box = dot(f_ref[...], entry, 0, 0).astype(BF)
    tables = jnp.concatenate([line_ref[...], small0_ref[...] + small1_ref[...], jnp.zeros((16, NB), F32)], 1).T
    blocks = [ref[0:1, p : p + UNIT] for ref in qv_refs for p in range(0, ref.shape[1], UNIT)]
    qv = [jnp.concatenate([y[:, at : at + 128] for y in blocks], 1) for at in (0, 256)]
    halves_of = []
    for n in range(2):
        cols = slice(n * middle, (n + 1) * middle)
        inner = in_ref[0:1, n * 2 * width : (n + 1) * 2 * width]
        sums = [
            two_ref[n : n + 1, :],
            one_ref[n : n + 1, :],
            qv[n],
            jnp.concatenate([one_ref[2:3, cols], two_ref[2:3, cols]], 1),
            inner[:, :width],
            inner[:, width:],
            jnp.zeros((E_ROWS - 6, width), F32),
        ]
        share = [tables[m * NB + n * NB // 2 : m * NB + (n + 1) * NB // 2, :] for m in range(3)]
        share = [jnp.pad(t, ((0, 0), (0, 128 - t.shape[1]))) for t in share]
        sides = [jnp.concatenate(sums, 0), jnp.concatenate(share + [jnp.zeros((E_ROWS, width - 3 * 128), F32)], 1)]
        q, h = x.shape[0] // 4, box.shape[0] // 4
        halves_of.append(
            jnp.concatenate(
                [
                    y
                    for m in range(2)
                    for y in (
                        x[(2 * n + m) * q : (2 * n + m + 1) * q],
                        box[(2 * n + m) * h : (2 * n + m + 1) * h],
                        sides[m].astype(BF),
                    )
                ],
                0,
            )
        )
    for m in range(2):
        rows = jnp.where(upper, halves_of[1 - m], halves_of[m])
        outs[m][...] = jnp.where(mine, rows[:, middle:], rows[:, :middle])
        outs[2 + m][...] = jnp.where(mine, rows[:, :middle], rows[:, middle:])


def last_grads(place, x, dx, f, own, other, *sums):
    rows = (x.shape[1] + f.shape[1]) // 4 + E_ROWS
    vmem = pl.BlockSpec(memory_space=pltpu.VMEM)
    return pl.pallas_call(
        last_kernel,
        in_specs=[pl.BlockSpec(memory_space=pltpu.SMEM)] + [vmem] * (5 + len(sums)),
        out_specs=[vmem] * 4,
        out_shape=[jax.ShapeDtypeStruct((2 * rows, UNIT), BF)] * 4,
        compiler_params=pltpu.CompilerParams(vmem_limit_bytes=VMEM),
        cost_estimate=SHORT,
        name="last_grads",
    )(place, x, dx, f, own, other, *sums)


def lay_kernel(place_ref, *refs, kind, rows):
    last = refs[4:8] if kind == "heads" else refs[:4]
    pieces, outs = refs[:4], refs[8 if kind == "heads" else 4 :]
    core, step = place_ref[0], pl.program_id(0)

    def lay_piece(ref, owner):
        blocks = ref.shape[0] // rows
        for n in range(blocks):
            x = ref[n * rows : (n + 1) * rows, :].astype(F32)
            if kind == "long":
                outs[0][n * rows : (n + 1) * rows, owner * UNIT : (owner + 1) * UNIT] = x
            elif kind == "wide":
                at = (owner * blocks + n) * UNIT
                outs[0][:, at : at + UNIT] = x
            elif n == 0:
                outs[0][:, owner * UNIT : (owner + 1) * UNIT] = x
            else:
                lay_pair(x, owner * 2 + n - 1)

    def lay_last(ref, owner):
        lay_pair(ref[:rows, :].astype(F32), 4 + owner)
        box = BOXF // 4
        cols = slice(owner * UNIT, (owner + 1) * UNIT)
        outs[2][:, cols] = ref[rows : rows + box, :].astype(F32)
        small = ref[rows + box : rows + box + E_ROWS, :].astype(F32)

        @pl.when(step == 0)
        def _():
            for n in range(3):
                outs[3 + n][:, cols] = small[n : n + 1]
            outs[6 + owner][...] = small[3]
            for n in range(2):
                at = n * 2 * UNIT + owner * UNIT
                outs[8][at : at + UNIT] = small[4 + n]

        if owner == 0:

            @pl.when(step == 1)
            def _():
                outs[9][...] = jnp.concatenate([small[:, n * 128 : n * 128 + H] for n in range(3)], 1)

    def lay_pair(x, pair):
        for m in range(3):
            at = (m * (H // 2) + pair) * 128
            outs[1][:, at : at + 128] = x[:, m * 128 : (m + 1) * 128]

    def choose(refs, side, lay_one):
        for other_side in range(2):
            for owner in range(2):
                for other_core in range(2):

                    @pl.when(((step == side) == (other_side == 0)) & (core == (owner ^ other_core)))
                    def _():
                        lay_one(refs[2 * other_side + other_core], owner)

    choose(pieces, place_ref[2], lay_piece)
    if kind == "heads":
        choose(last, place_ref[3], lay_last)


def lay(place, pieces, kind, rows):
    blocks = pieces[0].shape[0] // rows
    whole = None
    if kind == "long":
        shapes = [(2 * blocks * rows, 2 * UNIT)]
    elif kind == "wide":
        shapes = [(2 * rows, 2 * blocks * UNIT)]
    else:
        width = 2 * UNIT
        shapes = [(2 * rows, width), (2 * rows, 3 * width), (BOXF // 2, width)]
        whole = [(1, width)] * 3 + [(UNIT,)] * 2 + [(2 * width,), (NB // 2, 3 * H)]
    return pl.pallas_call(
        partial(lay_kernel, kind=kind, rows=rows),
        grid=(2,),
        in_specs=[pl.BlockSpec(memory_space=pltpu.SMEM)] + [pl.BlockSpec(x.shape, lambda i: (0, 0)) for x in pieces],
        out_specs=[pl.BlockSpec((m // 2, n), lambda i: (i, 0)) for m, n in shapes]
        + [pl.BlockSpec(shape, lambda i, n=len(shape): (0,) * n) for shape in whole or []],
        out_shape=[jax.ShapeDtypeStruct(shape, F32) for shape in shapes + (whole or [])],
        compiler_params=pltpu.CompilerParams(vmem_limit_bytes=VMEM),
        cost_estimate=SHORT,
        name="lay",
    )(place, *pieces)


def entry_kernel(a_ref, b_ref, w_ref, sum_ref, own_ref, other_ref):
    pairs = H // 2
    weight = jnp.concatenate([w_ref[:, (m * pairs + n) * 128 : (m * pairs + n + 1) * 128] for n in range(pairs) for m in range(3)], 1)
    both = jnp.concatenate([a_ref[...], b_ref[...]], 1)
    out = (sum_ref[...].astype(F32) + dot(both, weight, 1, 1)).astype(BF)
    local = own_ref.shape[1]
    own_ref[0] = out[:local]
    other_ref[0] = out[local:]


def entry_grad(first, last, weight, base, windows):
    tokens, width = base.shape
    tile = tokens // windows
    row = lambda x: pl.BlockSpec((tile, x.shape[1]), lambda i: (i, 0))
    out = pl.BlockSpec((1, tile // 2, width), lambda i: (i, 0, 0))
    return pl.pallas_call(
        entry_kernel,
        grid=(windows,),
        in_specs=[row(first), row(last), pl.BlockSpec(weight.shape, lambda i: (0, 0)), row(base)],
        out_specs=[out, out],
        out_shape=[jax.ShapeDtypeStruct((windows, tile // 2, width), BF)] * 2,
        compiler_params=pltpu.CompilerParams(vmem_limit_bytes=VMEM),
        cost_estimate=SHORT,
        name="entry_grad",
    )(first, last, weight, base)


def shards(
    docs,
    hidden_in,
    boxes,
    lengths,
    box_weight,
    qkv_weight,
    qv_bias,
    out_weight,
    out_bias,
    rel_tables,
    norm_one,
    ffn_in_weight,
    ffn_in_bias,
    ffn_out_weight,
    ffn_out_bias,
    norm_two,
    cotangent,
):
    half = lax.axis_index("half")
    doc = lax.axis_index("doc")
    core, side = doc & 1, (doc >> 1) & 1
    own, local_len, width = hidden_in.shape
    windows = own // 2
    length = 2 * local_len
    tokens = windows * length

    def swap_half(x):
        return lax.ppermute(x, "half", [(0, 1), (1, 0)])

    def swap_doc(x, bit):
        return lax.ppermute(x, "doc", [(i, i ^ (1 << bit)) for i in range(docs)])

    def part(x, index, axis):
        if isinstance(x, list):
            return jnp.where(index == 0, *x)
        size = x.shape[axis] // 2
        return lax.dynamic_slice_in_dim(x, index * size, size, axis)

    def ordered(index, mine, other, axis):
        return jnp.where(index == 0, jnp.concatenate([mine, other], axis), jnp.concatenate([other, mine], axis))

    def tie(x, *others):
        return lax.optimization_barrier((x,) + others)[0]

    meta = jnp.concatenate([jnp.stack([core, half, side, (doc >> 2) & 1]).astype(jnp.int32), lengths])
    box_other = swap_half(part(boxes, 1 - half, 1))
    hidden_other = swap_half(part(tie(hidden_in, box_other), 1 - half, 0))
    bias, maps, features = score_bias(meta, boxes, box_other, rel_tables)
    cot_other = swap_half(part(tie(cotangent, maps), 1 - half, 0))
    entry_low, qkv = front(meta, hidden_in, hidden_other, features, box_weight, qkv_weight, qv_bias)
    attended, e, r = attend(meta, qkv, bias)
    z_one, second_low, active, slope, out_mine, out_send, d_outer, sums_two = feed(
        meta,
        hidden_in,
        hidden_other,
        features,
        box_weight,
        attended,
        out_weight,
        out_bias,
        norm_one,
        ffn_in_weight,
        ffn_in_bias,
        ffn_out_weight,
        ffn_out_bias,
        norm_two,
        cotangent,
        cot_other,
    )

    pairs, early = H // 2, H // 3
    late_pairs = pairs - early
    step = early // 2
    more = list(range(2, docs.bit_length() - 1))
    place = meta
    last = [None]

    def now(x):
        return x if last[0] is None else tie(x, *last[0])

    def then(x, *more):
        last[0] = (x,) + more
        return x

    def joined(pieces):
        return jnp.concatenate(pieces, 0) if len(pieces) > 1 else pieces[0]

    def total(*xs):
        out = xs[0].astype(F32)
        for x in xs[1:]:
            out = out + x.astype(F32)
        return out.astype(BF)

    class Chain:
        def core(self, *parts):
            pieces, keep, keep_own = parts[:-2], parts[-2], parts[-1]
            count = len(pieces) // 2
            then(keep_own)
            pieces = [swap_doc(x, 0) for x in pieces]
            self.own = [keep, pieces[:count], keep_own, pieces[count:]]

        def half_later(self):
            keep, come, keep_own, come_own = self.own
            send = then(total(now(keep), joined(come)))
            self.own = [keep_own, come_own, swap_half(send)]

        def add_own(self):
            keep_own, come_own, come = self.own
            self.own = [then(total(now(keep_own), joined(come_own))), come]

        def half(self):
            keep, come, keep_own, come_own = self.own
            keep, keep_own = lax.optimization_barrier((keep, keep_own) + last[0])[:2]
            send, own = total(keep, joined(come)), total(keep_own, joined(come_own))
            then(send, own)
            self.own = [own, swap_half(send)]

        def split(self, bit):
            b = (doc >> bit) & 1
            own = [now(self.own[0])] + self.own[1:]
            send = then(total(*[part(x, 1 - b, 0) for x in own]))
            keep = total(*[part(x, b, 0) for x in own])
            self.own = [keep, swap_doc(send, bit)]

        def double(self, bits):
            x = then(total(now(self.own[0]), *self.own[1:]))
            for bit in bits[:-1]:
                x = total(x, swap_doc(x, bit))
            self.own = [x, swap_doc(x, bits[-1])]

        def back(self, bit):
            x = then(total(now(self.own[0]), *self.own[1:]))
            self.parted, self.own = bit, [x, swap_doc(x, bit)]

        def gather(self, bit=1):
            if hasattr(self, "parted"):
                x = then(ordered((doc >> self.parted) & 1, now(self.own[0]), self.own[1], 0))
            else:
                x = then(total(now(self.own[0]), *self.own[1:]))
            self.mine, self.across = x, swap_doc(x, bit)
            self.beside = swap_doc(x, 0)

        def settle(self, *others):
            then(*last[0], self.beside, *others)

        def pieces(self):
            return [now(self.mine), self.beside, self.across, swap_doc(now(self.across), 0)]

    def back(first, count, total_pairs, at, before):
        out = attend_back(meta, qkv, e, r, attended, now(d_attended), first, count, total_pairs, at, before)
        then(out[0])
        return out

    a, b, c, d = Chain(), Chain(), Chain(), Chain()
    block_rows = width // 4
    then(d_outer)
    a.core(*long_grads(place, active, now(d_outer)))
    a.half_later()
    d_inner, sums_in, d_branch, d_attended, sums_one = feed_back(
        now(d_outer), ffn_in_weight, ffn_out_weight, slope, z_one, norm_one, out_weight
    )
    then(d_branch)
    a.add_own()
    b.core(*wide_grads(place, [(second_low, now(d_inner))]))
    a.split(1)
    b.half()
    first_right, ds_0, line_0, qv_0 = back(0, step, early, 0, None)
    a.split(more[0])
    first_right, ds_1, line_1, qv_1 = back(step, early - step, early, step, first_right)
    a.double(more[1:])
    c.core(*wide_grads(place, [(attended, d_branch), (entry_low, now(first_right))]))
    b.split(1)
    c.half()
    last_right, ds_2, line_2, qv_2 = back(early, late_pairs, late_pairs, 0, None)
    a.back(more[0])
    b.split(more[0])
    small_0, line_grad = table_grads([ds_0, ds_1, now(ds_2)], [line_0, line_1, line_2], maps, 0)
    then(small_0)
    a.gather()
    b.double(more[1:])
    c.split(1)
    grad_mine, grad_send = entry_grad(first_right, now(last_right), qkv_weight, d_branch, windows)
    then(grad_send)
    a.settle()
    c.split(more[0])
    b.back(more[0])
    grad_other = swap_half(grad_send)
    small_1 = table_grads([ds_0, ds_1, now(ds_2)], [], maps, 1)[0]
    for w in range(2, windows):
        small_1 = small_1 + table_grads([ds_0, ds_1, ds_2], [], maps, w)[0]
    then(small_1)
    c.double(more[1:])
    b.gather()
    then(*last[0], grad_other, a.across)
    d.core(
        *last_grads(
            place, entry_low, last_right, features, now(grad_mine), grad_send, sums_two, sums_one, sums_in, qv_0, qv_1, qv_2, line_grad, small_0, small_1
        )
    )
    c.back(more[0])
    d.half()
    (ffn_out_grad,) = lay(place, a.pieces(), "long", block_rows)
    then(ffn_out_grad)
    d.split(more[0])
    out_other = swap_half(now(out_send))
    c.gather()
    b.settle()
    d.double(more[1:])
    (ffn_in_grad,) = lay(place, b.pieces(), "wide", block_rows)
    then(ffn_in_grad)
    d.double([1])
    hidden_grad = then(ordered(half, now(grad_mine), grad_other, 0))
    c.settle()
    c_pieces = c.pieces()
    d.gather(more[0])
    out_grad, qkv_grad, box, two, one, qv, out_sum, ffn_out_sum, ffn_in_sum, table = lay(
        place, c_pieces + d.pieces(), "heads", block_rows
    )
    layer_out = ordered(half, now(out_mine), out_other, 0)
    return (
        layer_out,
        hidden_grad,
        box,
        qkv_grad,
        qv,
        out_grad,
        out_sum,
        table,
        one,
        ffn_in_grad,
        ffn_in_sum,
        ffn_out_grad,
        ffn_out_sum,
        two,
    )


def solution(mesh):
    rep = P()
    rows = P("half", None)
    return jax.shard_map(
        partial(shards, mesh.shape["doc"]),
        mesh=mesh,
        in_specs=(P("doc", "half", None), P(None, "doc", "half"), P("doc")) + (rep,) * 12 + (P("doc", "half", None),),
        out_specs=(
            P("doc", "half", None),
            P("doc", "half", None),
            rows,
            rows,
            rows,
            rows,
            P("half"),
            rows,
            rows,
            rows,
            P("half"),
            rows,
            P("half"),
            rows,
        ),
        check_vma=False,
    )
```

```python
from functools import partial

import jax
import jax.numpy as jnp
import numpy as np
from jax import lax
from jax.experimental import pallas as pl
from jax.experimental.pallas import tpu as pltpu
from jax.sharding import PartitionSpec as P

H = 12
DH = 64
BOXF = 128
NB = 32
EPS = 1e-05
LOG2E = 1.4426950408889634
BF = jnp.bfloat16
F32 = jnp.float32
VMEM = 56 << 20
SHORT = pl.CostEstimate(flops=1, bytes_accessed=1, transcendentals=0)


def dot(a, b, ca=1, cb=0):
    return lax.dot_general(a, b, (((ca,), (cb,)), ((), ())), preferred_element_type=F32)


ROUND = 1.5 * 2.0**23 * 2.0**-8
SMALL = 1.6e-4


def unpack(both):
    first = (both + ROUND) - ROUND
    return first, (both - first) * (1.0 / SMALL)


def bucket_of(offset, shift):
    magnitude = jnp.abs(offset)
    if shift:
        magnitude = magnitude >> shift
    count = jnp.minimum(magnitude, 8)
    for n, bound in enumerate((12, 16, 24, 32, 48, 64, 96)):
        count = jnp.where(magnitude >= bound, 9 + n, count)
    return jnp.where(offset > 0, count + 16, count)


def look_up(table, index):
    dims = lax.GatherDimensionNumbers(
        offset_dims=(),
        collapsed_slice_dims=(1,),
        start_index_map=(1,),
        operand_batching_dims=(0,),
        start_indices_batching_dims=(0,),
    )
    return lax.gather(
        table, index[..., None], dims, slice_sizes=(1, 1), mode=lax.GatherScatterMode.PROMISE_IN_BOUNDS
    )


def sine(angle, quarter):
    n = jnp.round(angle * 0.6366197723675814)
    x = ((angle - n * 1.5703125) - n * 4.837512969970703125e-4) - n * 7.549789954891882e-8
    turn = n.astype(jnp.int32) + quarter
    y = x * x
    odd = x + x * y * (-1.6666654611e-1 + y * (8.3321608736e-3 + y * -1.9515295891e-4))
    even = 1.0 - 0.5 * y + y * y * (4.166664568298827e-2 + y * (-1.388731625493765e-3 + y * 2.443315711809948e-5))
    value = jnp.where((turn & 1) == 0, odd, even)
    return jnp.where((turn & 2) == 0, value, -value)


def window_length(meta_ref, w, windows):
    return meta_ref[4 + meta_ref[1] * windows + w]


def position(index, half, length):
    shifted = index + half * (length // 2)
    return jnp.where(shifted >= length, shifted - length, shifted)


def bias_kernel(meta_ref, own_ref, other_ref, rel_ref, freq_ref, out_ref, map_ref, feat_ref, line, maps, tabs, cols, *, rows):
    length = out_ref.shape[3]
    windows = other_ref.shape[1]
    blocks = length // 128
    span = (2 * blocks - 1) * 128
    w = pl.program_id(0)
    it = pl.program_id(1)
    half = meta_ref[1]

    def box_row(m):
        return jnp.concatenate([own_ref[m, pl.ds(half * windows + w, 1), :], other_ref[m, pl.ds(w, 1), :]], 1)

    @pl.when((w == 0) & (it == 0))
    def _():
        cols[...] = jnp.zeros_like(cols)
        cols[0:NB, 0 : 3 * H] = rel_ref[...] * LOG2E
        t = cols[0:128, :].T
        for kind in range(3):
            for hp in range(H // 2):
                n = kind * H + 2 * hp
                first = (t[n : n + 1, :] + ROUND) - ROUND
                tabs[3 * hp + kind : 3 * hp + kind + 1, :] = first + t[n + 1 : n + 2, :] * SMALL

        mpos = lax.broadcasted_iota(jnp.int32, (32, span), 1) - (length - 128)
        ipos = lax.broadcasted_iota(jnp.int32, (32, span), 0)

        def body(g, carry):
            sl = pl.ds(pl.multiple_of(g * 32, 32), 32)
            index = bucket_of(mpos - (ipos + g * 32), 0)
            for c in range(0, span, 128):
                for hp in range(H // 2):
                    table = jnp.broadcast_to(tabs[3 * hp : 3 * hp + 1, :], (32, 128))
                    a, b = unpack(look_up(table, index[:, c : c + 128]))
                    line[2 * hp, sl, c : c + 128] = a
                    line[2 * hp + 1, sl, c : c + 128] = b
            return carry

        lax.fori_loop(0, 4, body, 0)

    @pl.when(it == 0)
    def _():
        coords = jnp.concatenate([box_row(m) for m in range(4)] * 2, 0).astype(F32)
        by_token = coords.T
        cols[:, 0:8] = by_token
        lane = lax.broadcasted_iota(jnp.int32, (1, BOXF), 1)
        which = lane >> 5
        coord = jnp.where(
            which < 2,
            jnp.where(which == 0, by_token[:, 0:1], by_token[:, 1:2]),
            jnp.where(which == 2, by_token[:, 2:3], by_token[:, 3:4]),
        )
        feat_ref[...] = sine(coord * freq_ref[0:1, :], (lane >> 4) & 1).astype(BF)

    place = position(lax.broadcasted_iota(jnp.int32, (1, length), 1), half, length)
    dead = place >= window_length(meta_ref, w, windows)
    first = it * 128
    here = cols[pl.ds(pl.multiple_of(first, 128), 128), 0:8].astype(jnp.int32)
    for t in range(2):
        index = bucket_of(box_row(t) - here[:, t : t + 1], 2)
        map_ref[0, t] = index.astype(BF)
        maps[t] = index

    def block_of(n):
        return lax.rem(n + half * (blocks // 2), blocks)

    for r in range(0, 128, rows):
        rs = slice(r, r + rows)
        for n in range(blocks):
            cs = slice(n * 128, (n + 1) * 128)
            lc = pl.ds(pl.multiple_of((blocks - 1 + block_of(n) - block_of(it)) * 128, 128), 128)
            ia, idown = maps[0, rs, cs], maps[1, rs, cs]
            for hp in range(H // 2):
                ta = jnp.broadcast_to(tabs[3 * hp + 1 : 3 * hp + 2, :], (rows, 128))
                td = jnp.broadcast_to(tabs[3 * hp + 2 : 3 * hp + 3, :], (rows, 128))
                a, b = unpack(look_up(ta, ia) + look_up(td, idown))
                a = jnp.where(dead[:, cs], -1e9 * LOG2E, a + line[2 * hp, rs, lc])
                b = jnp.where(dead[:, cs], -1e9 * LOG2E, b + line[2 * hp + 1, rs, lc])
                out_ref[0, 2 * hp, rs, cs] = a.astype(BF)
                out_ref[0, 2 * hp + 1, rs, cs] = b.astype(BF)


def score_bias(meta, own, other, rel_tables):
    windows, length = other.shape[1], 2 * other.shape[2]
    span = (2 * (length // 128) - 1) * 128
    freq_count = BOXF // 8
    freqs = np.float32(1000.0) ** (-np.arange(freq_count, dtype=np.float32) / np.float32(freq_count))
    freqs = jnp.asarray(np.tile(freqs.astype(np.float32), (8, 8)))
    return pl.pallas_call(
        partial(bias_kernel, rows=128),
        grid=(windows, length // 128),
        in_specs=[
            pl.BlockSpec(memory_space=pltpu.SMEM),
            pl.BlockSpec(own.shape, lambda w, i: (0, 0, 0)),
            pl.BlockSpec(other.shape, lambda w, i: (0, 0, 0)),
            pl.BlockSpec((NB, 3 * H), lambda w, i: (0, 0)),
            pl.BlockSpec((8, BOXF), lambda w, i: (0, 0)),
        ],
        out_specs=[
            pl.BlockSpec((1, H, 128, length), lambda w, i: (w, 0, i, 0)),
            pl.BlockSpec((1, 2, 128, length), lambda w, i: (w, 0, i, 0)),
            pl.BlockSpec((length, BOXF), lambda w, i: (w, 0)),
        ],
        out_shape=[
            jax.ShapeDtypeStruct((windows, H, length, length), BF),
            jax.ShapeDtypeStruct((windows, 2, length, length), BF),
            jax.ShapeDtypeStruct((windows * length, BOXF), BF),
        ],
        scratch_shapes=[
            pltpu.VMEM((H, 128, span), F32),
            pltpu.VMEM((2, 128, length), jnp.int32),
            pltpu.VMEM((3 * H // 2 + 6, 128), F32),
            pltpu.VMEM((length, 128), F32),
        ],
        compiler_params=pltpu.CompilerParams(vmem_limit_bytes=VMEM),
        cost_estimate=SHORT,
        name="score_bias",
    )(meta, own, other, rel_tables, freqs)


def attend_kernel(meta_ref, q_ref, k_ref, v_ref, b_ref, o_ref, e_ref, r_ref, *, chunk):
    length = q_ref.shape[0]
    lane = lax.broadcasted_iota(jnp.int32, (length, 128), 1)
    place = position(lax.broadcasted_iota(jnp.int32, (length, 128), 0), meta_ref[1], length)
    live = place < window_length(meta_ref, pl.program_id(0), pl.num_programs(0))
    zero, one = jnp.zeros((), BF), jnp.ones((), BF)
    q, k, v = q_ref[...], k_ref[...], v_ref[...]
    outs = []
    for h in range(2):
        mine = (lane < DH) if h == 0 else (lane >= DH)
        keys = jnp.where(mine & live, k, zero)
        values = jnp.where(mine, v, jnp.where(lane == (DH if h == 0 else 0), one, zero))
        scores = dot(q, keys, 1, 1)
        for c in range(0, length, chunk):
            t = scores[c : c + chunk] * (LOG2E * DH**-0.5) + b_ref[0, h, c : c + chunk, :].astype(F32)
            e_ref[0, h, c : c + chunk, :] = jnp.exp2(t - jnp.max(t, 1, keepdims=True)).astype(BF)
        outs.append(dot(e_ref[0, h], values))
    r = jnp.where(lane < DH, 1.0 / outs[0][:, DH : DH + 1], 1.0 / outs[1][:, 0:1])
    r_ref[...] = r
    o_ref[...] = (jnp.where(lane < DH, outs[0], outs[1]) * r).astype(BF)


def attend(meta, qkv, bias):
    windows, _, length, _ = bias.shape
    pairs = H // 2
    col = lambda off: pl.BlockSpec((length, 128), lambda w, h: (w, off + h))
    sq = pl.BlockSpec((1, 2, length, length), lambda w, h: (w, h, 0, 0))
    width = H * DH
    return pl.pallas_call(
        partial(attend_kernel, chunk=64),
        grid=(windows, pairs),
        in_specs=[pl.BlockSpec(memory_space=pltpu.SMEM), col(0), col(pairs), col(2 * pairs), sq],
        out_specs=[col(0), sq, col(0)],
        out_shape=[
            jax.ShapeDtypeStruct((windows * length, width), BF),
            jax.ShapeDtypeStruct((windows, H, length, length), BF),
            jax.ShapeDtypeStruct((windows * length, width), F32),
        ],
        compiler_params=pltpu.CompilerParams(vmem_limit_bytes=VMEM),
        cost_estimate=SHORT,
        name="attend",
    )(meta, qkv, qkv, qkv, bias)


def attend_back_kernel(meta_ref, q_ref, k_ref, v_ref, e_ref, r_ref, o_ref, do_ref, *refs, chunk):
    d_ref, ds_ref, line_ref, sum_ref = refs[-4:]
    length = q_ref.shape[0]
    blocks = length // 128
    w = pl.program_id(1)
    lane = lax.broadcasted_iota(jnp.int32, (length, 128), 1)
    zero = jnp.zeros((), BF)
    q, k, v = q_ref[...], k_ref[...], v_ref[...]
    up = do_ref[...].astype(F32) * r_ref[...]
    both = up * o_ref[...].astype(F32)
    up = up.astype(BF)
    up_t, q_t = up.T, q.T
    dq, dv_t, dk_t = None, [], []

    def block_of(n):
        return lax.rem(n + meta_ref[1] * (blocks // 2), blocks)

    @pl.when(w == 0)
    def _():
        line_ref[...] = jnp.zeros_like(line_ref)

    for h in range(2):
        mine = (lane < DH) if h == 0 else (lane >= DH)
        center = jnp.sum(jnp.where(mine, both, 0.0), 1, keepdims=True)
        dp = dot(up, jnp.where(mine, v, zero), 1, 1)
        for c in range(0, length, chunk):
            e = e_ref[0, h, c : c + chunk, :].astype(F32)
            ds = e * (dp[c : c + chunk] - center[c : c + chunk])
            ds_ref[0, h, c : c + chunk, :] = ds.astype(BF)
            rows = slice(c % 128, c % 128 + chunk)
            for n in range(blocks):
                d = blocks - 1 + block_of(n) - block_of(c // 128)
                line_ref[h, rows, pl.ds(pl.multiple_of(d * 128, 128), 128)] += ds[:, n * 128 : (n + 1) * 128]
        ds = ds_ref[0, h]
        part = dot(ds, jnp.where(mine, k, zero))
        dq = part if dq is None else dq + part
        dv_t.append(dot(up_t[h * DH : (h + 1) * DH], e_ref[0, h]))
        dk_t.append(dot(q_t[h * DH : (h + 1) * DH], ds))
    parts = (dq * DH**-0.5, jnp.concatenate(dk_t, 0).T * DH**-0.5, jnp.concatenate(dv_t, 0).T)
    for n, x in enumerate(parts):
        cols = slice(n * 128, (n + 1) * 128)
        x = x.astype(BF)
        d_ref[:, cols] = x
        sums = jnp.broadcast_to(column_sums(x.astype(F32)), (8, 128))
        sum_ref[:, cols] = jnp.where(w == 0, sums, sum_ref[:, cols] + sums)


def attend_back(meta, qkv, e, r, o, do, first, count, total, at, before=None):
    windows, _, length, _ = e.shape
    pairs = H // 2
    col = lambda off: pl.BlockSpec((length, 128), lambda h, w: (w, off + h))
    sq = pl.BlockSpec((1, 2, length, length), lambda h, w: (w, first + h, 0, 0))
    span = (2 * (length // 128) - 1) * 128
    more = [] if before is None else [before]
    return pl.pallas_call(
        partial(attend_back_kernel, chunk=64),
        grid=(count, windows),
        in_specs=[pl.BlockSpec(memory_space=pltpu.SMEM)]
        + [col(first), col(pairs + first), col(2 * pairs + first), sq, col(first), col(first), col(first)]
        + [pl.BlockSpec(memory_space=pl.ANY)] * len(more),
        out_specs=[
            pl.BlockSpec((length, 384), lambda h, w: (w, at + h)),
            pl.BlockSpec((1, 2, length, length), lambda h, w: (w, h, 0, 0)),
            pl.BlockSpec((2, 128, span), lambda h, w: (h, 0, 0)),
            pl.BlockSpec((8, 384), lambda h, w: (0, h)),
        ],
        out_shape=[
            jax.ShapeDtypeStruct((windows * length, total * 384), BF),
            jax.ShapeDtypeStruct((windows, 2 * count, length, length), BF),
            jax.ShapeDtypeStruct((2 * count, 128, span), F32),
            jax.ShapeDtypeStruct((8, count * 384), F32),
        ],
        input_output_aliases={8: 0} if more else {},
        compiler_params=pltpu.CompilerParams(vmem_limit_bytes=VMEM),
        cost_estimate=SHORT,
        name="attend_back",
    )(meta, qkv, qkv, qkv, e, r, o, do, *more)


def spread(refs, rows, stride):
    h = 0
    for ref in refs:
        for n in range(ref.shape[-3]):
            x = (ref[0, n] if len(ref.shape) == 4 else ref[n]).astype(F32)
            for c in range(x.shape[1] // 128):
                rows[c, h * stride : h * stride + x.shape[0], :] = x[:, c * 128 : (c + 1) * 128]
            h += 1


def heads_of(rows, i, stride):
    return [rows[c, pl.ds(i, 16, stride=stride), :].astype(BF) for c in range(rows.shape[0])]


def one_hot(index):
    width = index.shape[1]
    ids = lax.broadcasted_iota(jnp.int32, (NB, width), 0).astype(BF)
    hit = jnp.broadcast_to(index, (NB, width)).astype(BF) == ids
    return jnp.where(hit, jnp.ones((), BF), jnp.zeros((), BF))


def table_kernel(*refs, parts, with_line):
    ds_refs, refs = refs[:parts], refs[parts:]
    line_refs, refs = refs[: parts * with_line], refs[parts * with_line :]
    map_ref, out_ref, rows, maps = refs[0], refs[1], refs[-2], refs[-1]
    tile = map_ref.shape[2]
    step = pl.program_id(0)

    @pl.when(step == 0)
    def _():
        out_ref[...] = jnp.zeros_like(out_ref)
        rows[...] = jnp.zeros_like(rows)

    if with_line:
        line_out, line_rows = refs[2], refs[3]
        share = line_refs[0].shape[1]
        span = line_refs[0].shape[2]

        @pl.when(step == 0)
        def _():
            line_out[...] = jnp.zeros_like(line_out)
            line_rows[...] = jnp.zeros_like(line_rows)

        spread(line_refs, line_rows, share + 8)
        offset = lax.broadcasted_iota(jnp.int32, (8, span), 1) - (span - 128) // 2
        down = lax.broadcasted_iota(jnp.int32, (8, span), 0) + step * share
        lhs, rhs = [], []
        for i in range(share):
            if i % 8 == 0:
                index = bucket_of(offset - (down + i), 0).astype(F32)
            lhs += heads_of(line_rows, i, share + 8)
            rhs.append(one_hot(index[i % 8 : i % 8 + 1, :]))
        line_out[...] += dot(jnp.concatenate(lhs, 1), jnp.concatenate(rhs, 1), 1, 1)

    spread(ds_refs, rows, tile + 8)
    maps[...] = map_ref[0].astype(F32)
    lhs, rhs = [], []
    for i in range(tile):
        lhs += heads_of(rows, i, tile + 8)
        rhs.append(jnp.concatenate([one_hot(maps[t, i : i + 1, :]) for t in range(2)], 0))
    out_ref[...] += dot(jnp.concatenate(lhs, 1), jnp.concatenate(rhs, 1), 1, 1)


def table_grads(ds_parts, lines, maps, w, share_of=1, share=0):
    _, _, length, _ = maps.shape
    tile = 64
    parts = len(ds_parts)
    steps = length // tile // share_of
    at = share * steps
    outs, out_shapes = [pl.BlockSpec((16, 2 * NB), lambda i: (0, 0))], [jax.ShapeDtypeStruct((16, 2 * NB), F32)]
    line_specs, line_rows = [], []
    if lines:
        rows, span = 128 // steps, lines[0].shape[2]
        line_specs = [pl.BlockSpec((x.shape[0], rows, span), lambda i: (0, i, 0)) for x in lines]
        line_rows = [pltpu.VMEM((span // 128, 16 * (rows + 8), 128), F32)]
        outs.append(pl.BlockSpec((16, NB), lambda i: (0, 0)))
        out_shapes.append(jax.ShapeDtypeStruct((16, NB), F32))
    return pl.pallas_call(
        partial(table_kernel, parts=parts, with_line=bool(lines)),
        grid=(steps,),
        in_specs=[pl.BlockSpec((1, x.shape[1], tile, length), lambda i: (w, 0, at + i, 0)) for x in ds_parts]
        + line_specs
        + [pl.BlockSpec((1, 2, tile, length), lambda i: (w, 0, at + i, 0))],
        out_specs=outs,
        out_shape=out_shapes,
        scratch_shapes=line_rows
        + [pltpu.VMEM((length // 128, 16 * (tile + 8), 128), F32), pltpu.VMEM((2, tile, length), F32)],
        compiler_params=pltpu.CompilerParams(vmem_limit_bytes=VMEM),
        cost_estimate=SHORT,
        name="table_grads",
    )(*ds_parts, *lines, maps)


def gelu_both(x):
    cdf = 0.5 + 0.5 * lax.erf(x * 0.7071067811865476)
    density = jnp.exp2((-0.5 * LOG2E) * (x * x)) * 0.3989422804014327
    return x * cdf, cdf + x * density


def norm_forward(summed, params):
    centered = summed - jnp.mean(summed, -1, keepdims=True)
    inverse = lax.rsqrt(jnp.mean(centered * centered, -1, keepdims=True) + EPS)
    normed = centered * inverse
    return normed * params[0:1] + params[1:2], normed, inverse


def norm_backward(upstream, normed, inverse, params):
    scaled = upstream * params[0:1]
    return inverse * (
        scaled - jnp.mean(scaled, -1, keepdims=True) - normed * jnp.mean(scaled * normed, -1, keepdims=True)
    )


def column_sums(x):
    return jnp.sum(x, 0, keepdims=True)


def tokens_of(own_ref, other_ref, chunk):
    windows, local, _ = other_ref.shape
    step = min(chunk, local)
    for w in range(windows):
        for n, ref in enumerate((own_ref, other_ref)):
            for c in range(0, local, step):
                yield slice((2 * w + n) * local + c, (2 * w + n) * local + c + step), ref[w, c : c + step, :]


def front_kernel(meta_ref, own_ref, other_ref, f_ref, box_ref, w_ref, qv_ref, low_ref, out_ref):
    step = pl.program_id(0)
    third = pl.num_programs(0) // 3

    @pl.when(step == 0)
    def _():
        for cs, x in tokens_of(own_ref, other_ref, 256):
            low_ref[cs, :] = (x.astype(F32) + dot(f_ref[cs, :], box_ref[...])).astype(BF)

    wide = out_ref.shape[1]
    cols = pl.ds(pl.multiple_of(lax.rem(step, third) * wide, wide), wide)
    shift = jnp.where(step < third, qv_ref[0:1, cols], jnp.where(step < 2 * third, 0.0, qv_ref[1:2, cols]))
    out_ref[...] = (dot(low_ref[...], w_ref[...]) + shift).astype(BF)


def front(meta, own, other, features, box_weight, qkv_weight, qv_bias):
    windows, local, width = other.shape
    tokens = 2 * windows * local
    cols = qkv_weight.shape[1]
    whole = lambda x: pl.BlockSpec(x.shape, lambda n, p: (0,) * len(x.shape))
    return pl.pallas_call(
        front_kernel,
        grid_spec=pltpu.PrefetchScalarGridSpec(
            num_scalar_prefetch=1,
            grid=(cols // width,),
            in_specs=[
                pl.BlockSpec(other.shape, lambda n, p: (p[1], 0, 0)),
                whole(other),
                whole(features),
                whole(box_weight),
                pl.BlockSpec((width, width), lambda n, p: (0, n)),
                whole(qv_bias),
            ],
            out_specs=[
                pl.BlockSpec((tokens, width), lambda n, p: (0, 0)),
                pl.BlockSpec((tokens, width), lambda n, p: (0, n)),
            ],
        ),
        out_shape=[jax.ShapeDtypeStruct((tokens, width), BF), jax.ShapeDtypeStruct((tokens, cols), BF)],
        compiler_params=pltpu.CompilerParams(vmem_limit_bytes=VMEM),
        cost_estimate=SHORT,
        name="front",
    )(meta, own, other, features, box_weight, qkv_weight, qv_bias)


def feed_kernel(meta_ref, own_ref, other_ref, f_ref, box_ref, att_ref, wo_ref, bo_ref, n1_ref, w1_ref, b1_ref, w2_ref, b2_ref, n2_ref, cot_own_ref, cot_other_ref, z_ref, low_ref, act_ref, slope_ref, out_own_ref, out_other_ref, dlow_ref, sum_ref, acc, *, chunk):
    step = pl.program_id(0)
    tokens = low_ref.shape[0]

    @pl.when(step == 0)
    def _():
        for cs, x in tokens_of(own_ref, other_ref, chunk):
            entry = x.astype(F32) + dot(f_ref[cs, :], box_ref[...])
            z = entry + (dot(att_ref[cs, :], wo_ref[...]) + bo_ref[...])
            second = norm_forward(z, n1_ref[...])[0]
            z_ref[cs, :] = z.astype(BF)
            low_ref[cs, :] = second.astype(BF)
            acc[cs, :] = second

    for c in range(0, tokens, chunk):
        cs = slice(c, c + chunk)
        active, slope = gelu_both(dot(low_ref[cs, :], w1_ref[...]) + b1_ref[...])
        active = active.astype(BF)
        act_ref[cs, :] = active
        slope_ref[cs, :] = slope.astype(BF)
        acc[cs, :] += dot(active, w2_ref[...])

    @pl.when(step == pl.num_programs(0) - 1)
    def _():
        sums = [0.0, 0.0, 0.0]
        local = cot_other_ref.shape[1]
        for cs, x in tokens_of(cot_own_ref, cot_other_ref, 128):
            result, normed, inverse = norm_forward(acc[cs, :] + b2_ref[...], n2_ref[...])
            place = cs.start % local
            out = (out_own_ref, out_other_ref)[cs.start // local % 2]
            out[cs.start // local // 2, place : place + 128, :] = result.astype(BF)
            up = x.astype(F32)
            low = norm_backward(up, normed, inverse, n2_ref[...]).astype(BF)
            dlow_ref[cs, :] = low
            sums = [sums[0] + column_sums(up * normed), sums[1] + column_sums(up), sums[2] + column_sums(low.astype(F32))]
        sum_ref[...] = jnp.concatenate(sums + [jnp.zeros((5, sums[0].shape[1]), F32)], 0)


def feed(meta, own, other, features, box_weight, attended, out_weight, out_bias, norm_one, w1, b1, w2, b2, norm_two, cot_own, cot_other):
    tokens, width = attended.shape
    inner = w1.shape[1]
    tile = 1024
    whole = lambda shape: pl.BlockSpec(shape, lambda n, p: (0,) * len(shape))
    mine = pl.BlockSpec(other.shape, lambda n, p: (p[1], 0, 0))
    full = whole((tokens, width))
    part = pl.BlockSpec((tokens, tile), lambda n, p: (0, n))
    return pl.pallas_call(
        partial(feed_kernel, chunk=512),
        grid_spec=pltpu.PrefetchScalarGridSpec(
            num_scalar_prefetch=1,
            grid=(inner // tile,),
            in_specs=[
                mine,
                whole(other.shape),
                whole(features.shape),
                whole(box_weight.shape),
                full,
                whole(out_weight.shape),
                whole((1, width)),
                whole((2, width)),
                pl.BlockSpec((width, tile), lambda n, p: (0, n)),
                pl.BlockSpec((1, tile), lambda n, p: (0, n)),
                pl.BlockSpec((tile, width), lambda n, p: (n, 0)),
                whole((1, width)),
                whole((2, width)),
                mine,
                whole(other.shape),
            ],
            out_specs=[full, full, part, part, whole(other.shape), whole(other.shape), full, whole((8, width))],
            scratch_shapes=[pltpu.VMEM((tokens, width), F32)],
        ),
        out_shape=[
            jax.ShapeDtypeStruct((tokens, width), BF),
            jax.ShapeDtypeStruct((tokens, width), BF),
            jax.ShapeDtypeStruct((tokens, inner), BF),
            jax.ShapeDtypeStruct((tokens, inner), BF),
            jax.ShapeDtypeStruct(other.shape, BF),
            jax.ShapeDtypeStruct(other.shape, BF),
            jax.ShapeDtypeStruct((tokens, width), BF),
            jax.ShapeDtypeStruct((8, width), F32),
        ],
        compiler_params=pltpu.CompilerParams(vmem_limit_bytes=VMEM),
        cost_estimate=SHORT,
        name="feed",
    )(
        meta, own, other, features, box_weight, attended, out_weight, out_bias.reshape(1, -1), norm_one,
        w1, b1.reshape(1, -1), w2, b2.reshape(1, -1), norm_two, cot_own, cot_other,
    )


def feed_back_kernel(dlow_ref, w1_ref, w2_ref, slope_ref, z_ref, n1_ref, wo_ref, din_ref, bias_ref, dbr_ref, datt_ref, sum_ref, acc, *, chunk):
    step = pl.program_id(0)
    tokens = dlow_ref.shape[0]

    @pl.when(step == 0)
    def _():
        acc[...] = dlow_ref[...].astype(F32)

    sums = 0.0
    for c in range(0, tokens, chunk):
        cs = slice(c, c + chunk)
        d_inner = (dot(dlow_ref[cs, :], w2_ref[...], 1, 1) * slope_ref[cs, :].astype(F32)).astype(BF)
        din_ref[cs, :] = d_inner
        sums = sums + column_sums(d_inner.astype(F32))
        acc[cs, :] += dot(d_inner, w1_ref[...], 1, 1)
    bias_ref[...] = jnp.concatenate([sums, jnp.zeros((7, sums.shape[1]), F32)], 0)

    @pl.when(step == pl.num_programs(0) - 1)
    def _():
        totals = [0.0, 0.0, 0.0]
        for c in range(0, tokens, 128):
            cs = slice(c, c + 128)
            _, normed, inverse = norm_forward(z_ref[cs, :].astype(F32), n1_ref[...])
            up = acc[cs, :]
            low = norm_backward(up, normed, inverse, n1_ref[...]).astype(BF)
            dbr_ref[cs, :] = low
            totals = [
                totals[0] + column_sums(up * normed),
                totals[1] + column_sums(up),
                totals[2] + column_sums(low.astype(F32)),
            ]
        sum_ref[...] = jnp.concatenate(totals + [jnp.zeros((5, totals[0].shape[1]), F32)], 0)
        datt_ref[...] = dot(dbr_ref[...], wo_ref[...], 1, 1).astype(BF)


def feed_back(d_outer, w1, w2, slope, z_one, norm_one, out_weight):
    tokens, width = z_one.shape
    inner = w1.shape[1]
    tile = 1024
    whole = lambda shape: pl.BlockSpec(shape, lambda n: (0, 0))
    full = whole((tokens, width))
    return pl.pallas_call(
        partial(feed_back_kernel, chunk=512),
        grid=(inner // tile,),
        in_specs=[
            full,
            pl.BlockSpec((width, tile), lambda n: (0, n)),
            pl.BlockSpec((tile, width), lambda n: (n, 0)),
            pl.BlockSpec((tokens, tile), lambda n: (0, n)),
            full,
            whole((2, width)),
            whole((width, width)),
        ],
        out_specs=[
            pl.BlockSpec((tokens, tile), lambda n: (0, n)),
            pl.BlockSpec((8, tile), lambda n: (0, n)),
            full,
            full,
            whole((8, width)),
        ],
        out_shape=[
            jax.ShapeDtypeStruct((tokens, inner), BF),
            jax.ShapeDtypeStruct((8, inner), F32),
            jax.ShapeDtypeStruct((tokens, width), BF),
            jax.ShapeDtypeStruct((tokens, width), BF),
            jax.ShapeDtypeStruct((8, width), F32),
        ],
        scratch_shapes=[pltpu.VMEM((tokens, width), F32)],
        compiler_params=pltpu.CompilerParams(vmem_limit_bytes=VMEM),
        cost_estimate=SHORT,
        name="feed_back",
    )(d_outer, w1, w2, slope, z_one, norm_one, out_weight)


UNIT = 384
PIECES = 2


def halves(full, place_ref):
    rows = full.shape[0] // 2
    upper = place_ref[1] == 0
    low, high = full[:rows], full[rows:]
    return jnp.where(upper, high, low).astype(BF), jnp.where(upper, low, high).astype(BF)


def wide_grads_kernel(place_ref, *refs, counts):
    step = pl.program_id(0)
    pairs = len(counts)
    outs = refs[3 * pairs :]
    at = 0
    for n, count in enumerate(counts):

        @pl.when((step >= at) & (step < at + count))
        def _():
            full = dot(refs[3 * n][...], jnp.concatenate([refs[3 * n + 1][...], refs[3 * n + 2][...]], 1), 0, 0)
            both = halves(full, place_ref)
            for m, x in enumerate(both):
                side = x.shape[0] // 2
                for k in range(2):
                    outs[2 * m + k][...] = x[k * side : (k + 1) * side, :UNIT].reshape(outs[2 * m + k].shape)
                outs[4 + m][...] = x[:, UNIT:].reshape(outs[4 + m].shape)

        at += count


def wide_grads(place, pairs):
    tokens, rows = pairs[0][0].shape
    counts = [right.shape[1] // (2 * UNIT) for _, right in pairs]
    specs, at = [], 0
    for (left, right), count in zip(pairs, counts):

        def block(i, p, send, at=at, count=count):
            owner = 1 - p[0] if send else p[0]
            return (0, owner * count + jnp.clip(i - at, 0, count - 1))

        specs += [
            pl.BlockSpec(left.shape, lambda i, p: (0, 0)),
            pl.BlockSpec((tokens, UNIT), partial(block, send=True)),
            pl.BlockSpec((tokens, UNIT), partial(block, send=False)),
        ]
        at += count
    piece = pl.BlockSpec((1, 1, rows // 4, UNIT), lambda i, p: (0, i, 0, 0))
    out = pl.BlockSpec((2, 1, rows // 4, UNIT), lambda i, p: (0, i, 0, 0))
    outs = pl.pallas_call(
        partial(wide_grads_kernel, counts=counts),
        grid_spec=pltpu.PrefetchScalarGridSpec(
            num_scalar_prefetch=1,
            grid=(at,),
            in_specs=specs,
            out_specs=[piece] * 4 + [out] * 2,
        ),
        out_shape=[jax.ShapeDtypeStruct((n, at, rows // 4, UNIT), BF) for n in (1, 1, 1, 1, 2, 2)],
        compiler_params=pltpu.CompilerParams(vmem_limit_bytes=VMEM),
        cost_estimate=SHORT,
        name="wide_grads",
    )(place, *[x for left, right in pairs for x in (left, right, right)])
    return [x.reshape(-1, UNIT) for x in outs]


def long_grads_kernel(place_ref, left_ref, send_ref, keep_ref, *outs):
    full = dot(left_ref[...], jnp.concatenate([send_ref[...], keep_ref[...]], 1), 0, 0).astype(BF)
    for n in range(4):

        @pl.when(pl.program_id(0) == n)
        def _():
            outs[n][...] = full[:, :UNIT]
            outs[4 + n // 2][...] = full[:, UNIT:]


def long_grads(place, left, right):
    tokens, rows = left.shape
    tile = rows // 4

    def quarter(i, p):
        owner = jnp.where(i < 2, 1 - p[1], p[1])
        return (0, owner * 2 + lax.rem(i, 2))

    piece = pl.BlockSpec((tile, UNIT), lambda i, p: (0, 0))
    other = pl.BlockSpec((tile, UNIT), lambda i, p: (jnp.minimum(i, 1), 0))
    own = pl.BlockSpec((tile, UNIT), lambda i, p: (jnp.maximum(i - 2, 0), 0))
    return pl.pallas_call(
        long_grads_kernel,
        grid_spec=pltpu.PrefetchScalarGridSpec(
            num_scalar_prefetch=1,
            grid=(4,),
            in_specs=[
                pl.BlockSpec((tokens, tile), quarter),
                pl.BlockSpec((tokens, UNIT), lambda i, p: (0, 1 - p[0])),
                pl.BlockSpec((tokens, UNIT), lambda i, p: (0, p[0])),
            ],
            out_specs=[piece] * 4 + [other, own],
        ),
        out_shape=[jax.ShapeDtypeStruct((n * tile, UNIT), BF) for n in (1, 1, 1, 1, 2, 2)],
        compiler_params=pltpu.CompilerParams(vmem_limit_bytes=VMEM),
        cost_estimate=SHORT,
        name="long_grads",
    )(place, left, right, right)


E_ROWS = 16


def last_kernel(place_ref, x_ref, dx_ref, f_ref, own_ref, other_ref, two_ref, one_ref, in_ref, *refs):
    qv_refs, line_ref, small_refs, outs = refs[:3], refs[3], refs[4:-4], refs[-4:]
    mine = place_ref[0] == 0
    upper = place_ref[1] == 0
    width = x_ref.shape[1]
    middle = width // 2
    x = dot(x_ref[...], dx_ref[...], 0, 0).astype(BF)
    entry = jnp.concatenate([ref[w] for w in range(own_ref.shape[0]) for ref in (own_ref, other_ref)], 0)
    box = dot(f_ref[...], entry, 0, 0).astype(BF)
    small = small_refs[0][...]
    for ref in small_refs[1:]:
        small = small + ref[...]
    tables = jnp.concatenate([line_ref[...], small, jnp.zeros((16, NB), F32)], 1).T
    blocks = [ref[0:1, p : p + UNIT] for ref in qv_refs for p in range(0, ref.shape[1], UNIT)]
    qv = [jnp.concatenate([y[:, at : at + 128] for y in blocks], 1) for at in (0, 256)]
    halves_of = []
    for n in range(2):
        cols = slice(n * middle, (n + 1) * middle)
        inner = in_ref[0:1, n * 2 * width : (n + 1) * 2 * width]
        sums = [
            two_ref[n : n + 1, :],
            one_ref[n : n + 1, :],
            qv[n],
            jnp.concatenate([one_ref[2:3, cols], two_ref[2:3, cols]], 1),
            inner[:, :width],
            inner[:, width:],
            jnp.zeros((E_ROWS - 6, width), F32),
        ]
        share = [tables[m * NB + n * NB // 2 : m * NB + (n + 1) * NB // 2, :] for m in range(3)]
        share = [jnp.pad(t, ((0, 0), (0, 128 - t.shape[1]))) for t in share]
        sides = [jnp.concatenate(sums, 0), jnp.concatenate(share + [jnp.zeros((E_ROWS, width - 3 * 128), F32)], 1)]
        q, h = x.shape[0] // 4, box.shape[0] // 4
        halves_of.append(
            jnp.concatenate(
                [
                    y
                    for m in range(2)
                    for y in (
                        x[(2 * n + m) * q : (2 * n + m + 1) * q],
                        box[(2 * n + m) * h : (2 * n + m + 1) * h],
                        sides[m].astype(BF),
                    )
                ],
                0,
            )
        )
    for m in range(2):
        rows = jnp.where(upper, halves_of[1 - m], halves_of[m])
        outs[m][...] = jnp.where(mine, rows[:, middle:], rows[:, :middle])
        outs[2 + m][...] = jnp.where(mine, rows[:, :middle], rows[:, middle:])


def last_grads(place, x, dx, f, own, other, *sums):
    rows = (x.shape[1] + f.shape[1]) // 4 + E_ROWS
    vmem = pl.BlockSpec(memory_space=pltpu.VMEM)
    return pl.pallas_call(
        last_kernel,
        in_specs=[pl.BlockSpec(memory_space=pltpu.SMEM)] + [vmem] * (5 + len(sums)),
        out_specs=[vmem] * 4,
        out_shape=[jax.ShapeDtypeStruct((2 * rows, UNIT), BF)] * 4,
        compiler_params=pltpu.CompilerParams(vmem_limit_bytes=VMEM),
        cost_estimate=SHORT,
        name="last_grads",
    )(place, x, dx, f, own, other, *sums)


def lay_kernel(place_ref, *refs, kind, rows):
    last = refs[4:8] if kind == "heads" else refs[:4]
    pieces, outs = refs[:4], refs[8 if kind == "heads" else 4 :]
    core, step = place_ref[0], pl.program_id(0)

    def lay_piece(ref, owner):
        blocks = ref.shape[0] // rows
        for n in range(blocks):
            x = ref[n * rows : (n + 1) * rows, :].astype(F32)
            if kind == "long":
                outs[0][n * rows : (n + 1) * rows, owner * UNIT : (owner + 1) * UNIT] = x
            elif kind == "wide":
                at = (owner * blocks + n) * UNIT
                outs[0][:, at : at + UNIT] = x
            elif n == 0:
                outs[0][:, owner * UNIT : (owner + 1) * UNIT] = x
            else:
                lay_pair(x, owner * 2 + n - 1)

    def lay_last(ref, owner):
        lay_pair(ref[:rows, :].astype(F32), 4 + owner)
        box = BOXF // 4
        cols = slice(owner * UNIT, (owner + 1) * UNIT)
        outs[2][:, cols] = ref[rows : rows + box, :].astype(F32)
        small = ref[rows + box : rows + box + E_ROWS, :].astype(F32)

        @pl.when(step == 0)
        def _():
            for n in range(3):
                outs[3 + n][:, cols] = small[n : n + 1]
            outs[6 + owner][...] = small[3]
            for n in range(2):
                at = n * 2 * UNIT + owner * UNIT
                outs[8][at : at + UNIT] = small[4 + n]

        if owner == 0:

            @pl.when(step == 1)
            def _():
                outs[9][...] = jnp.concatenate([small[:, n * 128 : n * 128 + H] for n in range(3)], 1)

    def lay_pair(x, pair):
        for m in range(3):
            at = (m * (H // 2) + pair) * 128
            outs[1][:, at : at + 128] = x[:, m * 128 : (m + 1) * 128]

    def choose(refs, side, lay_one):
        for other_side in range(2):
            for owner in range(2):
                for other_core in range(2):

                    @pl.when(((step == side) == (other_side == 0)) & (core == (owner ^ other_core)))
                    def _():
                        lay_one(refs[2 * other_side + other_core], owner)

    choose(pieces, place_ref[2], lay_piece)
    if kind == "heads":
        choose(last, place_ref[3], lay_last)


def lay(place, pieces, kind, rows):
    blocks = pieces[0].shape[0] // rows
    whole = None
    if kind == "long":
        shapes = [(2 * blocks * rows, 2 * UNIT)]
    elif kind == "wide":
        shapes = [(2 * rows, 2 * blocks * UNIT)]
    else:
        width = 2 * UNIT
        shapes = [(2 * rows, width), (2 * rows, 3 * width), (BOXF // 2, width)]
        whole = [(1, width)] * 3 + [(UNIT,)] * 2 + [(2 * width,), (NB // 2, 3 * H)]
    return pl.pallas_call(
        partial(lay_kernel, kind=kind, rows=rows),
        grid=(2,),
        in_specs=[pl.BlockSpec(memory_space=pltpu.SMEM)] + [pl.BlockSpec(x.shape, lambda i: (0, 0)) for x in pieces],
        out_specs=[pl.BlockSpec((m // 2, n), lambda i: (i, 0)) for m, n in shapes]
        + [pl.BlockSpec(shape, lambda i, n=len(shape): (0,) * n) for shape in whole or []],
        out_shape=[jax.ShapeDtypeStruct(shape, F32) for shape in shapes + (whole or [])],
        compiler_params=pltpu.CompilerParams(vmem_limit_bytes=VMEM),
        cost_estimate=SHORT,
        name="lay",
    )(place, *pieces)


def entry_kernel(a_ref, b_ref, w_ref, sum_ref, own_ref, other_ref):
    pairs = H // 2
    weight = jnp.concatenate([w_ref[:, (m * pairs + n) * 128 : (m * pairs + n + 1) * 128] for n in range(pairs) for m in range(3)], 1)
    both = jnp.concatenate([a_ref[...], b_ref[...]], 1)
    out = (sum_ref[...].astype(F32) + dot(both, weight, 1, 1)).astype(BF)
    local = own_ref.shape[1]
    own_ref[0] = out[:local]
    other_ref[0] = out[local:]


def entry_grad(first, last, weight, base, windows):
    tokens, width = base.shape
    tile = tokens // windows
    row = lambda x: pl.BlockSpec((tile, x.shape[1]), lambda i: (i, 0))
    out = pl.BlockSpec((1, tile // 2, width), lambda i: (i, 0, 0))
    return pl.pallas_call(
        entry_kernel,
        grid=(windows,),
        in_specs=[row(first), row(last), pl.BlockSpec(weight.shape, lambda i: (0, 0)), row(base)],
        out_specs=[out, out],
        out_shape=[jax.ShapeDtypeStruct((windows, tile // 2, width), BF)] * 2,
        compiler_params=pltpu.CompilerParams(vmem_limit_bytes=VMEM),
        cost_estimate=SHORT,
        name="entry_grad",
    )(first, last, weight, base)


def shards(
    docs,
    hidden_in,
    boxes,
    lengths,
    box_weight,
    qkv_weight,
    qv_bias,
    out_weight,
    out_bias,
    rel_tables,
    norm_one,
    ffn_in_weight,
    ffn_in_bias,
    ffn_out_weight,
    ffn_out_bias,
    norm_two,
    cotangent,
):
    half = lax.axis_index("half")
    doc = lax.axis_index("doc")
    core, side = doc & 1, (doc >> 1) & 1
    own, local_len, width = hidden_in.shape
    windows = own // 2
    length = 2 * local_len
    tokens = windows * length

    def swap_half(x):
        return lax.ppermute(x, "half", [(0, 1), (1, 0)])

    def swap_doc(x, bit):
        return lax.ppermute(x, "doc", [(i, i ^ (1 << bit)) for i in range(docs)])

    def part(x, index, axis):
        if isinstance(x, list):
            return jnp.where(index == 0, *x)
        size = x.shape[axis] // 2
        return lax.dynamic_slice_in_dim(x, index * size, size, axis)

    def ordered(index, mine, other, axis):
        return jnp.where(index == 0, jnp.concatenate([mine, other], axis), jnp.concatenate([other, mine], axis))

    def tie(x, *others):
        return lax.optimization_barrier((x,) + others)[0]

    meta = jnp.concatenate([jnp.stack([core, half, side, (doc >> 2) & 1]).astype(jnp.int32), lengths])
    box_other = swap_half(part(boxes, 1 - half, 1))
    hidden_other = swap_half(part(tie(hidden_in, box_other), 1 - half, 0))
    bias, maps, features = score_bias(meta, boxes, box_other, rel_tables)
    cot_other = swap_half(part(tie(cotangent, maps), 1 - half, 0))
    entry_low, qkv = front(meta, hidden_in, hidden_other, features, box_weight, qkv_weight, qv_bias)
    attended, e, r = attend(meta, qkv, bias)
    z_one, second_low, active, slope, out_mine, out_send, d_outer, sums_two = feed(
        meta,
        hidden_in,
        hidden_other,
        features,
        box_weight,
        attended,
        out_weight,
        out_bias,
        norm_one,
        ffn_in_weight,
        ffn_in_bias,
        ffn_out_weight,
        ffn_out_bias,
        norm_two,
        cotangent,
        cot_other,
    )

    pairs, early = H // 2, H // 3
    late_pairs = pairs - early
    step = early // 2
    more = list(range(2, docs.bit_length() - 1))
    place = meta
    last = [None]

    def now(x):
        return x if last[0] is None else tie(x, *last[0])

    def then(x, *more):
        last[0] = (x,) + more
        return x

    def joined(pieces):
        return jnp.concatenate(pieces, 0) if len(pieces) > 1 else pieces[0]

    def total(*xs):
        out = xs[0].astype(F32)
        for x in xs[1:]:
            out = out + x.astype(F32)
        return out.astype(BF)

    class Chain:
        def core(self, *parts):
            pieces, keep, keep_own = parts[:-2], parts[-2], parts[-1]
            count = len(pieces) // 2
            then(keep_own)
            pieces = [swap_doc(x, 0) for x in pieces]
            self.own = [keep, pieces[:count], keep_own, pieces[count:]]

        def half_later(self):
            keep, come, keep_own, come_own = self.own
            send = then(total(now(keep), joined(come)))
            self.own = [keep_own, come_own, swap_half(send)]

        def add_own(self):
            keep_own, come_own, come = self.own
            self.own = [then(total(now(keep_own), joined(come_own))), come]

        def half(self):
            keep, come, keep_own, come_own = self.own
            keep, keep_own = lax.optimization_barrier((keep, keep_own) + last[0])[:2]
            send, own = total(keep, joined(come)), total(keep_own, joined(come_own))
            then(send, own)
            self.own = [own, swap_half(send)]

        def split(self, bit):
            b = (doc >> bit) & 1
            own = [now(self.own[0])] + self.own[1:]
            send = then(total(*[part(x, 1 - b, 0) for x in own]))
            keep = total(*[part(x, b, 0) for x in own])
            self.own = [keep, swap_doc(send, bit)]

        def double(self, bits):
            x = then(total(now(self.own[0]), *self.own[1:]))
            for bit in bits[:-1]:
                x = total(x, swap_doc(x, bit))
            self.own = [x, swap_doc(x, bits[-1])]

        def back(self, bit):
            x = then(total(now(self.own[0]), *self.own[1:]))
            self.parted, self.own = bit, [x, swap_doc(x, bit)]

        def gather(self, bit=1):
            if hasattr(self, "parted"):
                x = then(ordered((doc >> self.parted) & 1, now(self.own[0]), self.own[1], 0))
            else:
                x = then(total(now(self.own[0]), *self.own[1:]))
            self.mine, self.across = x, swap_doc(x, bit)
            self.beside = swap_doc(x, 0)

        def settle(self, *others):
            then(*last[0], self.beside, *others)

        def pieces(self):
            return [now(self.mine), self.beside, self.across, swap_doc(now(self.across), 0)]

    def back(first, count, total_pairs, at, before):
        out = attend_back(meta, qkv, e, r, attended, now(d_attended), first, count, total_pairs, at, before)
        then(out[0])
        return out

    a, b, c, d = Chain(), Chain(), Chain(), Chain()
    block_rows = width // 4
    then(d_outer)
    a.core(*long_grads(place, active, now(d_outer)))
    a.half_later()
    d_inner, sums_in, d_branch, d_attended, sums_one = feed_back(
        now(d_outer), ffn_in_weight, ffn_out_weight, slope, z_one, norm_one, out_weight
    )
    then(d_branch)
    a.add_own()
    b.core(*wide_grads(place, [(second_low, now(d_inner))]))
    a.split(1)
    b.half()
    first_right, ds_0, line_0, qv_0 = back(0, step, early, 0, None)
    a.split(more[0])
    first_right, ds_1, line_1, qv_1 = back(step, early - step, early, step, first_right)
    a.double(more[1:])
    c.core(*wide_grads(place, [(attended, d_branch), (entry_low, now(first_right))]))
    b.split(1)
    c.half()
    last_right, ds_2, line_2, qv_2 = back(early, late_pairs, late_pairs, 0, None)
    a.back(more[0])
    b.split(more[0])
    small_0, line_grad = table_grads([ds_0, ds_1, now(ds_2)], [line_0, line_1, line_2], maps, 0)
    then(small_0)
    b.double(more[1:])
    c.split(1)
    a.gather()
    grad_mine, grad_send = entry_grad(first_right, now(last_right), qkv_weight, d_branch, windows)
    then(grad_send)
    a.settle()
    c.split(more[0])
    b.back(more[0])
    grad_other = swap_half(grad_send)
    smalls = [small_0, then(table_grads([ds_0, ds_1, now(ds_2)], [], maps, 1, 2, 0)[0])]
    c.double(more[1:])
    smalls.append(then(table_grads([ds_0, ds_1, now(ds_2)], [], maps, 1, 2, 1)[0]))
    for w in range(2, windows):
        smalls.append(then(table_grads([ds_0, ds_1, now(ds_2)], [], maps, w)[0]))
    b.gather()
    then(*last[0], grad_other, a.across)
    d.core(
        *last_grads(
            place, entry_low, last_right, features, now(grad_mine), grad_send, sums_two, sums_one, sums_in, qv_0, qv_1, qv_2, line_grad, *smalls
        )
    )
    c.back(more[0])
    d.half()
    (ffn_out_grad,) = lay(place, a.pieces(), "long", block_rows)
    then(ffn_out_grad)
    hidden_grad = then(ordered(half, now(grad_mine), grad_other, 0))
    d.split(more[0])
    out_other = swap_half(now(out_send))
    c.gather()
    b.settle()
    d.double(more[1:])
    (ffn_in_grad,) = lay(place, b.pieces(), "wide", block_rows)
    then(ffn_in_grad)
    d.double([1])
    c.settle()
    c_pieces = c.pieces()
    d.gather(more[0])
    out_grad, qkv_grad, box, two, one, qv, out_sum, ffn_out_sum, ffn_in_sum, table = lay(
        place, c_pieces + d.pieces(), "heads", block_rows
    )
    layer_out = ordered(half, now(out_mine), out_other, 0)
    return (
        layer_out,
        hidden_grad,
        box,
        qkv_grad,
        qv,
        out_grad,
        out_sum,
        table,
        one,
        ffn_in_grad,
        ffn_in_sum,
        ffn_out_grad,
        ffn_out_sum,
        two,
    )


def solution(mesh):
    rep = P()
    rows = P("half", None)
    return jax.shard_map(
        partial(shards, mesh.shape["doc"]),
        mesh=mesh,
        in_specs=(P("doc", "half", None), P(None, "doc", "half"), P("doc")) + (rep,) * 12 + (P("doc", "half", None),),
        out_specs=(
            P("doc", "half", None),
            P("doc", "half", None),
            rows,
            rows,
            rows,
            rows,
            P("half"),
            rows,
            rows,
            rows,
            P("half"),
            rows,
            P("half"),
            rows,
        ),
        check_vma=False,
    )
```

```python
from functools import partial

import jax
import jax.numpy as jnp
import numpy as np
from jax import lax
from jax.experimental import pallas as pl
from jax.experimental.pallas import tpu as pltpu
from jax.sharding import PartitionSpec as P

H = 12
DH = 64
BOXF = 128
NB = 32
EPS = 1e-05
LOG2E = 1.4426950408889634
BF = jnp.bfloat16
F32 = jnp.float32
VMEM = 56 << 20
LESS = 28 << 20
SHORT = pl.CostEstimate(flops=1, bytes_accessed=1, transcendentals=0)


def dot(a, b, ca=1, cb=0):
    return lax.dot_general(a, b, (((ca,), (cb,)), ((), ())), preferred_element_type=F32)


ROUND = 1.5 * 2.0**23 * 2.0**-8
SMALL = 1.6e-4


def unpack(both):
    first = (both + ROUND) - ROUND
    return first, (both - first) * (1.0 / SMALL)


def bucket_of(offset, shift):
    magnitude = jnp.abs(offset)
    if shift:
        magnitude = magnitude >> shift
    count = jnp.minimum(magnitude, 8)
    for n, bound in enumerate((12, 16, 24, 32, 48, 64, 96)):
        count = jnp.where(magnitude >= bound, 9 + n, count)
    return jnp.where(offset > 0, count + 16, count)


def look_up(table, index):
    dims = lax.GatherDimensionNumbers(
        offset_dims=(),
        collapsed_slice_dims=(1,),
        start_index_map=(1,),
        operand_batching_dims=(0,),
        start_indices_batching_dims=(0,),
    )
    return lax.gather(
        table, index[..., None], dims, slice_sizes=(1, 1), mode=lax.GatherScatterMode.PROMISE_IN_BOUNDS
    )


def sine(angle, quarter):
    n = jnp.round(angle * 0.6366197723675814)
    x = ((angle - n * 1.5703125) - n * 4.837512969970703125e-4) - n * 7.549789954891882e-8
    turn = n.astype(jnp.int32) + quarter
    y = x * x
    odd = x + x * y * (-1.6666654611e-1 + y * (8.3321608736e-3 + y * -1.9515295891e-4))
    even = 1.0 - 0.5 * y + y * y * (4.166664568298827e-2 + y * (-1.388731625493765e-3 + y * 2.443315711809948e-5))
    value = jnp.where((turn & 1) == 0, odd, even)
    return jnp.where((turn & 2) == 0, value, -value)


def window_length(meta_ref, w, windows):
    return meta_ref[4 + meta_ref[1] * windows + w]


def position(index, half, length):
    shifted = index + half * (length // 2)
    return jnp.where(shifted >= length, shifted - length, shifted)


def bias_kernel(meta_ref, own_ref, other_ref, rel_ref, freq_ref, out_ref, map_ref, feat_ref, line, maps, tabs, cols, *, rows):
    length = out_ref.shape[3]
    windows = other_ref.shape[1]
    blocks = length // 128
    span = (2 * blocks - 1) * 128
    w = pl.program_id(0)
    it = pl.program_id(1)
    half = meta_ref[1]

    def box_row(m):
        return jnp.concatenate([own_ref[m, pl.ds(half * windows + w, 1), :], other_ref[m, pl.ds(w, 1), :]], 1)

    @pl.when((w == 0) & (it == 0))
    def _():
        cols[...] = jnp.zeros_like(cols)
        cols[0:NB, 0 : 3 * H] = rel_ref[...] * LOG2E
        t = cols[0:128, :].T
        for kind in range(3):
            for hp in range(H // 2):
                n = kind * H + 2 * hp
                first = (t[n : n + 1, :] + ROUND) - ROUND
                tabs[3 * hp + kind : 3 * hp + kind + 1, :] = first + t[n + 1 : n + 2, :] * SMALL

        mpos = lax.broadcasted_iota(jnp.int32, (32, span), 1) - (length - 128)
        ipos = lax.broadcasted_iota(jnp.int32, (32, span), 0)

        def body(g, carry):
            sl = pl.ds(pl.multiple_of(g * 32, 32), 32)
            index = bucket_of(mpos - (ipos + g * 32), 0)
            for c in range(0, span, 128):
                for hp in range(H // 2):
                    table = jnp.broadcast_to(tabs[3 * hp : 3 * hp + 1, :], (32, 128))
                    a, b = unpack(look_up(table, index[:, c : c + 128]))
                    line[2 * hp, sl, c : c + 128] = a
                    line[2 * hp + 1, sl, c : c + 128] = b
            return carry

        lax.fori_loop(0, 4, body, 0)

    @pl.when(it == 0)
    def _():
        coords = jnp.concatenate([box_row(m) for m in range(4)] * 2, 0).astype(F32)
        by_token = coords.T
        cols[:, 0:8] = by_token
        lane = lax.broadcasted_iota(jnp.int32, (1, BOXF), 1)
        which = lane >> 5
        coord = jnp.where(
            which < 2,
            jnp.where(which == 0, by_token[:, 0:1], by_token[:, 1:2]),
            jnp.where(which == 2, by_token[:, 2:3], by_token[:, 3:4]),
        )
        feat_ref[...] = sine(coord * freq_ref[0:1, :], (lane >> 4) & 1).astype(BF)

    place = position(lax.broadcasted_iota(jnp.int32, (1, length), 1), half, length)
    dead = place >= window_length(meta_ref, w, windows)
    first = it * 128
    here = cols[pl.ds(pl.multiple_of(first, 128), 128), 0:8].astype(jnp.int32)
    for t in range(2):
        index = bucket_of(box_row(t) - here[:, t : t + 1], 2)
        map_ref[0, t] = index.astype(BF)
        maps[t] = index

    def block_of(n):
        return lax.rem(n + half * (blocks // 2), blocks)

    for r in range(0, 128, rows):
        rs = slice(r, r + rows)
        for n in range(blocks):
            cs = slice(n * 128, (n + 1) * 128)
            lc = pl.ds(pl.multiple_of((blocks - 1 + block_of(n) - block_of(it)) * 128, 128), 128)
            ia, idown = maps[0, rs, cs], maps[1, rs, cs]
            for hp in range(H // 2):
                ta = jnp.broadcast_to(tabs[3 * hp + 1 : 3 * hp + 2, :], (rows, 128))
                td = jnp.broadcast_to(tabs[3 * hp + 2 : 3 * hp + 3, :], (rows, 128))
                a, b = unpack(look_up(ta, ia) + look_up(td, idown))
                a = jnp.where(dead[:, cs], -1e9 * LOG2E, a + line[2 * hp, rs, lc])
                b = jnp.where(dead[:, cs], -1e9 * LOG2E, b + line[2 * hp + 1, rs, lc])
                out_ref[0, 2 * hp, rs, cs] = a.astype(BF)
                out_ref[0, 2 * hp + 1, rs, cs] = b.astype(BF)


def score_bias(meta, own, other, rel_tables):
    windows, length = other.shape[1], 2 * other.shape[2]
    span = (2 * (length // 128) - 1) * 128
    freq_count = BOXF // 8
    freqs = np.float32(1000.0) ** (-np.arange(freq_count, dtype=np.float32) / np.float32(freq_count))
    freqs = jnp.asarray(np.tile(freqs.astype(np.float32), (8, 8)))
    return pl.pallas_call(
        partial(bias_kernel, rows=128),
        grid=(windows, length // 128),
        in_specs=[
            pl.BlockSpec(memory_space=pltpu.SMEM),
            pl.BlockSpec(own.shape, lambda w, i: (0, 0, 0)),
            pl.BlockSpec(other.shape, lambda w, i: (0, 0, 0)),
            pl.BlockSpec((NB, 3 * H), lambda w, i: (0, 0)),
            pl.BlockSpec((8, BOXF), lambda w, i: (0, 0)),
        ],
        out_specs=[
            pl.BlockSpec((1, H, 128, length), lambda w, i: (w, 0, i, 0)),
            pl.BlockSpec((1, 2, 128, length), lambda w, i: (w, 0, i, 0)),
            pl.BlockSpec((length, BOXF), lambda w, i: (w, 0)),
        ],
        out_shape=[
            jax.ShapeDtypeStruct((windows, H, length, length), BF),
            jax.ShapeDtypeStruct((windows, 2, length, length), BF),
            jax.ShapeDtypeStruct((windows * length, BOXF), BF),
        ],
        scratch_shapes=[
            pltpu.VMEM((H, 128, span), F32),
            pltpu.VMEM((2, 128, length), jnp.int32),
            pltpu.VMEM((3 * H // 2 + 6, 128), F32),
            pltpu.VMEM((length, 128), F32),
        ],
        compiler_params=pltpu.CompilerParams(vmem_limit_bytes=VMEM),
        cost_estimate=SHORT,
        name="score_bias",
    )(meta, own, other, rel_tables, freqs)


def attend_kernel(meta_ref, q_ref, k_ref, v_ref, b_ref, o_ref, e_ref, r_ref, *, chunk):
    length = q_ref.shape[0]
    lane = lax.broadcasted_iota(jnp.int32, (length, 128), 1)
    place = position(lax.broadcasted_iota(jnp.int32, (length, 128), 0), meta_ref[1], length)
    live = place < window_length(meta_ref, pl.program_id(0), pl.num_programs(0))
    zero, one = jnp.zeros((), BF), jnp.ones((), BF)
    q, k, v = q_ref[...], k_ref[...], v_ref[...]
    outs = []
    for h in range(2):
        mine = (lane < DH) if h == 0 else (lane >= DH)
        keys = jnp.where(mine & live, k, zero)
        values = jnp.where(mine, v, jnp.where(lane == (DH if h == 0 else 0), one, zero))
        scores = dot(q, keys, 1, 1)
        for c in range(0, length, chunk):
            t = scores[c : c + chunk] * (LOG2E * DH**-0.5) + b_ref[0, h, c : c + chunk, :].astype(F32)
            e_ref[0, h, c : c + chunk, :] = jnp.exp2(t - jnp.max(t, 1, keepdims=True)).astype(BF)
        outs.append(dot(e_ref[0, h], values))
    r = jnp.where(lane < DH, 1.0 / outs[0][:, DH : DH + 1], 1.0 / outs[1][:, 0:1])
    r_ref[...] = r
    o_ref[...] = (jnp.where(lane < DH, outs[0], outs[1]) * r).astype(BF)


def attend(meta, qkv, bias):
    windows, _, length, _ = bias.shape
    pairs = H // 2
    col = lambda off: pl.BlockSpec((length, 128), lambda w, h: (w, off + h))
    sq = pl.BlockSpec((1, 2, length, length), lambda w, h: (w, h, 0, 0))
    width = H * DH
    return pl.pallas_call(
        partial(attend_kernel, chunk=64),
        grid=(windows, pairs),
        in_specs=[pl.BlockSpec(memory_space=pltpu.SMEM), col(0), col(pairs), col(2 * pairs), sq],
        out_specs=[col(0), sq, col(0)],
        out_shape=[
            jax.ShapeDtypeStruct((windows * length, width), BF),
            jax.ShapeDtypeStruct((windows, H, length, length), BF),
            jax.ShapeDtypeStruct((windows * length, width), F32),
        ],
        compiler_params=pltpu.CompilerParams(vmem_limit_bytes=VMEM),
        cost_estimate=SHORT,
        name="attend",
    )(meta, qkv, qkv, qkv, bias)


def attend_back_kernel(meta_ref, q_ref, k_ref, v_ref, e_ref, r_ref, o_ref, do_ref, *refs, chunk):
    d_ref, ds_ref, line_ref, sum_ref = refs[-4:]
    length = q_ref.shape[0]
    blocks = length // 128
    w = pl.program_id(1)
    lane = lax.broadcasted_iota(jnp.int32, (length, 128), 1)
    zero = jnp.zeros((), BF)
    q, k, v = q_ref[...], k_ref[...], v_ref[...]
    up = do_ref[...].astype(F32) * r_ref[...]
    both = up * o_ref[...].astype(F32)
    up = up.astype(BF)
    up_t, q_t = up.T, q.T
    dq, dv_t, dk_t = None, [], []

    def block_of(n):
        return lax.rem(n + meta_ref[1] * (blocks // 2), blocks)

    @pl.when(w == 0)
    def _():
        line_ref[...] = jnp.zeros_like(line_ref)

    for h in range(2):
        mine = (lane < DH) if h == 0 else (lane >= DH)
        center = jnp.sum(jnp.where(mine, both, 0.0), 1, keepdims=True)
        dp = dot(up, jnp.where(mine, v, zero), 1, 1)
        for c in range(0, length, chunk):
            e = e_ref[0, h, c : c + chunk, :].astype(F32)
            ds = e * (dp[c : c + chunk] - center[c : c + chunk])
            ds_ref[0, h, c : c + chunk, :] = ds.astype(BF)
            rows = slice(c % 128, c % 128 + chunk)
            for n in range(blocks):
                d = blocks - 1 + block_of(n) - block_of(c // 128)
                line_ref[h, rows, pl.ds(pl.multiple_of(d * 128, 128), 128)] += ds[:, n * 128 : (n + 1) * 128]
        ds = ds_ref[0, h]
        part = dot(ds, jnp.where(mine, k, zero))
        dq = part if dq is None else dq + part
        dv_t.append(dot(up_t[h * DH : (h + 1) * DH], e_ref[0, h]))
        dk_t.append(dot(q_t[h * DH : (h + 1) * DH], ds))
    parts = (dq * DH**-0.5, jnp.concatenate(dk_t, 0).T * DH**-0.5, jnp.concatenate(dv_t, 0).T)
    for n, x in enumerate(parts):
        cols = slice(n * 128, (n + 1) * 128)
        x = x.astype(BF)
        d_ref[:, cols] = x
        sums = jnp.broadcast_to(column_sums(x.astype(F32)), (8, 128))
        sum_ref[:, cols] = jnp.where(w == 0, sums, sum_ref[:, cols] + sums)


def attend_back(meta, qkv, e, r, o, do, first, count, total, at, before=None):
    windows, _, length, _ = e.shape
    pairs = H // 2
    col = lambda off: pl.BlockSpec((length, 128), lambda h, w: (w, off + h))
    sq = pl.BlockSpec((1, 2, length, length), lambda h, w: (w, first + h, 0, 0))
    span = (2 * (length // 128) - 1) * 128
    more = [] if before is None else [before]
    return pl.pallas_call(
        partial(attend_back_kernel, chunk=64),
        grid=(count, windows),
        in_specs=[pl.BlockSpec(memory_space=pltpu.SMEM)]
        + [col(first), col(pairs + first), col(2 * pairs + first), sq, col(first), col(first), col(first)]
        + [pl.BlockSpec(memory_space=pl.ANY)] * len(more),
        out_specs=[
            pl.BlockSpec((length, 384), lambda h, w: (w, at + h)),
            pl.BlockSpec((1, 2, length, length), lambda h, w: (w, h, 0, 0)),
            pl.BlockSpec((2, 128, span), lambda h, w: (h, 0, 0)),
            pl.BlockSpec((8, 384), lambda h, w: (0, h)),
        ],
        out_shape=[
            jax.ShapeDtypeStruct((windows * length, total * 384), BF),
            jax.ShapeDtypeStruct((windows, 2 * count, length, length), BF),
            jax.ShapeDtypeStruct((2 * count, 128, span), F32),
            jax.ShapeDtypeStruct((8, count * 384), F32),
        ],
        input_output_aliases={8: 0} if more else {},
        compiler_params=pltpu.CompilerParams(vmem_limit_bytes=VMEM),
        cost_estimate=SHORT,
        name="attend_back",
    )(meta, qkv, qkv, qkv, e, r, o, do, *more)


def spread(refs, rows, stride):
    h = 0
    for ref in refs:
        for n in range(ref.shape[-3]):
            x = (ref[0, n] if len(ref.shape) == 4 else ref[n]).astype(F32)
            for c in range(x.shape[1] // 128):
                rows[c, h * stride : h * stride + x.shape[0], :] = x[:, c * 128 : (c + 1) * 128]
            h += 1


def heads_of(rows, i, stride):
    return [rows[c, pl.ds(i, 16, stride=stride), :].astype(BF) for c in range(rows.shape[0])]


def one_hot(index):
    width = index.shape[1]
    ids = lax.broadcasted_iota(jnp.int32, (NB, width), 0).astype(BF)
    hit = jnp.broadcast_to(index, (NB, width)).astype(BF) == ids
    return jnp.where(hit, jnp.ones((), BF), jnp.zeros((), BF))


def table_kernel(*refs, parts, with_line):
    ds_refs, refs = refs[:parts], refs[parts:]
    line_refs, refs = refs[: parts * with_line], refs[parts * with_line :]
    map_ref, out_ref, rows, maps = refs[0], refs[1], refs[-2], refs[-1]
    tile = map_ref.shape[2]
    step = pl.program_id(0)

    @pl.when(step == 0)
    def _():
        out_ref[...] = jnp.zeros_like(out_ref)
        rows[...] = jnp.zeros_like(rows)

    if with_line:
        line_out, line_rows = refs[2], refs[3]
        share = line_refs[0].shape[1]
        span = line_refs[0].shape[2]

        @pl.when(step == 0)
        def _():
            line_out[...] = jnp.zeros_like(line_out)
            line_rows[...] = jnp.zeros_like(line_rows)

        spread(line_refs, line_rows, share + 8)
        offset = lax.broadcasted_iota(jnp.int32, (8, span), 1) - (span - 128) // 2
        down = lax.broadcasted_iota(jnp.int32, (8, span), 0) + step * share
        lhs, rhs = [], []
        for i in range(share):
            if i % 8 == 0:
                index = bucket_of(offset - (down + i), 0).astype(F32)
            lhs += heads_of(line_rows, i, share + 8)
            rhs.append(one_hot(index[i % 8 : i % 8 + 1, :]))
        line_out[...] += dot(jnp.concatenate(lhs, 1), jnp.concatenate(rhs, 1), 1, 1)

    spread(ds_refs, rows, tile + 8)
    maps[...] = map_ref[0].astype(F32)
    lhs, rhs = [], []
    for i in range(tile):
        lhs += heads_of(rows, i, tile + 8)
        rhs.append(jnp.concatenate([one_hot(maps[t, i : i + 1, :]) for t in range(2)], 0))
    out_ref[...] += dot(jnp.concatenate(lhs, 1), jnp.concatenate(rhs, 1), 1, 1)


def table_grads(ds_parts, lines, maps, w, share_of=1, share=0):
    _, _, length, _ = maps.shape
    tile = 64
    parts = len(ds_parts)
    steps = length // tile // share_of
    at = share * steps
    outs, out_shapes = [pl.BlockSpec((16, 2 * NB), lambda i: (0, 0))], [jax.ShapeDtypeStruct((16, 2 * NB), F32)]
    line_specs, line_rows = [], []
    if lines:
        rows, span = 128 // steps, lines[0].shape[2]
        line_specs = [pl.BlockSpec((x.shape[0], rows, span), lambda i: (0, i, 0)) for x in lines]
        line_rows = [pltpu.VMEM((span // 128, 16 * (rows + 8), 128), F32)]
        outs.append(pl.BlockSpec((16, NB), lambda i: (0, 0)))
        out_shapes.append(jax.ShapeDtypeStruct((16, NB), F32))
    return pl.pallas_call(
        partial(table_kernel, parts=parts, with_line=bool(lines)),
        grid=(steps,),
        in_specs=[pl.BlockSpec((1, x.shape[1], tile, length), lambda i: (w, 0, at + i, 0)) for x in ds_parts]
        + line_specs
        + [pl.BlockSpec((1, 2, tile, length), lambda i: (w, 0, at + i, 0))],
        out_specs=outs,
        out_shape=out_shapes,
        scratch_shapes=line_rows
        + [pltpu.VMEM((length // 128, 16 * (tile + 8), 128), F32), pltpu.VMEM((2, tile, length), F32)],
        compiler_params=pltpu.CompilerParams(vmem_limit_bytes=VMEM),
        cost_estimate=SHORT,
        name="table_grads",
    )(*ds_parts, *lines, maps)


def gelu_both(x):
    cdf = 0.5 + 0.5 * lax.erf(x * 0.7071067811865476)
    density = jnp.exp2((-0.5 * LOG2E) * (x * x)) * 0.3989422804014327
    return x * cdf, cdf + x * density


def norm_forward(summed, params):
    centered = summed - jnp.mean(summed, -1, keepdims=True)
    inverse = lax.rsqrt(jnp.mean(centered * centered, -1, keepdims=True) + EPS)
    normed = centered * inverse
    return normed * params[0:1] + params[1:2], normed, inverse


def norm_backward(upstream, normed, inverse, params):
    scaled = upstream * params[0:1]
    return inverse * (
        scaled - jnp.mean(scaled, -1, keepdims=True) - normed * jnp.mean(scaled * normed, -1, keepdims=True)
    )


def column_sums(x):
    return jnp.sum(x, 0, keepdims=True)


def tokens_of(own_ref, other_ref, chunk):
    windows, local, _ = other_ref.shape
    step = min(chunk, local)
    for w in range(windows):
        for n, ref in enumerate((own_ref, other_ref)):
            for c in range(0, local, step):
                yield slice((2 * w + n) * local + c, (2 * w + n) * local + c + step), ref[w, c : c + step, :]


def front_kernel(meta_ref, own_ref, other_ref, f_ref, box_ref, w_ref, qv_ref, low_ref, out_ref):
    step = pl.program_id(0)
    third = pl.num_programs(0) // 3

    @pl.when(step == 0)
    def _():
        for cs, x in tokens_of(own_ref, other_ref, 256):
            low_ref[cs, :] = (x.astype(F32) + dot(f_ref[cs, :], box_ref[...])).astype(BF)

    wide = out_ref.shape[1]
    cols = pl.ds(pl.multiple_of(lax.rem(step, third) * wide, wide), wide)
    shift = jnp.where(step < third, qv_ref[0:1, cols], jnp.where(step < 2 * third, 0.0, qv_ref[1:2, cols]))
    out_ref[...] = (dot(low_ref[...], w_ref[...]) + shift).astype(BF)


def front(meta, own, other, features, box_weight, qkv_weight, qv_bias):
    windows, local, width = other.shape
    tokens = 2 * windows * local
    cols = qkv_weight.shape[1]
    whole = lambda x: pl.BlockSpec(x.shape, lambda n, p: (0,) * len(x.shape))
    return pl.pallas_call(
        front_kernel,
        grid_spec=pltpu.PrefetchScalarGridSpec(
            num_scalar_prefetch=1,
            grid=(cols // width,),
            in_specs=[
                pl.BlockSpec(other.shape, lambda n, p: (p[1], 0, 0)),
                whole(other),
                whole(features),
                whole(box_weight),
                pl.BlockSpec((width, width), lambda n, p: (0, n)),
                whole(qv_bias),
            ],
            out_specs=[
                pl.BlockSpec((tokens, width), lambda n, p: (0, 0)),
                pl.BlockSpec((tokens, width), lambda n, p: (0, n)),
            ],
        ),
        out_shape=[jax.ShapeDtypeStruct((tokens, width), BF), jax.ShapeDtypeStruct((tokens, cols), BF)],
        compiler_params=pltpu.CompilerParams(vmem_limit_bytes=VMEM),
        cost_estimate=SHORT,
        name="front",
    )(meta, own, other, features, box_weight, qkv_weight, qv_bias)


def feed_kernel(meta_ref, own_ref, other_ref, f_ref, box_ref, att_ref, wo_ref, bo_ref, n1_ref, w1_ref, b1_ref, w2_ref, b2_ref, n2_ref, cot_own_ref, cot_other_ref, z_ref, low_ref, act_ref, slope_ref, out_own_ref, out_other_ref, dlow_ref, sum_ref, acc, *, chunk):
    step = pl.program_id(0)
    tokens = low_ref.shape[0]

    @pl.when(step == 0)
    def _():
        for cs, x in tokens_of(own_ref, other_ref, chunk):
            entry = x.astype(F32) + dot(f_ref[cs, :], box_ref[...])
            z = entry + (dot(att_ref[cs, :], wo_ref[...]) + bo_ref[...])
            second = norm_forward(z, n1_ref[...])[0]
            z_ref[cs, :] = z.astype(BF)
            low_ref[cs, :] = second.astype(BF)
            acc[cs, :] = second

    for c in range(0, tokens, chunk):
        cs = slice(c, c + chunk)
        active, slope = gelu_both(dot(low_ref[cs, :], w1_ref[...]) + b1_ref[...])
        active = active.astype(BF)
        act_ref[cs, :] = active
        slope_ref[cs, :] = slope.astype(BF)
        acc[cs, :] += dot(active, w2_ref[...])

    @pl.when(step == pl.num_programs(0) - 1)
    def _():
        sums = [0.0, 0.0, 0.0]
        local = cot_other_ref.shape[1]
        for cs, x in tokens_of(cot_own_ref, cot_other_ref, 128):
            result, normed, inverse = norm_forward(acc[cs, :] + b2_ref[...], n2_ref[...])
            place = cs.start % local
            out = (out_own_ref, out_other_ref)[cs.start // local % 2]
            out[cs.start // local // 2, place : place + 128, :] = result.astype(BF)
            up = x.astype(F32)
            low = norm_backward(up, normed, inverse, n2_ref[...]).astype(BF)
            dlow_ref[cs, :] = low
            sums = [sums[0] + column_sums(up * normed), sums[1] + column_sums(up), sums[2] + column_sums(low.astype(F32))]
        sum_ref[...] = jnp.concatenate(sums + [jnp.zeros((5, sums[0].shape[1]), F32)], 0)


def feed(meta, own, other, features, box_weight, attended, out_weight, out_bias, norm_one, w1, b1, w2, b2, norm_two, cot_own, cot_other):
    tokens, width = attended.shape
    inner = w1.shape[1]
    tile = 1024
    whole = lambda shape: pl.BlockSpec(shape, lambda n, p: (0,) * len(shape))
    mine = pl.BlockSpec(other.shape, lambda n, p: (p[1], 0, 0))
    full = whole((tokens, width))
    part = pl.BlockSpec((tokens, tile), lambda n, p: (0, n))
    return pl.pallas_call(
        partial(feed_kernel, chunk=512),
        grid_spec=pltpu.PrefetchScalarGridSpec(
            num_scalar_prefetch=1,
            grid=(inner // tile,),
            in_specs=[
                mine,
                whole(other.shape),
                whole(features.shape),
                whole(box_weight.shape),
                full,
                whole(out_weight.shape),
                whole((1, width)),
                whole((2, width)),
                pl.BlockSpec((width, tile), lambda n, p: (0, n)),
                pl.BlockSpec((1, tile), lambda n, p: (0, n)),
                pl.BlockSpec((tile, width), lambda n, p: (n, 0)),
                whole((1, width)),
                whole((2, width)),
                mine,
                whole(other.shape),
            ],
            out_specs=[full, full, part, part, whole(other.shape), whole(other.shape), full, whole((8, width))],
            scratch_shapes=[pltpu.VMEM((tokens, width), F32)],
        ),
        out_shape=[
            jax.ShapeDtypeStruct((tokens, width), BF),
            jax.ShapeDtypeStruct((tokens, width), BF),
            jax.ShapeDtypeStruct((tokens, inner), BF),
            jax.ShapeDtypeStruct((tokens, inner), BF),
            jax.ShapeDtypeStruct(other.shape, BF),
            jax.ShapeDtypeStruct(other.shape, BF),
            jax.ShapeDtypeStruct((tokens, width), BF),
            jax.ShapeDtypeStruct((8, width), F32),
        ],
        compiler_params=pltpu.CompilerParams(vmem_limit_bytes=VMEM),
        cost_estimate=SHORT,
        name="feed",
    )(
        meta, own, other, features, box_weight, attended, out_weight, out_bias.reshape(1, -1), norm_one,
        w1, b1.reshape(1, -1), w2, b2.reshape(1, -1), norm_two, cot_own, cot_other,
    )


def feed_back_kernel(dlow_ref, w1_ref, w2_ref, slope_ref, z_ref, n1_ref, wo_ref, din_ref, bias_ref, dbr_ref, datt_ref, sum_ref, acc, *, chunk):
    step = pl.program_id(0)
    tokens = dlow_ref.shape[0]

    @pl.when(step == 0)
    def _():
        acc[...] = dlow_ref[...].astype(F32)

    sums = 0.0
    for c in range(0, tokens, chunk):
        cs = slice(c, c + chunk)
        d_inner = (dot(dlow_ref[cs, :], w2_ref[...], 1, 1) * slope_ref[cs, :].astype(F32)).astype(BF)
        din_ref[cs, :] = d_inner
        sums = sums + column_sums(d_inner.astype(F32))
        acc[cs, :] += dot(d_inner, w1_ref[...], 1, 1)
    bias_ref[...] = jnp.concatenate([sums, jnp.zeros((7, sums.shape[1]), F32)], 0)

    @pl.when(step == pl.num_programs(0) - 1)
    def _():
        totals = [0.0, 0.0, 0.0]
        for c in range(0, tokens, 128):
            cs = slice(c, c + 128)
            _, normed, inverse = norm_forward(z_ref[cs, :].astype(F32), n1_ref[...])
            up = acc[cs, :]
            low = norm_backward(up, normed, inverse, n1_ref[...]).astype(BF)
            dbr_ref[cs, :] = low
            totals = [
                totals[0] + column_sums(up * normed),
                totals[1] + column_sums(up),
                totals[2] + column_sums(low.astype(F32)),
            ]
        sum_ref[...] = jnp.concatenate(totals + [jnp.zeros((5, totals[0].shape[1]), F32)], 0)
        datt_ref[...] = dot(dbr_ref[...], wo_ref[...], 1, 1).astype(BF)


def feed_back(d_outer, w1, w2, slope, z_one, norm_one, out_weight):
    tokens, width = z_one.shape
    inner = w1.shape[1]
    tile = 1024
    whole = lambda shape: pl.BlockSpec(shape, lambda n: (0, 0))
    full = whole((tokens, width))
    return pl.pallas_call(
        partial(feed_back_kernel, chunk=512),
        grid=(inner // tile,),
        in_specs=[
            full,
            pl.BlockSpec((width, tile), lambda n: (0, n)),
            pl.BlockSpec((tile, width), lambda n: (n, 0)),
            pl.BlockSpec((tokens, tile), lambda n: (0, n)),
            full,
            whole((2, width)),
            whole((width, width)),
        ],
        out_specs=[
            pl.BlockSpec((tokens, tile), lambda n: (0, n)),
            pl.BlockSpec((8, tile), lambda n: (0, n)),
            full,
            full,
            whole((8, width)),
        ],
        out_shape=[
            jax.ShapeDtypeStruct((tokens, inner), BF),
            jax.ShapeDtypeStruct((8, inner), F32),
            jax.ShapeDtypeStruct((tokens, width), BF),
            jax.ShapeDtypeStruct((tokens, width), BF),
            jax.ShapeDtypeStruct((8, width), F32),
        ],
        scratch_shapes=[pltpu.VMEM((tokens, width), F32)],
        compiler_params=pltpu.CompilerParams(vmem_limit_bytes=VMEM),
        cost_estimate=SHORT,
        name="feed_back",
    )(d_outer, w1, w2, slope, z_one, norm_one, out_weight)


UNIT = 384
PIECES = 2


def halves(full, place_ref):
    rows = full.shape[0] // 2
    upper = place_ref[1] == 0
    low, high = full[:rows], full[rows:]
    return jnp.where(upper, high, low).astype(BF), jnp.where(upper, low, high).astype(BF)


def wide_grads_kernel(place_ref, *refs, counts):
    step = pl.program_id(0)
    pairs = len(counts)
    outs = refs[3 * pairs :]
    at = 0
    for n, count in enumerate(counts):

        @pl.when((step >= at) & (step < at + count))
        def _():
            full = dot(refs[3 * n][...], jnp.concatenate([refs[3 * n + 1][...], refs[3 * n + 2][...]], 1), 0, 0)
            both = halves(full, place_ref)
            for m, x in enumerate(both):
                side = x.shape[0] // 2
                for k in range(2):
                    outs[2 * m + k][...] = x[k * side : (k + 1) * side, :UNIT].reshape(outs[2 * m + k].shape)
                outs[4 + m][...] = x[:, UNIT:].reshape(outs[4 + m].shape)

        at += count


def wide_grads(place, pairs):
    tokens, rows = pairs[0][0].shape
    counts = [right.shape[1] // (2 * UNIT) for _, right in pairs]
    specs, at = [], 0
    for (left, right), count in zip(pairs, counts):

        def block(i, p, send, at=at, count=count):
            owner = 1 - p[0] if send else p[0]
            return (0, owner * count + jnp.clip(i - at, 0, count - 1))

        specs += [
            pl.BlockSpec(left.shape, lambda i, p: (0, 0)),
            pl.BlockSpec((tokens, UNIT), partial(block, send=True)),
            pl.BlockSpec((tokens, UNIT), partial(block, send=False)),
        ]
        at += count
    piece = pl.BlockSpec((1, 1, rows // 4, UNIT), lambda i, p: (0, i, 0, 0))
    out = pl.BlockSpec((2, 1, rows // 4, UNIT), lambda i, p: (0, i, 0, 0))
    outs = pl.pallas_call(
        partial(wide_grads_kernel, counts=counts),
        grid_spec=pltpu.PrefetchScalarGridSpec(
            num_scalar_prefetch=1,
            grid=(at,),
            in_specs=specs,
            out_specs=[piece] * 4 + [out] * 2,
        ),
        out_shape=[jax.ShapeDtypeStruct((n, at, rows // 4, UNIT), BF) for n in (1, 1, 1, 1, 2, 2)],
        compiler_params=pltpu.CompilerParams(vmem_limit_bytes=VMEM),
        cost_estimate=SHORT,
        name="wide_grads",
    )(place, *[x for left, right in pairs for x in (left, right, right)])
    return [x.reshape(-1, UNIT) for x in outs]


def long_grads_kernel(place_ref, left_ref, send_ref, keep_ref, *outs):
    full = dot(left_ref[...], jnp.concatenate([send_ref[...], keep_ref[...]], 1), 0, 0).astype(BF)
    for n in range(4):

        @pl.when(pl.program_id(0) == n)
        def _():
            outs[n][...] = full[:, :UNIT]
            outs[4 + n // 2][...] = full[:, UNIT:]


def long_grads(place, left, right):
    tokens, rows = left.shape
    tile = rows // 4

    def quarter(i, p):
        owner = jnp.where(i < 2, 1 - p[1], p[1])
        return (0, owner * 2 + lax.rem(i, 2))

    piece = pl.BlockSpec((tile, UNIT), lambda i, p: (0, 0))
    other = pl.BlockSpec((tile, UNIT), lambda i, p: (jnp.minimum(i, 1), 0))
    own = pl.BlockSpec((tile, UNIT), lambda i, p: (jnp.maximum(i - 2, 0), 0))
    return pl.pallas_call(
        long_grads_kernel,
        grid_spec=pltpu.PrefetchScalarGridSpec(
            num_scalar_prefetch=1,
            grid=(4,),
            in_specs=[
                pl.BlockSpec((tokens, tile), quarter),
                pl.BlockSpec((tokens, UNIT), lambda i, p: (0, 1 - p[0])),
                pl.BlockSpec((tokens, UNIT), lambda i, p: (0, p[0])),
            ],
            out_specs=[piece] * 4 + [other, own],
        ),
        out_shape=[jax.ShapeDtypeStruct((n * tile, UNIT), BF) for n in (1, 1, 1, 1, 2, 2)],
        compiler_params=pltpu.CompilerParams(vmem_limit_bytes=VMEM),
        cost_estimate=SHORT,
        name="long_grads",
    )(place, left, right, right)


E_ROWS = 16


def last_kernel(place_ref, x_ref, dx_ref, f_ref, own_ref, other_ref, two_ref, one_ref, in_ref, *refs):
    qv_refs, line_ref, small_refs, outs = refs[:3], refs[3], refs[4:-4], refs[-4:]
    mine = place_ref[0] == 0
    upper = place_ref[1] == 0
    width = x_ref.shape[1]
    middle = width // 2
    x = dot(x_ref[...], dx_ref[...], 0, 0).astype(BF)
    entry = jnp.concatenate([ref[w] for w in range(own_ref.shape[0]) for ref in (own_ref, other_ref)], 0)
    box = dot(f_ref[...], entry, 0, 0).astype(BF)
    small = small_refs[0][...]
    for ref in small_refs[1:]:
        small = small + ref[...]
    tables = jnp.concatenate([line_ref[...], small, jnp.zeros((16, NB), F32)], 1).T
    blocks = [ref[0:1, p : p + UNIT] for ref in qv_refs for p in range(0, ref.shape[1], UNIT)]
    qv = [jnp.concatenate([y[:, at : at + 128] for y in blocks], 1) for at in (0, 256)]
    halves_of = []
    for n in range(2):
        cols = slice(n * middle, (n + 1) * middle)
        inner = in_ref[0:1, n * 2 * width : (n + 1) * 2 * width]
        sums = [
            two_ref[n : n + 1, :],
            one_ref[n : n + 1, :],
            qv[n],
            jnp.concatenate([one_ref[2:3, cols], two_ref[2:3, cols]], 1),
            inner[:, :width],
            inner[:, width:],
            jnp.zeros((E_ROWS - 6, width), F32),
        ]
        share = [tables[m * NB + n * NB // 2 : m * NB + (n + 1) * NB // 2, :] for m in range(3)]
        share = [jnp.pad(t, ((0, 0), (0, 128 - t.shape[1]))) for t in share]
        sides = [jnp.concatenate(sums, 0), jnp.concatenate(share + [jnp.zeros((E_ROWS, width - 3 * 128), F32)], 1)]
        q, h = x.shape[0] // 4, box.shape[0] // 4
        halves_of.append(
            jnp.concatenate(
                [
                    y
                    for m in range(2)
                    for y in (
                        x[(2 * n + m) * q : (2 * n + m + 1) * q],
                        box[(2 * n + m) * h : (2 * n + m + 1) * h],
                        sides[m].astype(BF),
                    )
                ],
                0,
            )
        )
    for m in range(2):
        rows = jnp.where(upper, halves_of[1 - m], halves_of[m])
        outs[m][...] = jnp.where(mine, rows[:, middle:], rows[:, :middle])
        outs[2 + m][...] = jnp.where(mine, rows[:, :middle], rows[:, middle:])


def last_grads(place, x, dx, f, own, other, *sums):
    rows = (x.shape[1] + f.shape[1]) // 4 + E_ROWS
    vmem = pl.BlockSpec(memory_space=pltpu.VMEM)
    return pl.pallas_call(
        last_kernel,
        in_specs=[pl.BlockSpec(memory_space=pltpu.SMEM)] + [vmem] * (5 + len(sums)),
        out_specs=[vmem] * 4,
        out_shape=[jax.ShapeDtypeStruct((2 * rows, UNIT), BF)] * 4,
        compiler_params=pltpu.CompilerParams(vmem_limit_bytes=LESS),
        cost_estimate=SHORT,
        name="last_grads",
    )(place, x, dx, f, own, other, *sums)


def lay_kernel(place_ref, *refs, kind, rows):
    last = refs[4:8] if kind == "heads" else refs[:4]
    pieces, outs = refs[:4], refs[8 if kind == "heads" else 4 :]
    core, step = place_ref[0], pl.program_id(0)

    def lay_piece(ref, owner):
        blocks = ref.shape[0] // rows
        for n in range(blocks):
            x = ref[n * rows : (n + 1) * rows, :].astype(F32)
            if kind == "long":
                outs[0][n * rows : (n + 1) * rows, owner * UNIT : (owner + 1) * UNIT] = x
            elif kind == "wide":
                at = (owner * blocks + n) * UNIT
                outs[0][:, at : at + UNIT] = x
            elif n == 0:
                outs[0][:, owner * UNIT : (owner + 1) * UNIT] = x
            else:
                lay_pair(x, owner * 2 + n - 1)

    def lay_last(ref, owner):
        lay_pair(ref[:rows, :].astype(F32), 4 + owner)
        box = BOXF // 4
        cols = slice(owner * UNIT, (owner + 1) * UNIT)
        outs[2][:, cols] = ref[rows : rows + box, :].astype(F32)
        small = ref[rows + box : rows + box + E_ROWS, :].astype(F32)

        @pl.when(step == 0)
        def _():
            for n in range(3):
                outs[3 + n][:, cols] = small[n : n + 1]
            outs[6 + owner][...] = small[3]
            for n in range(2):
                at = n * 2 * UNIT + owner * UNIT
                outs[8][at : at + UNIT] = small[4 + n]

        if owner == 0:

            @pl.when(step == 1)
            def _():
                outs[9][...] = jnp.concatenate([small[:, n * 128 : n * 128 + H] for n in range(3)], 1)

    def lay_pair(x, pair):
        for m in range(3):
            at = (m * (H // 2) + pair) * 128
            outs[1][:, at : at + 128] = x[:, m * 128 : (m + 1) * 128]

    def choose(refs, side, lay_one):
        for other_side in range(2):
            for owner in range(2):
                for other_core in range(2):

                    @pl.when(((step == side) == (other_side == 0)) & (core == (owner ^ other_core)))
                    def _():
                        lay_one(refs[2 * other_side + other_core], owner)

    choose(pieces, place_ref[2], lay_piece)
    if kind == "heads":
        choose(last, place_ref[3], lay_last)


def lay(place, pieces, kind, rows):
    blocks = pieces[0].shape[0] // rows
    whole = None
    if kind == "long":
        shapes = [(2 * blocks * rows, 2 * UNIT)]
    elif kind == "wide":
        shapes = [(2 * rows, 2 * blocks * UNIT)]
    else:
        width = 2 * UNIT
        shapes = [(2 * rows, width), (2 * rows, 3 * width), (BOXF // 2, width)]
        whole = [(1, width)] * 3 + [(UNIT,)] * 2 + [(2 * width,), (NB // 2, 3 * H)]
    return pl.pallas_call(
        partial(lay_kernel, kind=kind, rows=rows),
        grid=(2,),
        in_specs=[pl.BlockSpec(memory_space=pltpu.SMEM)] + [pl.BlockSpec(x.shape, lambda i: (0, 0)) for x in pieces],
        out_specs=[pl.BlockSpec((m // 2, n), lambda i: (i, 0)) for m, n in shapes]
        + [pl.BlockSpec(shape, lambda i, n=len(shape): (0,) * n) for shape in whole or []],
        out_shape=[jax.ShapeDtypeStruct(shape, F32) for shape in shapes + (whole or [])],
        compiler_params=pltpu.CompilerParams(vmem_limit_bytes=LESS),
        cost_estimate=SHORT,
        name="lay",
    )(place, *pieces)


def entry_kernel(a_ref, b_ref, w_ref, sum_ref, own_ref, other_ref):
    pairs = H // 2
    weight = jnp.concatenate([w_ref[:, (m * pairs + n) * 128 : (m * pairs + n + 1) * 128] for n in range(pairs) for m in range(3)], 1)
    both = jnp.concatenate([a_ref[...], b_ref[...]], 1)
    out = (sum_ref[...].astype(F32) + dot(both, weight, 1, 1)).astype(BF)
    local = own_ref.shape[1]
    own_ref[0] = out[:local]
    other_ref[0] = out[local:]


def entry_grad(first, last, weight, base, windows):
    tokens, width = base.shape
    tile = tokens // windows
    row = lambda x: pl.BlockSpec((tile, x.shape[1]), lambda i: (i, 0))
    out = pl.BlockSpec((1, tile // 2, width), lambda i: (i, 0, 0))
    return pl.pallas_call(
        entry_kernel,
        grid=(windows,),
        in_specs=[row(first), row(last), pl.BlockSpec(weight.shape, lambda i: (0, 0)), row(base)],
        out_specs=[out, out],
        out_shape=[jax.ShapeDtypeStruct((windows, tile // 2, width), BF)] * 2,
        compiler_params=pltpu.CompilerParams(vmem_limit_bytes=VMEM),
        cost_estimate=SHORT,
        name="entry_grad",
    )(first, last, weight, base)


def shards(
    docs,
    hidden_in,
    boxes,
    lengths,
    box_weight,
    qkv_weight,
    qv_bias,
    out_weight,
    out_bias,
    rel_tables,
    norm_one,
    ffn_in_weight,
    ffn_in_bias,
    ffn_out_weight,
    ffn_out_bias,
    norm_two,
    cotangent,
):
    half = lax.axis_index("half")
    doc = lax.axis_index("doc")
    core, side = doc & 1, (doc >> 1) & 1
    own, local_len, width = hidden_in.shape
    windows = own // 2
    length = 2 * local_len
    tokens = windows * length

    def swap_half(x):
        return lax.ppermute(x, "half", [(0, 1), (1, 0)])

    def swap_doc(x, bit):
        return lax.ppermute(x, "doc", [(i, i ^ (1 << bit)) for i in range(docs)])

    def part(x, index, axis):
        if isinstance(x, list):
            return jnp.where(index == 0, *x)
        size = x.shape[axis] // 2
        return lax.dynamic_slice_in_dim(x, index * size, size, axis)

    def ordered(index, mine, other, axis):
        return jnp.where(index == 0, jnp.concatenate([mine, other], axis), jnp.concatenate([other, mine], axis))

    def tie(x, *others):
        return lax.optimization_barrier((x,) + others)[0]

    meta = jnp.concatenate([jnp.stack([core, half, side, (doc >> 2) & 1]).astype(jnp.int32), lengths])
    box_other = swap_half(part(boxes, 1 - half, 1))
    hidden_other = swap_half(part(tie(hidden_in, box_other), 1 - half, 0))
    bias, maps, features = score_bias(meta, boxes, box_other, rel_tables)
    cot_other = swap_half(part(tie(cotangent, maps), 1 - half, 0))
    entry_low, qkv = front(meta, hidden_in, hidden_other, features, box_weight, qkv_weight, qv_bias)
    attended, e, r = attend(meta, qkv, bias)
    z_one, second_low, active, slope, out_mine, out_send, d_outer, sums_two = feed(
        meta,
        hidden_in,
        hidden_other,
        features,
        box_weight,
        attended,
        out_weight,
        out_bias,
        norm_one,
        ffn_in_weight,
        ffn_in_bias,
        ffn_out_weight,
        ffn_out_bias,
        norm_two,
        cotangent,
        cot_other,
    )

    pairs, early = H // 2, H // 3
    late_pairs = pairs - early
    step = early // 2
    more = list(range(2, docs.bit_length() - 1))
    place = meta
    last = [None]

    def now(x):
        return x if last[0] is None else tie(x, *last[0])

    def then(x, *more):
        last[0] = (x,) + more
        return x

    def joined(pieces):
        return jnp.concatenate(pieces, 0) if len(pieces) > 1 else pieces[0]

    def total(*xs):
        out = xs[0].astype(F32)
        for x in xs[1:]:
            out = out + x.astype(F32)
        return out.astype(BF)

    class Chain:
        def core(self, *parts):
            pieces, keep, keep_own = parts[:-2], parts[-2], parts[-1]
            count = len(pieces) // 2
            then(keep_own)
            pieces = [swap_doc(x, 0) for x in pieces]
            self.own = [keep, pieces[:count], keep_own, pieces[count:]]

        def half_later(self):
            keep, come, keep_own, come_own = self.own
            send = then(total(now(keep), joined(come)))
            self.own = [keep_own, come_own, swap_half(send)]

        def add_own(self):
            keep_own, come_own, come = self.own
            self.own = [then(total(now(keep_own), joined(come_own))), come]

        def half(self):
            keep, come, keep_own, come_own = self.own
            keep, keep_own = lax.optimization_barrier((keep, keep_own) + last[0])[:2]
            send, own = total(keep, joined(come)), total(keep_own, joined(come_own))
            then(send, own)
            self.own = [own, swap_half(send)]

        def split(self, bit):
            b = (doc >> bit) & 1
            own = [now(self.own[0])] + self.own[1:]
            send = then(total(*[part(x, 1 - b, 0) for x in own]))
            keep = total(*[part(x, b, 0) for x in own])
            self.own = [keep, swap_doc(send, bit)]

        def double(self, bits):
            x = then(total(now(self.own[0]), *self.own[1:]))
            for bit in bits[:-1]:
                x = total(x, swap_doc(x, bit))
            self.own = [x, swap_doc(x, bits[-1])]

        def back(self, bit):
            x = then(total(now(self.own[0]), *self.own[1:]))
            self.parted, self.own = bit, [x, swap_doc(x, bit)]

        def gather(self, bit=1):
            if hasattr(self, "parted"):
                x = then(ordered((doc >> self.parted) & 1, now(self.own[0]), self.own[1], 0))
            else:
                x = then(total(now(self.own[0]), *self.own[1:]))
            self.mine, self.across = x, swap_doc(x, bit)
            self.beside = swap_doc(x, 0)

        def settle(self, *others):
            then(*last[0], self.beside, *others)

        def pieces(self):
            return [now(self.mine), self.beside, self.across, swap_doc(now(self.across), 0)]

    def back(first, count, total_pairs, at, before):
        out = attend_back(meta, qkv, e, r, attended, now(d_attended), first, count, total_pairs, at, before)
        then(out[0])
        return out

    a, b, c, d = Chain(), Chain(), Chain(), Chain()
    block_rows = width // 4
    then(d_outer)
    a.core(*long_grads(place, active, now(d_outer)))
    a.half_later()
    d_inner, sums_in, d_branch, d_attended, sums_one = feed_back(
        now(d_outer), ffn_in_weight, ffn_out_weight, slope, z_one, norm_one, out_weight
    )
    then(d_branch)
    a.add_own()
    b.core(*wide_grads(place, [(second_low, now(d_inner))]))
    a.split(1)
    b.half()
    first_right, ds_0, line_0, qv_0 = back(0, step, early, 0, None)
    a.split(more[0])
    first_right, ds_1, line_1, qv_1 = back(step, early - step, early, step, first_right)
    a.double(more[1:])
    c.core(*wide_grads(place, [(attended, d_branch), (entry_low, now(first_right))]))
    b.split(1)
    c.half()
    last_right, ds_2, line_2, qv_2 = back(early, late_pairs, late_pairs, 0, None)
    a.back(more[0])
    b.split(more[0])
    small_0, line_grad = table_grads([ds_0, ds_1, now(ds_2)], [line_0, line_1, line_2], maps, 0)
    then(small_0)
    b.double(more[1:])
    c.split(1)
    a.gather()
    grad_mine, grad_send = entry_grad(first_right, now(last_right), qkv_weight, d_branch, windows)
    then(grad_send)
    a.settle()
    c.split(more[0])
    b.back(more[0])
    grad_other = swap_half(grad_send)
    smalls = [small_0, then(table_grads([ds_0, ds_1, now(ds_2)], [], maps, 1, 2, 0)[0])]
    c.double(more[1:])
    smalls.append(then(table_grads([ds_0, ds_1, now(ds_2)], [], maps, 1, 2, 1)[0]))
    for w in range(2, windows):
        smalls.append(then(table_grads([ds_0, ds_1, now(ds_2)], [], maps, w)[0]))
    b.gather()
    then(*last[0], grad_other, a.across)
    d.core(
        *last_grads(
            place, entry_low, last_right, features, now(grad_mine), grad_send, sums_two, sums_one, sums_in, qv_0, qv_1, qv_2, line_grad, *smalls
        )
    )
    c.back(more[0])
    d.half()
    (ffn_out_grad,) = lay(place, a.pieces(), "long", block_rows)
    then(ffn_out_grad)
    hidden_grad = then(ordered(half, now(grad_mine), grad_other, 0))
    d.split(more[0])
    out_other = swap_half(now(out_send))
    c.gather()
    b.settle()
    d.double(more[1:])
    (ffn_in_grad,) = lay(place, b.pieces(), "wide", block_rows)
    then(ffn_in_grad)
    d.double([1])
    c.settle()
    c_pieces = c.pieces()
    d.gather(more[0])
    out_grad, qkv_grad, box, two, one, qv, out_sum, ffn_out_sum, ffn_in_sum, table = lay(
        place, c_pieces + d.pieces(), "heads", block_rows
    )
    layer_out = ordered(half, now(out_mine), out_other, 0)
    return (
        layer_out,
        hidden_grad,
        box,
        qkv_grad,
        qv,
        out_grad,
        out_sum,
        table,
        one,
        ffn_in_grad,
        ffn_in_sum,
        ffn_out_grad,
        ffn_out_sum,
        two,
    )


def solution(mesh):
    rep = P()
    rows = P("half", None)
    return jax.shard_map(
        partial(shards, mesh.shape["doc"]),
        mesh=mesh,
        in_specs=(P("doc", "half", None), P(None, "doc", "half"), P("doc")) + (rep,) * 12 + (P("doc", "half", None),),
        out_specs=(
            P("doc", "half", None),
            P("doc", "half", None),
            rows,
            rows,
            rows,
            rows,
            P("half"),
            rows,
            rows,
            rows,
            P("half"),
            rows,
            P("half"),
            rows,
        ),
        check_vma=False,
    )
```
